32 devices in a mesh: dp: 32 (over z, y, x, core).
Axes of the slice: x: 2, y: 2, z: 4, core: 2. Of those that a mesh axis runs over, the one named last changes fastest.
Arguments:
- visible: bfloat16 [16384, 768], P('dp'), may hold values from -6 to 6
- embed_weight: bfloat16 [768, 512], replicated, may hold values from -0.21875 to 0.21875
- embed_bias: float32 [512], replicated, may hold values from -3 to 3
- mask_token: float32 [512], replicated, may hold values from -5 to 5
- pos_embed: float32 [512, 512], replicated, may hold values from -1 to 1
- norm1_gain: float32 [512], replicated, may hold values from 0.5 to 1.5
- qkv_weight: bfloat16 [512, 1536], replicated, may hold values from -0.25 to 0.25
- rel_table: float32 [16, 49], replicated, may hold values from -4 to 4
- out_weight: bfloat16 [512, 512], replicated, may hold values from -0.75 to 0.75
- out_bias: float32 [512], replicated, may hold values from -3 to 3
- norm2_gain: float32 [512], replicated, may hold values from 0.5 to 1.5
- up_weight: bfloat16 [512, 2048], replicated, may hold values from -0.25 to 0.25
- up_bias: float32 [2048], replicated, may hold values from -3 to 3
- down_weight: bfloat16 [2048, 512], replicated, may hold values from -0.125 to 0.125
- down_bias: float32 [512], replicated, may hold values from -3 to 3
- cotangent: bfloat16 [65536, 512], P('dp'), may hold values from -6 to 6
- visible_index: int32 [32, 32, 16], P('dp'), may hold values from 0 to 2047, as said below
- slot_counts: int32 [32, 32], P('dp'), may hold values from 8 to 16, as said below
- segment_ids: int32 [8192], replicated, may hold values from 1 to 96, as said below
Outputs:
- out: bfloat16 [65536, 512], P('dp')
- grad_visible: bfloat16 [16384, 768], P('dp')
- grad_embed_weight: float32 [768, 512], replicated
- grad_embed_bias: float32 [512], replicated
- grad_mask_token: float32 [512], replicated
- grad_norm1_gain: float32 [512], replicated
- grad_qkv_weight: float32 [512, 1536], replicated
- grad_rel_table: float32 [16, 49], replicated
- grad_out_weight: float32 [512, 512], replicated
- grad_out_bias: float32 [512], replicated
- grad_norm2_gain: float32 [512], replicated
- grad_up_weight: float32 [512, 2048], replicated
- grad_up_bias: float32 [2048], replicated
- grad_down_weight: float32 [2048, 512], replicated
- grad_down_bias: float32 [512], replicated
The draws below stay inside these ranges and needn't reach their ends.
Inputs may be any that keep to these rules, and one draw needn't show every extreme that they name: For each slab d the 512 entries visible_index[d] are distinct token positions of that slab; entry [d, s, k] is used only where k < slot_counts[d, s]. slot_counts[d, s] rows go from device s to slab d; every slab receives 16 rows from its own device. `segment_ids`: frames with equal ids form one clip of one or more whole position grids; clips start only at multiples of 64 frames that are not multiples of 256; the time axis is a cycle, so the last clip continues into frame 0.
All inputs are finite; a program needn't handle non-finite values.
Results may differ from the reference program's by a relative error of at most 0.013.
Values may be sent and summed in bfloat16 or wider, within the bound.
No kernel may reach another device: no remote copies, remote signals or barrier semaphores. Data moves between devices by JAX's collectives and lax.ppermute only.
A program may use at most 256 MiB of HBM per device.

```python
import jax
import jax.numpy as jnp
from jax import lax

D = 512
HEADS = 16
HD = 32
FF = 2048
E_IN = 768
BANDS = 8
GRID_FR = 64
WIN = 4
SHIFT = 2
RELS = 49
FR = 256
TOK_DEV = 2048
RECV = 512
SLOT = 16
VIS_ROWS = 16384
NF = 8192
TOKENS = 65536


def routing_plan(key):
    base_key = jax.random.fold_in(key, 11)
    perm_key, drop_key = jax.random.split(base_key)
    device_count = RECV // SLOT
    order_keys = jax.random.split(perm_key, device_count)
    orders = jax.vmap(lambda single_key: jax.random.permutation(single_key, TOK_DEV))(order_keys)
    places = orders[:, :RECV].reshape(device_count, device_count, SLOT).astype(jnp.int32)
    dropped = jax.random.randint(drop_key, (device_count, device_count), 0, SLOT // 2 + 1)
    device_rank = jnp.arange(device_count)
    counts = jnp.where(device_rank[:, None] == device_rank[None, :], SLOT, SLOT - dropped).astype(jnp.int32)
    return (places, counts)


def draw_visible_index(key, part):
    return routing_plan(key)[0]


def draw_slot_counts(key, part):
    return routing_plan(key)[1]


def draw_segment_ids(key, part):
    edge_total = NF // GRID_FR - NF // FR
    frame_ids = jnp.arange(NF)
    grid_edge = (frame_ids % GRID_FR == 0) & (frame_ids % FR != 0)
    edge_rank = jnp.cumsum(grid_edge.astype(jnp.int32))
    coin_flips = jax.random.randint(jax.random.fold_in(key, 5), (NF,), 0, 2)
    chosen = grid_edge & ((coin_flips == 0) | (edge_rank == 1) | (edge_rank == edge_total))
    labels = lax.cummax(jnp.where(chosen, edge_rank, 0).astype(jnp.int32), axis=0)
    return jnp.where(labels == 0, edge_total, labels).astype(jnp.int32)


def block_levels(own_key, dims, cuts, smallest, largest):
    def one(position, blocks):
        draws = jax.random.uniform(jax.random.fold_in(jax.random.fold_in(own_key, 6), position), (blocks,), jnp.float32, smallest / len(cuts), largest / len(cuts))
        return jnp.repeat(jnp.exp(draws), dims[position] // blocks).reshape((-1,) + (1,) * (len(dims) - position - 1))

    factor_of = one(*cuts[0])
    for cut in cuts[1:]:
        factor_of = factor_of * one(*cut)
    return factor_of


def gaussian(key, extent, deviation, most, shards=(), held_as=jnp.bfloat16):
    values = deviation * jax.random.normal(key, extent, jnp.float32)
    if shards:
        values = values * block_levels(key, extent, shards, -0.22, 0.18)
    return jnp.clip(values, -most, most).astype(held_as)


def setup_inputs(seed: int = 0) -> dict:
    key_of = jax.random.split(jax.random.key(seed), 20)
    return {
        "visible": gaussian(key_of[0], (VIS_ROWS, E_IN), 1.0, 6.0, ((0, 32),)),
        "embed_weight": gaussian(key_of[1], (E_IN, D), E_IN ** -0.5, 0.21875),
        "embed_bias": gaussian(key_of[2], (D,), 0.5, 3.0, (), jnp.float32),
        "mask_token": gaussian(key_of[3], (D,), 1.0, 5.0, (), jnp.float32),
        "pos_embed": jnp.clip(jax.random.uniform(key_of[4], (GRID_FR * BANDS, D), jnp.float32, -1.0, 1.0), -1.0, 1.0),
        "norm1_gain": jnp.clip(1.0 + 0.1 * jax.random.normal(key_of[5], (D,), jnp.float32), 0.5, 1.5),
        "qkv_weight": gaussian(key_of[6], (D, 3 * D), D ** -0.5, 0.25),
        "rel_table": gaussian(key_of[7], (HEADS, RELS), 1.0, 4.0, (), jnp.float32),
        "out_weight": gaussian(key_of[8], (D, D), (D // 8) ** -0.5, 0.75),
        "out_bias": gaussian(key_of[9], (D,), 0.5, 3.0, (), jnp.float32),
        "norm2_gain": jnp.clip(1.0 + 0.1 * jax.random.normal(key_of[10], (D,), jnp.float32), 0.5, 1.5),
        "up_weight": gaussian(key_of[11], (D, FF), D ** -0.5, 0.25),
        "up_bias": gaussian(key_of[12], (FF,), 0.5, 3.0, (), jnp.float32),
        "down_weight": gaussian(key_of[13], (FF, D), FF ** -0.5, 0.125),
        "down_bias": gaussian(key_of[14], (D,), 0.5, 3.0, (), jnp.float32),
        "cotangent": gaussian(key_of[15], (TOKENS, D), 1.0, 6.0, ((0, 32),)),
        "visible_index": draw_visible_index(jax.random.fold_in(key_of[19], 71), 0),
        "slot_counts": draw_slot_counts(jax.random.fold_in(key_of[19], 71), 0),
        "segment_ids": draw_segment_ids(jax.random.fold_in(key_of[19], 71), 0),
    }


@jax.custom_vjp
def low(v):
    return lax.optimization_barrier(v.astype(jnp.bfloat16)).astype(jnp.float32)

@jax.custom_vjp
def low_back(v):
    return v

def low_keep(v):
    return (low(v), None)

def low_pass(kept, grad):
    return (grad,)

def back_keep(v):
    return (v, None)

def back_low(kept, grad):
    return (low(grad),)
low.defvjp(low_keep, low_pass)
low_back.defvjp(back_keep, back_low)
EPSILON = 1e-06
MASKED = -1e+30
PRECISE = lax.Precision.HIGHEST

def matmul_high(left, right):
    return jnp.dot(left, right, precision=PRECISE, preferred_element_type=jnp.float32)

def layer_norm(inputs, norm_gain):
    row_mean = lax.optimization_barrier(jnp.mean(inputs, axis=-1, keepdims=True))
    centred = inputs - row_mean
    row_var = lax.optimization_barrier(jnp.mean(centred * centred, axis=-1, keepdims=True))
    return centred * lax.rsqrt(row_var + EPSILON) * norm_gain

def relative_onehot():
    spots = jnp.arange(WIN * WIN)
    frame_off = spots // WIN
    band_off = spots % WIN
    rel_index = (frame_off[:, None] - frame_off[None, :] + WIN - 1) * (2 * WIN - 1) + (band_off[:, None] - band_off[None, :] + WIN - 1)
    return (rel_index[:, :, None] == jnp.arange((2 * WIN - 1) ** 2)[None, None, :]).astype(jnp.float32)

def split_windows(tape_rows, frames, head_count):
    model_width = tape_rows.shape[-1]
    blocks = tape_rows.reshape(frames // WIN, WIN, BANDS // WIN, WIN, head_count, model_width // head_count)
    return blocks.transpose(0, 2, 4, 1, 3, 5).reshape(frames // WIN, BANDS // WIN, head_count, WIN * WIN, model_width // head_count)

def join_windows(windows, frames):
    head_count = windows.shape[2]
    head_size = windows.shape[4]
    blocks = windows.reshape(frames // WIN, BANDS // WIN, head_count, WIN, WIN, head_size)
    return blocks.transpose(0, 3, 1, 4, 2, 5).reshape(frames * BANDS, head_count * head_size)

def clip_mask(seg_tape, frames):
    per_frame = seg_tape.reshape(frames // WIN, WIN)
    per_token = jnp.repeat(per_frame, WIN, axis=1)
    return per_token[:, :, None] == per_token[:, None, :]

def forward(visible, embed_weight, embed_bias, mask_token, norm1_gain, qkv_weight, rel_table, out_weight, out_bias, norm2_gain, up_weight, up_bias, down_weight, down_bias, pos_embed, targets, live_slot, seen_mask, segment_ids):
    device_count = RECV // SLOT
    embedded = low_back(low(matmul_high(visible, embed_weight) + embed_bias))
    by_dest = embedded.reshape(device_count, device_count, SLOT, D).transpose(1, 0, 2, 3).reshape(device_count * RECV, D)
    filled = jnp.zeros((TOKENS, D), jnp.float32).at[targets].add(by_dest * live_slot[:, None])
    start = filled + (1.0 - seen_mask)[:, None] * mask_token + jnp.tile(pos_embed, (NF // GRID_FR, 1))
    h_one = low(layer_norm(start, norm1_gain))
    qkv = low_back(low(matmul_high(h_one, qkv_weight)))
    shifted = jnp.roll(qkv, -SHIFT * BANDS, axis=0)
    seg_tape = jnp.roll(segment_ids, -SHIFT)
    queries = split_windows(shifted[:, :D], NF, HEADS)
    keys_win = split_windows(shifted[:, D:2 * D], NF, HEADS)
    values_win = split_windows(shifted[:, 2 * D:], NF, HEADS)
    pos_bias = jnp.einsum('hr,ijr->hij', rel_table, relative_onehot(), precision=PRECISE)
    raw_scores = jnp.einsum('abhid,abhjd->abhij', queries, keys_win, precision=PRECISE) * HD ** (-0.5)
    same_clip = clip_mask(seg_tape, NF)
    scores = jnp.where(same_clip[:, None, None], low_back(raw_scores) + pos_bias, MASKED)
    row_top = lax.optimization_barrier(jnp.max(scores, axis=-1, keepdims=True))
    expd = jnp.exp(scores - row_top)
    probs = expd / lax.optimization_barrier(jnp.sum(expd, axis=-1, keepdims=True))
    context_win = jnp.einsum('abhij,abhjd->abhid', low(probs), values_win, precision=PRECISE)
    context = low_back(low(jnp.roll(join_windows(context_win, NF), SHIFT * BANDS, axis=0)))
    middle = start + low_back(matmul_high(context, out_weight)) + out_bias
    h_two = low(layer_norm(middle, norm2_gain))
    up_value = low_back(matmul_high(h_two, up_weight)) + up_bias
    activated = low(jax.nn.gelu(up_value, approximate=False))
    return middle + low_back(matmul_high(activated, down_weight)) + down_bias

def reference(visible, embed_weight, embed_bias, mask_token, pos_embed, norm1_gain, qkv_weight, rel_table, out_weight, out_bias, norm2_gain, up_weight, up_bias, down_weight, down_bias, cotangent, visible_index, slot_counts, segment_ids):
    device_count = RECV // SLOT
    local_places = visible_index.reshape(device_count * RECV).astype(jnp.int32)
    dest_rank = jnp.repeat(jnp.arange(device_count, dtype=jnp.int32), RECV)
    targets = (dest_rank * TOK_DEV + local_places).astype(jnp.int32)
    live_slot = (jnp.arange(SLOT, dtype=jnp.int32)[None, None, :] < slot_counts[:, :, None]).reshape(device_count * RECV).astype(jnp.float32)
    seen_mask = jnp.zeros((TOKENS,), jnp.float32).at[targets].add(live_slot)
    params = (visible, embed_weight, embed_bias, mask_token, norm1_gain, qkv_weight, rel_table, out_weight, out_bias, norm2_gain, up_weight, up_bias, down_weight, down_bias)
    params = tuple((item.astype(jnp.float32) for item in params))
    pos_float = pos_embed.astype(jnp.float32)

    def closed(*inner):
        return forward(*inner, pos_float, targets, live_slot, seen_mask, segment_ids)
    result, pullback = jax.vjp(closed, *params)
    grads = pullback(cotangent.astype(jnp.float32))
    return (result.astype(jnp.bfloat16), grads[0].astype(jnp.bfloat16), grads[1], grads[2], grads[3], grads[4], grads[5], grads[6], grads[7], grads[8], grads[9], grads[10], grads[11], grads[12], grads[13])
```

```python
from functools import partial

import jax
import jax.numpy as jnp
import numpy as np
from jax import lax
from jax.experimental import pallas as pl
from jax.experimental.pallas import tpu as pltpu
from jax.sharding import Mesh, PartitionSpec as P

HEADS = 16
HD = 32
BANDS = 8
WIN = 4
SHIFT = 2
RIM = SHIFT * BANDS
SPOTS = WIN * WIN
OCT = 8
OCT_D = OCT * HD
OCT_S = OCT * SPOTS
RIM_SLOTS = 128
EPSILON = 1e-06
MASKED = -1e30
SCALE = HD ** (-0.5)
PRECISE = lax.Precision.HIGHEST
VMEM_LIMIT = 56 * 2**20
bf16 = jnp.bfloat16
f32 = jnp.float32
AXES = ("z", "p", "c")


def mm(a, b):
    return jnp.dot(a, b, preferred_element_type=f32)


def mm_nt(a, b):
    return lax.dot_general(a, b, (((1,), (1,)), ((), ())), preferred_element_type=f32)


def mm_tn(a, b):
    return lax.dot_general(a, b, (((0,), (0,)), ((), ())), preferred_element_type=f32)


def window_order(x):
    return (
        x.reshape(-1, WIN, BANDS // WIN, WIN, x.shape[-1])
        .transpose(0, 2, 1, 3, 4)
        .reshape(x.shape)
    )


def frame_order(x):
    return (
        x.reshape(-1, BANDS // WIN, WIN, WIN, x.shape[-1])
        .transpose(0, 2, 1, 3, 4)
        .reshape(x.shape)
    )


def window_row(token):
    group, rest = token // (WIN * BANDS), token % (WIN * BANDS)
    frame, band = rest // BANDS, rest % BANDS
    return group * (WIN * BANDS) + (band // WIN) * SPOTS + frame * WIN + band % WIN


def spread(x, block_ones):
    return jnp.concatenate([x] * OCT, axis=0) * block_ones


def own_heads(z):
    lane_head = lax.broadcasted_iota(jnp.int32, (SPOTS, 128), 1) // HD
    halves = []
    per = 128 // HD
    for t in range(OCT_D // 128):
        total = None
        for q in range(per):
            piece = z[(t * per + q) * SPOTS : (t * per + q + 1) * SPOTS, t * 128 : (t + 1) * 128]
            piece = jnp.where(lane_head == q, piece, 0.0)
            total = piece if total is None else total + piece
        halves.append(total)
    return jnp.concatenate(halves, axis=1)


def normalized(x):
    centred = x - jnp.mean(x, axis=-1, keepdims=True)
    inverse = lax.rsqrt(jnp.mean(centred * centred, axis=-1, keepdims=True) + EPSILON)
    return centred * inverse, inverse


def norm_back(grad, n, inverse):
    return inverse * (
        grad
        - jnp.mean(grad, axis=-1, keepdims=True)
        - n * jnp.mean(grad * n, axis=-1, keepdims=True)
    )


def slot_onehot(step, rows, places):
    row = lax.broadcasted_iota(jnp.int32, (rows, places.shape[1]), 0) + step * rows
    return jnp.where(row == places, 1.0, 0.0)


def head_slices(w, o):
    return slice(w * SPOTS, (w + 1) * SPOTS), slice(o * OCT_S, (o + 1) * OCT_S)


def forward_kernel(
    first, cut, arrived, rim, embed_w, embed_b, places, positions, mask_token, gain1, qkv_w, bias,
    across, ones, out_w, out_b, gain2, *rest
):
    start_o, h_one_o, qkv_o, probs_o, context_o, middle_o, h_two_o, slots_s, score_s, context_s = (
        rest[-10:]
    )
    rows, width = start_o.shape
    own = arrived.shape[0]
    step = pl.program_id(0)

    @pl.when(step == 0)
    def _():
        slots_s[0:own, :] = (mm(arrived[...], embed_w[...]) + embed_b[...]).astype(bf16)
        slots_s[own:, :] = (mm(rim[...], embed_w[...]) + embed_b[...]).astype(bf16)

    onehot = slot_onehot(step + first, rows, places[...])
    seen = jnp.sum(onehot, axis=1, keepdims=True)
    start = mm(onehot.astype(bf16), slots_s[...]) + (1.0 - seen) * mask_token[...] + positions[...]
    start_o[...] = start
    h_one = (normalized(start)[0] * gain1[...]).astype(bf16)
    h_one_o[...] = h_one
    qkv_o[...] = mm(h_one, qkv_w[...]).astype(bf16)
    block_ones = ones[...]
    windows = rows // SPOTS
    for w in range(windows):
        cut_w = cut[(step + first) * windows + w]
        for o in range(HEADS // OCT):
            r, s = head_slices(w, o)
            q = qkv_o[r, o * OCT_D : (o + 1) * OCT_D]
            k = qkv_o[r, width + o * OCT_D : width + (o + 1) * OCT_D]
            raw = mm_nt(k, spread(q, block_ones)) * SCALE + bias[:, s]
            score_s[r, s] = raw + cut_w * across[:, s]
    scores = score_s[...].reshape(windows, SPOTS, HEADS * SPOTS)
    expd = jnp.exp(scores - jnp.max(scores, axis=1, keepdims=True))
    probs = expd / jnp.sum(expd, axis=1, keepdims=True)
    probs_o[...] = probs.reshape(rows, HEADS * SPOTS)
    for w in range(windows):
        for o in range(HEADS // OCT):
            r, s = head_slices(w, o)
            v = qkv_o[r, 2 * width + o * OCT_D : 2 * width + (o + 1) * OCT_D]
            context_s[r, o * OCT_D : (o + 1) * OCT_D] = own_heads(mm_tn(probs_o[r, s].astype(bf16), v))
    context = context_s[...].astype(bf16)
    context_o[...] = context
    middle = start + mm(context, out_w[...]) + out_b[...]
    middle_o[...] = middle
    h_two_o[...] = (normalized(middle)[0] * gain2[...]).astype(bf16)


def feed_kernel(
    core, h_two, cotangent, up_w, up_b, down_w, after, act_o, grad_h_o, keep_o, send_o, bias_o,
    down_s, up_s
):
    del after
    step = pl.program_id(0)
    width = h_two.shape[1]
    hidden = down_w.shape[0]

    @pl.when(step == 0)
    def _():
        down_s[...] = jnp.zeros_like(down_s)
        up_s[...] = jnp.zeros_like(up_s)
        bias_o[...] = jnp.zeros_like(bias_o)

    h = h_two[...]
    cot = cotangent[...]
    up_value = mm(h, up_w[...]) + up_b[...]
    below = 0.5 * (1.0 + lax.erf(up_value * (0.5**0.5)))
    act = (up_value * below).astype(bf16)
    act_o[...] = act
    slope = below + up_value * (jnp.exp(-0.5 * up_value * up_value) * 0.3989422804014327)
    grad_up = mm_nt(cot, down_w[...]) * slope
    bias_o[...] += jnp.sum(grad_up, axis=0, keepdims=True)
    grad_low = grad_up.astype(bf16)
    down_s[...] += mm_tn(act, cot)
    up_s[...] += mm_tn(h, grad_low)
    grad_h_o[...] = mm_nt(grad_low, up_w[...])

    def give(down_o, up_o):
        down_o[...] = down_s[...].astype(bf16)
        for block in range(hidden // width):
            at = slice(block * width, (block + 1) * width)
            up_o[at, :] = up_s[:, at].astype(bf16)

    last = step == pl.num_programs(0) - 1

    @pl.when(last & (core[0] == 0))
    def _():
        give(keep_o, send_o)

    @pl.when(last & (core[0] == 1))
    def _():
        give(send_o, keep_o)


def attend_back_kernel(
    core, grad_h_a, grad_h_b, cotangent, middle, context, qkv, probs, h_one, gain2, out_w, ones,
    after, gqkv_o, grad_middle_o, keep_o, send_o, sums_o, rel_o, out_s, qkv_s, score_s,
):
    del after
    step = pl.program_id(0)
    rows, width = middle.shape
    windows = rows // SPOTS

    @pl.when(step == 0)
    def _():
        out_s[...] = jnp.zeros_like(out_s)
        qkv_s[...] = jnp.zeros_like(qkv_s)
        sums_o[...] = jnp.zeros_like(sums_o)
        rel_o[...] = jnp.zeros_like(rel_o)

    cot = cotangent[...].astype(f32)
    grad_h_two = grad_h_a[...] + grad_h_b[...]
    n2, r2 = normalized(middle[...])
    sums_o[0:1, :] += jnp.sum(grad_h_two * n2, axis=0, keepdims=True)
    grad_middle = cot + norm_back(grad_h_two * gain2[...], n2, r2)
    grad_middle_o[...] = grad_middle
    sums_o[1:2, :] += jnp.sum(grad_middle, axis=0, keepdims=True)
    sums_o[2:3, :] += jnp.sum(cot, axis=0, keepdims=True)
    grad_middle_low = grad_middle.astype(bf16)
    out_s[...] += mm_tn(context[...], grad_middle_low)
    grad_context = mm_nt(grad_middle_low, out_w[...]).astype(bf16)
    block_ones = ones[...]
    for w in range(windows):
        for o in range(HEADS // OCT):
            r, s = head_slices(w, o)
            heads = slice(o * OCT_D, (o + 1) * OCT_D)
            v_at = slice(2 * width + o * OCT_D, 2 * width + (o + 1) * OCT_D)
            wide = spread(grad_context[r, heads], block_ones)
            score_s[r, s] = mm_nt(qkv[r, v_at], wide)
            gqkv_o[r, v_at] = mm(probs[r, s].astype(bf16), wide).astype(bf16)
    pr = probs[...].reshape(windows, SPOTS, HEADS * SPOTS)
    grad_probs = score_s[...].reshape(windows, SPOTS, HEADS * SPOTS)
    delta = jnp.sum(grad_probs * pr, axis=1, keepdims=True)
    grad_scores = pr * (grad_probs - delta)
    rel_o[...] += jnp.sum(grad_scores, axis=0)
    score_s[...] = grad_scores.reshape(rows, HEADS * SPOTS)
    for w in range(windows):
        for o in range(HEADS // OCT):
            r, s = head_slices(w, o)
            q_at = slice(o * OCT_D, (o + 1) * OCT_D)
            k_at = slice(width + o * OCT_D, width + (o + 1) * OCT_D)
            low = score_s[r, s].astype(bf16)
            gqkv_o[r, q_at] = (own_heads(mm_tn(low, qkv[r, k_at])) * SCALE).astype(bf16)
            gqkv_o[r, k_at] = (mm(low, spread(qkv[r, q_at], block_ones)) * SCALE).astype(bf16)
    qkv_s[...] += mm_tn(h_one[...], gqkv_o[...])

    def give(low_o, high_o):
        low_o[0:width, :] = qkv_s[:, 0:width].astype(bf16)
        low_o[width : 2 * width, :] = qkv_s[:, width : 2 * width].astype(bf16)
        high_o[0:width, :] = qkv_s[:, 2 * width : 3 * width].astype(bf16)
        high_o[width : 2 * width, :] = out_s[...].astype(bf16)

    last = step == pl.num_programs(0) - 1

    @pl.when(last & (core[0] == 0))
    def _():
        give(keep_o, send_o)

    @pl.when(last & (core[0] == 1))
    def _():
        give(send_o, keep_o)


def scatter_back_kernel(
    core, gqkv, start, grad_middle, places, qkv_w, gain1, arrived, rim, sums, rel, up_bias_a,
    up_bias_b, after_a, after_b, slots_o, keep_o, send_o, slots_s, embed_s, sums_s,
):
    del after_a, after_b
    step = pl.program_id(0)
    rows, width = start.shape
    own, e_in = arrived.shape

    @pl.when(step == 0)
    def _():
        slots_s[...] = jnp.zeros_like(slots_s)
        sums_s[...] = jnp.zeros_like(sums_s)

    grad_h_one = mm_nt(gqkv[...], qkv_w[...])
    n1, r1 = normalized(start[...])
    sums_s[3:4, :] += jnp.sum(grad_h_one * n1, axis=0, keepdims=True)
    grad_start = grad_middle[...] + norm_back(grad_h_one * gain1[...], n1, r1)
    onehot = slot_onehot(step, rows, places[...])
    hidden = 1.0 - jnp.sum(onehot, axis=1, keepdims=True)
    sums_s[4:5, :] += jnp.sum(hidden * grad_start, axis=0, keepdims=True)
    slots_s[...] += mm_tn(onehot.astype(bf16), grad_start.astype(bf16))

    def give(low_o, high_o):
        half = low_o.shape[0]
        low_o[...] = embed_s[0:half, :].astype(bf16)
        left = e_in - half
        high_o[...] = jnp.zeros_like(high_o)
        if left > 0:
            high_o[0:left, :] = embed_s[half:e_in, :].astype(bf16)
        left = max(left, 0)
        high_o[left : left + 16, :] = sums_s[...].astype(bf16)
        high_o[left + 16 : left + 16 + SPOTS, 0 : HEADS * SPOTS] = rel[...].astype(bf16)

    last = step == pl.num_programs(0) - 1

    @pl.when(last)
    def _():
        slots = slots_s[...].astype(bf16)
        slots_o[...] = slots
        embed_s[0:e_in, :] = mm_tn(arrived[...], slots[0:own]) + mm_tn(rim[...], slots[own:])
        sums_s[0:3, :] = sums[0:3, :]
        sums_s[5:6, :] = jnp.sum(slots.astype(f32), axis=0, keepdims=True)
        at = 6
        for up_bias in (up_bias_a, up_bias_b):
            for block in range(up_bias.shape[1] // width):
                sums_s[at : at + 1, :] = up_bias[:, block * width : (block + 1) * width]
                at += 1

    @pl.when(last & (core[0] == 0))
    def _():
        give(keep_o, send_o)

    @pl.when(last & (core[0] == 1))
    def _():
        give(send_o, keep_o)


def prepare_kernel(cotangent, next_cot, pos_embed, order, cot_o, positions_o):
    block = order.shape[0]
    tokens = cotangent.shape[0]
    for at in range(0, tokens, block):
        if at + block < tokens:
            rows = cotangent[at + RIM : at + RIM + block, :]
        else:
            rows = jnp.concatenate([cotangent[at + RIM :, :], next_cot[...]], axis=0)
        cot_o[at : at + block, :] = mm(order[...].astype(bf16), rows).astype(bf16)
    grid_rows = pos_embed.shape[0]
    for at in range(0, grid_rows, block):
        if at + block < grid_rows:
            rows = pos_embed[at + RIM : at + RIM + block, :]
        else:
            rows = jnp.concatenate([pos_embed[at + RIM :, :], pos_embed[0:RIM, :]], axis=0)
        positions_o[at : at + block, :] = jnp.dot(
            order[...], rows, precision=PRECISE, preferred_element_type=f32
        )


def out_kernel(
    middle, act_a, act_b, down_a, down_b, down_bias, order, after, out_o, rim_o
):
    del after
    step = pl.program_id(0)
    last = pl.num_programs(0) - 1
    rows = middle.shape[0]
    block = order.shape[0]
    result = (
        middle[...] + mm(act_a[...], down_a[...]) + mm(act_b[...], down_b[...]) + down_bias[...]
    ).astype(bf16)
    result = jnp.concatenate(
        [mm_tn(order[...], result[b : b + block]).astype(bf16) for b in range(0, rows, block)],
        axis=0,
    )

    @pl.when(step < last)
    def _():
        out_o[pl.ds(pl.multiple_of(step * rows + RIM, RIM), rows), :] = result

    @pl.when(step == last)
    def _():
        out_o[pl.ds(pl.multiple_of(step * rows + RIM, RIM), rows - RIM), :] = result[: rows - RIM]
        rim_o[...] = result[rows - RIM :]
        out_o[0:RIM, :] = jnp.zeros((RIM, result.shape[1]), bf16)


def pair_sum_kernel(keep, got, after, sum_o):
    del after
    sum_o[...] = (keep[...].astype(f32) + got[...].astype(f32)).astype(bf16)


def cell_sum_kernel(count, *refs):
    parts, out = refs[:count], refs[-1]
    at = 0
    for part in parts:
        total = jnp.sum(part[...].astype(f32), axis=0).astype(bf16)
        chunks = out.shape[0]
        rows = total.shape[0] // chunks
        out[:, at : at + rows, :] = total.reshape(chunks, rows, total.shape[1])
        at += rows


def repeat_sum_kernel(part, after, out):
    del after
    total = jnp.sum(part[...].astype(f32), axis=0).astype(bf16)
    for copy in range(out.shape[0]):
        out[copy] = total


def repeat_kernel(part, after, out):
    del after
    for copy in range(out.shape[0]):
        out[copy] = part[...]


def feed_unpack_kernel(core, mine, other, down_o, up_o):
    parts = mine.shape[2]
    width = down_o.shape[1]

    def give(down, up):
        for f in range(parts):
            rows = down[:, :, f].reshape(-1, width).astype(f32)
            piece = rows.shape[0]
            down_o[f * piece : (f + 1) * piece, :] = rows
            rows = up[:, :, f].reshape(-1, width).astype(f32)
            for block in range(piece // width):
                up_o[:, f * piece + block * width : f * piece + (block + 1) * width] = rows[
                    block * width : (block + 1) * width
                ]

    @pl.when(core[0] == 0)
    def _():
        give(mine, other)

    @pl.when(core[0] == 1)
    def _():
        give(other, mine)


def rest_unpack_kernel(split, core, mine, other, qkv_o, out_o, embed_o, small_o):
    width = out_o.shape[1]
    e_in = embed_o.shape[0]

    def give(low, high):
        rows = low[:, :, 0:split].reshape(-1, width).astype(f32)
        qkv_o[:, 0:width] = rows[0:width]
        qkv_o[:, width : 2 * width] = rows[width:]
        rows = high[:, :, 0:split].reshape(-1, width).astype(f32)
        qkv_o[:, 2 * width :] = rows[0:width]
        out_o[...] = rows[width:]
        rows = low[:, :, split:].reshape(-1, width).astype(f32)
        half = rows.shape[0]
        embed_o[0 : min(half, e_in), :] = rows[0 : min(half, e_in)]
        rows = high[:, :, split:].reshape(-1, width).astype(f32)
        left = max(e_in - half, 0)
        if left:
            embed_o[half:e_in, :] = rows[0:left]
        small_o[...] = rows[left : left + small_o.shape[0]]

    @pl.when(core[0] == 0)
    def _():
        give(mine, other)

    @pl.when(core[0] == 1)
    def _():
        give(other, mine)


ANY = pl.BlockSpec(memory_space=pl.ANY)
SMEM = pl.BlockSpec(memory_space=pltpu.SMEM)


def whole(s):
    return pl.BlockSpec(s, lambda *i: (0,) * len(s))


def tile(rows, width, first=0):
    return pl.BlockSpec((rows, width), lambda i: (i + first, 0))


def params():
    return pltpu.CompilerParams(vmem_limit_bytes=VMEM_LIMIT)


def shape(s, d):
    return jax.ShapeDtypeStruct(s, d)


def at_once(kernel, args, outs, specs=None):
    if specs is None:
        specs = [whole(a.shape) for a in args]
    many = isinstance(outs, (list, tuple))
    out_specs = [whole(o.shape) for o in outs] if many else whole(outs.shape)
    return pl.pallas_call(
        kernel,
        grid=(1,),
        in_specs=specs,
        out_specs=out_specs,
        out_shape=outs,
        compiler_params=params(),
    )(*args)


def swap_cores(x):
    return lax.ppermute(x, "c", [(0, 1), (1, 0)])


def exchange(x, axis):
    return lax.all_to_all(x, axis, 0, 0, tiled=True)


def chip_share(keep, send, after):
    return at_once(
        pair_sum_kernel,
        (keep, swap_cores(send), after),
        shape(keep.shape, bf16),
        [whole(keep.shape)] * 2 + [ANY],
    )


def plane_exchange(share):
    cells = lax.axis_size("p")
    return exchange(share.reshape(cells, -1, share.shape[1]), "p")


def z_exchange(parts, after):
    planes = lax.axis_size("z")
    width = parts[0].shape[2]
    rows = sum(p.shape[1] for p in parts) // planes
    shares = at_once(
        partial(cell_sum_kernel, len(parts)),
        (*parts, *after),
        shape((planes, rows, width), bf16),
        [whole(p.shape) for p in parts] + [ANY] * len(after),
    )
    return shares, exchange(shares, "z")


def z_gather(part, after):
    repeated = at_once(
        repeat_sum_kernel, (part, after), shape(part.shape, bf16), [whole(part.shape), ANY]
    )
    return repeated, exchange(repeated, "z")


def plane_gather(part, after):
    cells = lax.axis_size("p")
    repeated = at_once(
        repeat_kernel, (part, after), shape((cells, *part.shape), bf16), [whole(part.shape), ANY]
    )
    return repeated, exchange(repeated, "p")


def order_matrix(block):
    token = np.arange(block)
    group, rest = token // (WIN * BANDS), token % (WIN * BANDS)
    frame, band = rest // BANDS, rest % BANDS
    row = group * (WIN * BANDS) + (band // WIN) * SPOTS + frame * WIN + band % WIN
    matrix = np.zeros((block, block), np.float32)
    matrix[row, token] = 1.0
    return matrix


def per_device(
    visible, embed_weight, embed_bias, mask_token, pos_embed, norm1_gain, qkv_weight, rel_table,
    out_weight, out_bias, norm2_gain, up_weight, up_bias, down_weight, down_bias, cotangent,
    visible_index, slot_counts, segment_ids,
):
    device_count = lax.axis_size(AXES)
    device_rank = lax.axis_index(AXES)
    core = lax.axis_index("c").reshape(1).astype(jnp.int32)
    planes, cells = lax.axis_size("z"), lax.axis_size("p")
    tokens, width = cotangent.shape
    frames = tokens // BANDS
    hidden = down_weight.shape[0]
    e_in = visible.shape[1]
    slot_rows = visible_index.shape[2]
    slots = device_count * slot_rows
    ext = slots + RIM_SLOTS
    back = [(i, (i - 1) % device_count) for i in range(device_count)]
    ahead = [(i, (i + 1) % device_count) for i in range(device_count)]
    row = lambda v: v.reshape(1, -1)

    arrived = exchange(visible, AXES)

    spot = visible_index.reshape(slots)
    live = (
        jnp.arange(slot_rows)[None, :] < slot_counts.reshape(device_count, 1)
    ).reshape(slots)
    rim_hot = ((jnp.arange(RIM)[:, None] == spot[None, :]) & live[None, :]).astype(bf16)
    rim_seen = jnp.sum(rim_hot.astype(f32), axis=1, keepdims=True).astype(bf16)
    sent_back = jnp.concatenate(
        [cotangent[:RIM], jnp.broadcast_to(rim_seen, (RIM, width))], axis=0
    )
    from_next = lax.ppermute(sent_back, AXES, back)
    next_seen = from_next[RIM:, 0].astype(f32)
    own_places = jnp.where(live & (spot >= RIM), window_row(spot - RIM), -1)
    rim_places = jnp.where(
        next_seen > 0.5, window_row(tokens - RIM + np.arange(RIM)), -1
    )
    places = jnp.concatenate(
        [own_places, rim_places, np.full((RIM_SLOTS - RIM,), -1, np.int32)]
    ).reshape(1, ext).astype(jnp.int32)

    seg_cycle = jnp.concatenate([segment_ids, segment_ids[:SHIFT]])
    seg_tape = lax.dynamic_slice_in_dim(seg_cycle, device_rank * frames + SHIFT, frames)
    seg_win = seg_tape.reshape(frames // WIN, WIN)
    cut = jnp.repeat(
        (seg_win[:, SHIFT - 1] != seg_win[:, SHIFT]).astype(f32), BANDS // WIN
    )

    spots = np.arange(SPOTS)
    frame_of, band_of = spots // WIN, spots % WIN
    rels = 2 * WIN - 1
    rel_index = (frame_of[:, None] - frame_of[None, :] + WIN - 1) * rels + (
        band_of[:, None] - band_of[None, :] + WIN - 1
    )
    rel_hot = (rel_index[:, :, None] == np.arange(rels * rels)).astype(np.float32)
    bias = jnp.einsum("hr,ijr->jhi", rel_table, rel_hot, precision=PRECISE).reshape(
        SPOTS, HEADS * SPOTS
    )
    halves = frame_of // SHIFT
    across = np.tile(
        np.where(halves[:, None] != halves[None, :], MASKED, 0.0).astype(np.float32), (1, HEADS)
    )
    ones = jnp.asarray(
        np.arange(OCT_S)[:, None] // SPOTS == np.arange(OCT_D)[None, :] // HD, bf16
    )
    order = order_matrix(256)
    cot, positions = at_once(
        prepare_kernel,
        (cotangent, from_next[:RIM], pos_embed, order),
        [shape(cotangent.shape, bf16), shape(pos_embed.shape, f32)],
    )

    tm = min(512, tokens)
    steps = tokens // tm
    grid = (steps,)
    pos_blocks = pos_embed.shape[0] // tm
    forward_outs = [
        (width, f32), (width, bf16), (3 * width, bf16), (HEADS * SPOTS, f32), (width, bf16),
        (width, f32), (width, bf16),
    ]

    def forward(first, count, rim, held):
        fixed = [
            cut, arrived, rim, embed_weight, row(embed_bias), places, positions, row(mask_token),
            row(norm1_gain), qkv_weight, bias, across, ones, out_weight, row(out_bias),
            row(norm2_gain),
        ]
        specs = [SMEM] + [whole(a.shape) for a in fixed[1:]]
        specs[6] = pl.BlockSpec((tm, width), lambda i: (lax.rem(i + first, pos_blocks), 0))
        return pl.pallas_call(
            partial(forward_kernel, first),
            grid=(count,),
            in_specs=specs + [ANY] * len(held),
            out_specs=[tile(tm, w, first) for w, _ in forward_outs],
            out_shape=[shape((tokens, w), d) for w, d in forward_outs],
            input_output_aliases={len(fixed) + i: i for i in range(len(held))},
            scratch_shapes=[
                pltpu.VMEM((ext, width), bf16),
                pltpu.VMEM((tm, HEADS * SPOTS), f32),
                pltpu.VMEM((tm, width), f32),
            ],
            compiler_params=params(),
        )(*fixed, *held)

    rim_rows = jnp.dot(rim_hot, arrived, preferred_element_type=f32).astype(bf16)
    next_rows = lax.ppermute(rim_rows, AXES, back)
    rim = jnp.pad(next_rows, ((0, RIM_SLOTS - RIM), (0, 0)))
    held = forward(0, steps - 1, jnp.zeros((RIM_SLOTS, e_in), bf16), ())
    start, h_one, qkv, probs, context, middle, h_two = forward(steps - 1, 1, rim, held)

    parts = 2
    piece = hidden // parts

    def feed(f, after):
        return pl.pallas_call(
            feed_kernel,
            grid=grid,
            in_specs=[
                SMEM,
                tile(tm, width),
                tile(tm, width),
                pl.BlockSpec((width, piece), lambda i: (0, f)),
                pl.BlockSpec((1, piece), lambda i: (0, f)),
                pl.BlockSpec((piece, width), lambda i: (f, 0)),
                ANY,
            ],
            out_specs=[
                tile(tm, piece),
                tile(tm, width),
                whole((piece, width)),
                whole((piece, width)),
                whole((1, piece)),
            ],
            out_shape=[
                shape((tokens, piece), bf16),
                shape((tokens, width), f32),
                shape((piece, width), bf16),
                shape((piece, width), bf16),
                shape((1, piece), f32),
            ],
            scratch_shapes=[pltpu.VMEM((piece, width), f32), pltpu.VMEM((width, piece), f32)],
            compiler_params=params(),
        )(core, h_two, cot, up_weight, row(up_bias), down_weight, after)

    act_a, grad_h_a, keep_a, send_a, up_bias_a = feed(0, cot)
    share_a = chip_share(keep_a, send_a, cot)
    plane_a = plane_exchange(share_a)
    act_b, grad_h_b, keep_b, send_b, up_bias_b = feed(1, share_a)
    share_b = chip_share(keep_b, send_b, cot)
    plane_b = plane_exchange(share_b)

    gqkv, grad_middle, keep_c, send_c, sums, rel_sum = pl.pallas_call(
        attend_back_kernel,
        grid=grid,
        in_specs=[
            SMEM,
            tile(tm, width),
            tile(tm, width),
            tile(tm, width),
            tile(tm, width),
            tile(tm, width),
            tile(tm, 3 * width),
            tile(tm, HEADS * SPOTS),
            tile(tm, width),
            whole((1, width)),
            whole((width, width)),
            whole((OCT_S, OCT_D)),
            ANY,
        ],
        out_specs=[
            tile(tm, 3 * width),
            tile(tm, width),
            whole((2 * width, width)),
            whole((2 * width, width)),
            whole((8, width)),
            whole((SPOTS, HEADS * SPOTS)),
        ],
        out_shape=[
            shape((tokens, 3 * width), bf16),
            shape((tokens, width), f32),
            shape((2 * width, width), bf16),
            shape((2 * width, width), bf16),
            shape((8, width), f32),
            shape((SPOTS, HEADS * SPOTS), f32),
        ],
        scratch_shapes=[
            pltpu.VMEM((width, width), f32),
            pltpu.VMEM((width, 3 * width), f32),
            pltpu.VMEM((tm, HEADS * SPOTS), f32),
        ],
        compiler_params=params(),
    )(
        core, grad_h_a, grad_h_b, cot, middle, context, qkv, probs, h_one, row(norm2_gain),
        out_weight, ones, share_b,
    )
    feed_shares, feed_z = z_exchange((plane_a, plane_b), (sums,))
    share_c = chip_share(keep_c, send_c, cot)
    plane_c = plane_exchange(share_c)

    unit = 16 * planes * cells
    half = -(-width // unit) * unit
    grad_slots, keep_d, send_d = pl.pallas_call(
        scatter_back_kernel,
        grid=grid,
        in_specs=[
            SMEM,
            tile(tm, 3 * width),
            tile(tm, width),
            tile(tm, width),
            whole((1, ext)),
            whole((width, 3 * width)),
            whole((1, width)),
            whole((slots, e_in)),
            whole((RIM_SLOTS, e_in)),
            whole((8, width)),
            whole((SPOTS, HEADS * SPOTS)),
            whole((1, piece)),
            whole((1, piece)),
            ANY,
            ANY,
        ],
        out_specs=[whole((ext, width)), whole((half, width)), whole((half, width))],
        out_shape=[shape((ext, width), bf16), shape((half, width), bf16), shape((half, width), bf16)],
        scratch_shapes=[
            pltpu.VMEM((ext, width), f32),
            pltpu.VMEM((max(e_in, half), width), f32),
            pltpu.VMEM((16, width), f32),
        ],
        compiler_params=params(),
    )(
        core, gqkv, start, grad_middle, places, qkv_weight, row(norm1_gain), arrived, rim, sums,
        rel_sum, up_bias_a, up_bias_b, feed_shares, share_c,
    )
    share_d = chip_share(keep_d, send_d, cot)
    plane_d = plane_exchange(share_d)
    rim_grad = lax.ppermute(grad_slots[slots : slots + RIM], AXES, ahead)
    feed_repeated, feed_z_all = z_gather(feed_z, share_d)

    out, rim_out = pl.pallas_call(
        out_kernel,
        grid=grid,
        in_specs=[
            tile(tm, width),
            tile(tm, piece),
            tile(tm, piece),
            pl.BlockSpec((piece, width), lambda i: (0, 0)),
            pl.BlockSpec((piece, width), lambda i: (1, 0)),
            whole((1, width)),
            whole(order.shape),
            ANY,
        ],
        out_specs=[whole((tokens, width)), whole((RIM, width))],
        out_shape=[shape((tokens, width), bf16), shape((RIM, width), bf16)],
        compiler_params=params(),
    )(
        middle, act_a, act_b, down_weight, down_weight, row(down_bias), jnp.asarray(order, bf16),
        feed_repeated,
    )
    rest_shares, rest_z = z_exchange((plane_c, plane_d), (rim_out,))
    feed_plane_repeated, feed_all = plane_gather(feed_z_all, rest_shares)

    grad_embedded = (
        grad_slots[:slots].astype(f32)
        + lax.dot_general(rim_hot, rim_grad, (((0,), (0,)), ((), ())), preferred_element_type=f32)
    ).astype(bf16)
    returned = exchange(grad_embedded, AXES)
    grad_visible = lax.dot_general(
        returned, embed_weight, (((1,), (1,)), ((), ())), preferred_element_type=f32
    ).astype(bf16)
    first_rows = lax.ppermute(rim_out, AXES, ahead)
    out = lax.dynamic_update_slice(out, first_rows, (0, 0))

    rest_repeated, rest_z_all = z_gather(rest_z, feed_plane_repeated)
    rest_plane_repeated, rest_all = plane_gather(rest_z_all, rest_repeated)

    chunk = piece // (cells * planes)
    feed_all = feed_all.reshape(cells, planes, parts, chunk, width)
    grad_down_weight, grad_up_weight = at_once(
        feed_unpack_kernel,
        (core, feed_all, swap_cores(feed_all)),
        [shape((hidden, width), f32), shape((width, hidden), f32)],
        [SMEM, whole(feed_all.shape), whole(feed_all.shape)],
    )
    split = 2 * width // (cells * planes)
    small_rows = 16 + SPOTS
    rest_all = rest_all.reshape(cells, planes, -1, width)
    grad_qkv_weight, grad_out_weight, grad_embed_weight, small = at_once(
        partial(rest_unpack_kernel, split),
        (core, rest_all, swap_cores(rest_all)),
        [
            shape((width, 3 * width), f32),
            shape((width, width), f32),
            shape((e_in, width), f32),
            shape((small_rows, width), f32),
        ],
        [SMEM, whole(rest_all.shape), whole(rest_all.shape)],
    )
    grad_rel = jnp.einsum(
        "jhi,ijr->hr",
        small[16:, : HEADS * SPOTS].reshape(SPOTS, HEADS, SPOTS),
        rel_hot,
        precision=PRECISE,
    )
    up_rows = hidden // width
    return (
        out,
        grad_visible,
        grad_embed_weight,
        small[5],
        small[4],
        small[3],
        grad_qkv_weight,
        grad_rel,
        grad_out_weight,
        small[1],
        small[0],
        grad_up_weight,
        small[6 : 6 + up_rows].reshape(hidden),
        grad_down_weight,
        small[2],
    )


def solution(mesh):
    planes = 4
    grid = Mesh(mesh.devices.reshape(planes, -1, 2), AXES)
    split = P(AXES)
    in_specs = (split,) + (P(),) * 14 + (split, split, split, P())
    out_specs = (split, split) + (P(),) * 13
    return jax.shard_map(
        per_device, mesh=grid, in_specs=in_specs, out_specs=out_specs, check_vma=False
    )
```

```python
from functools import partial

import jax
import jax.numpy as jnp
import numpy as np
from jax import lax
from jax.experimental import pallas as pl
from jax.experimental.pallas import tpu as pltpu
from jax.sharding import Mesh, PartitionSpec as P

HEADS = 16
HD = 32
BANDS = 8
WIN = 4
SHIFT = 2
RIM = SHIFT * BANDS
SPOTS = WIN * WIN
OCT = 8
OCT_D = OCT * HD
OCT_S = OCT * SPOTS
RIM_SLOTS = 128
EPSILON = 1e-06
MASKED = -1e30
SCALE = HD ** (-0.5)
PRECISE = lax.Precision.HIGHEST
VMEM_LIMIT = 60 * 2**20
FEED_PIECE = 1024
bf16 = jnp.bfloat16
f32 = jnp.float32
AXES = ("z", "p", "c")


def mm(a, b):
    return jnp.dot(a, b, preferred_element_type=f32)


def mm_nt(a, b):
    return lax.dot_general(a, b, (((1,), (1,)), ((), ())), preferred_element_type=f32)


def mm_tn(a, b):
    return lax.dot_general(a, b, (((0,), (0,)), ((), ())), preferred_element_type=f32)


def window_order(x):
    return (
        x.reshape(-1, WIN, BANDS // WIN, WIN, x.shape[-1])
        .transpose(0, 2, 1, 3, 4)
        .reshape(x.shape)
    )


def frame_order(x):
    return (
        x.reshape(-1, BANDS // WIN, WIN, WIN, x.shape[-1])
        .transpose(0, 2, 1, 3, 4)
        .reshape(x.shape)
    )


def window_row(token):
    group, rest = token // (WIN * BANDS), token % (WIN * BANDS)
    frame, band = rest // BANDS, rest % BANDS
    return group * (WIN * BANDS) + (band // WIN) * SPOTS + frame * WIN + band % WIN


def spread(x, block_ones):
    return jnp.concatenate([x] * OCT, axis=0) * block_ones


def own_heads(z):
    lane_head = lax.broadcasted_iota(jnp.int32, (SPOTS, 128), 1) // HD
    halves = []
    per = 128 // HD
    for t in range(OCT_D // 128):
        total = None
        for q in range(per):
            piece = z[(t * per + q) * SPOTS : (t * per + q + 1) * SPOTS, t * 128 : (t + 1) * 128]
            piece = jnp.where(lane_head == q, piece, 0.0)
            total = piece if total is None else total + piece
        halves.append(total)
    return jnp.concatenate(halves, axis=1)


def normalized(x):
    centred = x - jnp.mean(x, axis=-1, keepdims=True)
    inverse = lax.rsqrt(jnp.mean(centred * centred, axis=-1, keepdims=True) + EPSILON)
    return centred * inverse, inverse


def norm_back(grad, n, inverse):
    return inverse * (
        grad
        - jnp.mean(grad, axis=-1, keepdims=True)
        - n * jnp.mean(grad * n, axis=-1, keepdims=True)
    )


def slot_onehot(step, rows, places):
    row = lax.broadcasted_iota(jnp.int32, (rows, places.shape[1]), 0) + step * rows
    return jnp.where(row == places, 1.0, 0.0)


def head_slices(w, o):
    return slice(w * SPOTS, (w + 1) * SPOTS), slice(o * OCT_S, (o + 1) * OCT_S)


def forward_kernel(
    cut, arrived, rim, embed_w, embed_b, places, positions, mask_token, gain1, qkv_w, bias,
    across, ones, out_w, out_b, gain2, after, start_o, h_one_o, qkv_o, probs_o, context_o, middle_o,
    h_two_o, slots_s, score_s, context_s,
):
    del after
    rows, width = start_o.shape
    own = arrived.shape[0]
    step = pl.program_id(0)

    @pl.when(step == 0)
    def _():
        slots_s[0:own, :] = (mm(arrived[...], embed_w[...]) + embed_b[...]).astype(bf16)
        slots_s[own:, :] = (mm(rim[...], embed_w[...]) + embed_b[...]).astype(bf16)

    onehot = slot_onehot(step, rows, places[...])
    seen = jnp.sum(onehot, axis=1, keepdims=True)
    start = mm(onehot.astype(bf16), slots_s[...]) + (1.0 - seen) * mask_token[...] + positions[...]
    start_o[...] = start
    h_one = (normalized(start)[0] * gain1[...]).astype(bf16)
    h_one_o[...] = h_one
    qkv_o[...] = mm(h_one, qkv_w[...]).astype(bf16)
    block_ones = ones[...]
    windows = rows // SPOTS
    for w in range(windows):
        cut_w = cut[step * windows + w]
        for o in range(HEADS // OCT):
            r, s = head_slices(w, o)
            q = qkv_o[r, o * OCT_D : (o + 1) * OCT_D]
            k = qkv_o[r, width + o * OCT_D : width + (o + 1) * OCT_D]
            raw = mm_nt(k, spread(q, block_ones)) * SCALE + bias[:, s]
            score_s[r, s] = raw + cut_w * across[:, s]
    scores = score_s[...].reshape(windows, SPOTS, HEADS * SPOTS)
    expd = jnp.exp(scores - jnp.max(scores, axis=1, keepdims=True))
    probs = expd / jnp.sum(expd, axis=1, keepdims=True)
    probs_o[...] = probs.reshape(rows, HEADS * SPOTS)
    for w in range(windows):
        for o in range(HEADS // OCT):
            r, s = head_slices(w, o)
            v = qkv_o[r, 2 * width + o * OCT_D : 2 * width + (o + 1) * OCT_D]
            context_s[r, o * OCT_D : (o + 1) * OCT_D] = own_heads(mm_tn(probs_o[r, s].astype(bf16), v))
    context = context_s[...].astype(bf16)
    context_o[...] = context
    middle = start + mm(context, out_w[...]) + out_b[...]
    middle_o[...] = middle
    h_two_o[...] = (normalized(middle)[0] * gain2[...]).astype(bf16)


def rim_kernel(hot, arrived, after, out):
    del after
    out[...] = mm(hot[...], arrived[...]).astype(bf16)


def act_back_kernel(cotangent, down_w, after, out):
    del after
    out[...] = mm_nt(cotangent[...], down_w[...]).astype(bf16)


def feed_kernel(
    h_two, cotangent, grad_act, up_w, up_b, act_o, grad_h_o, down_o, up_o, bias_o, down_s, up_s
):
    step = pl.program_id(0)

    @pl.when(step == 0)
    def _():
        down_s[...] = jnp.zeros_like(down_s)
        up_s[...] = jnp.zeros_like(up_s)
        bias_o[...] = jnp.zeros_like(bias_o)

    h = h_two[...]
    cot = cotangent[...]
    hidden = up_w.shape[1]
    piece = min(FEED_PIECE, hidden)
    grad_h = None
    for at in range(0, hidden, piece):
        f = slice(at, at + piece)
        up_value = mm(h, up_w[:, f]) + up_b[:, f]
        below = 0.5 * (1.0 + lax.erf(up_value * (0.5**0.5)))
        act = (up_value * below).astype(bf16)
        act_o[:, f] = act
        slope = below + up_value * (jnp.exp(-0.5 * up_value * up_value) * 0.3989422804014327)
        grad_up = grad_act[:, f].astype(f32) * slope
        bias_o[:, f] += jnp.sum(grad_up, axis=0, keepdims=True)
        grad_low = grad_up.astype(bf16)
        down_s[f, :] += mm_tn(act, cot)
        up_s[:, f] += mm_tn(h, grad_low)
        part = mm_nt(grad_low, up_w[:, f])
        grad_h = part if grad_h is None else grad_h + part
    grad_h_o[...] = grad_h

    @pl.when(step == pl.num_programs(0) - 1)
    def _():
        down_o[...] = down_s[...].astype(bf16)
        up_o[...] = up_s[...].astype(bf16)


def attend_back_kernel(
    core, grad_h, cotangent, middle, context, qkv, probs, h_one, gain2, out_w, ones, gqkv_o,
    grad_middle_o, keep_o, send_o, sums_o, rel_o, out_s, qkv_s, score_s,
):
    step = pl.program_id(0)
    rows, width = middle.shape
    windows = rows // SPOTS

    @pl.when(step == 0)
    def _():
        out_s[...] = jnp.zeros_like(out_s)
        qkv_s[...] = jnp.zeros_like(qkv_s)
        sums_o[...] = jnp.zeros_like(sums_o)
        rel_o[...] = jnp.zeros_like(rel_o)

    cot = cotangent[...].astype(f32)
    grad_h_two = grad_h[...]
    n2, r2 = normalized(middle[...])
    sums_o[0:1, :] += jnp.sum(grad_h_two * n2, axis=0, keepdims=True)
    grad_middle = cot + norm_back(grad_h_two * gain2[...], n2, r2)
    grad_middle_o[...] = grad_middle
    sums_o[1:2, :] += jnp.sum(grad_middle, axis=0, keepdims=True)
    sums_o[2:3, :] += jnp.sum(cot, axis=0, keepdims=True)
    grad_middle_low = grad_middle.astype(bf16)
    out_s[...] += mm_tn(context[...], grad_middle_low)
    grad_context = mm_nt(grad_middle_low, out_w[...]).astype(bf16)
    block_ones = ones[...]
    for w in range(windows):
        for o in range(HEADS // OCT):
            r, s = head_slices(w, o)
            heads = slice(o * OCT_D, (o + 1) * OCT_D)
            v_at = slice(2 * width + o * OCT_D, 2 * width + (o + 1) * OCT_D)
            wide = spread(grad_context[r, heads], block_ones)
            score_s[r, s] = mm_nt(qkv[r, v_at], wide)
            gqkv_o[r, v_at] = mm(probs[r, s].astype(bf16), wide).astype(bf16)
    pr = probs[...].reshape(windows, SPOTS, HEADS * SPOTS)
    grad_probs = score_s[...].reshape(windows, SPOTS, HEADS * SPOTS)
    delta = jnp.sum(grad_probs * pr, axis=1, keepdims=True)
    grad_scores = pr * (grad_probs - delta)
    rel_o[...] += jnp.sum(grad_scores, axis=0)
    score_s[...] = grad_scores.reshape(rows, HEADS * SPOTS)
    for w in range(windows):
        for o in range(HEADS // OCT):
            r, s = head_slices(w, o)
            q_at = slice(o * OCT_D, (o + 1) * OCT_D)
            k_at = slice(width + o * OCT_D, width + (o + 1) * OCT_D)
            low = score_s[r, s].astype(bf16)
            gqkv_o[r, q_at] = (own_heads(mm_tn(low, qkv[r, k_at])) * SCALE).astype(bf16)
            gqkv_o[r, k_at] = (mm(low, spread(qkv[r, q_at], block_ones)) * SCALE).astype(bf16)
    qkv_s[...] += mm_tn(h_one[...], gqkv_o[...])

    def give(low_o, high_o):
        low_o[0:width, :] = qkv_s[:, 0:width].astype(bf16)
        low_o[width : 2 * width, :] = qkv_s[:, width : 2 * width].astype(bf16)
        high_o[0:width, :] = qkv_s[:, 2 * width : 3 * width].astype(bf16)
        high_o[width : 2 * width, :] = out_s[...].astype(bf16)

    last = step == pl.num_programs(0) - 1

    @pl.when(last & (core[0] == 0))
    def _():
        give(keep_o, send_o)

    @pl.when(last & (core[0] == 1))
    def _():
        give(send_o, keep_o)


def scatter_back_kernel(
    core, gqkv, start, grad_middle, places, qkv_w, gain1, arrived, rim, sums, rel, up_bias,
    slots_o, keep_o, send_o, slots_s, embed_s, sums_s,
):
    step = pl.program_id(0)
    rows, width = start.shape
    own, e_in = arrived.shape

    @pl.when(step == 0)
    def _():
        slots_s[...] = jnp.zeros_like(slots_s)
        sums_s[...] = jnp.zeros_like(sums_s)
        embed_s[...] = jnp.zeros_like(embed_s)

    grad_h_one = mm_nt(gqkv[...], qkv_w[...])
    n1, r1 = normalized(start[...])
    sums_s[3:4, :] += jnp.sum(grad_h_one * n1, axis=0, keepdims=True)
    grad_start = grad_middle[...] + norm_back(grad_h_one * gain1[...], n1, r1)
    onehot = slot_onehot(step, rows, places[...])
    hidden = 1.0 - jnp.sum(onehot, axis=1, keepdims=True)
    sums_s[4:5, :] += jnp.sum(hidden * grad_start, axis=0, keepdims=True)
    slots_s[...] += mm_tn(onehot.astype(bf16), grad_start.astype(bf16))

    def give(low_o, high_o):
        half = low_o.shape[0]
        low_o[...] = embed_s[0:half, :].astype(bf16)
        left = e_in - half
        high_o[...] = jnp.zeros_like(high_o)
        if left > 0:
            high_o[0:left, :] = embed_s[half:e_in, :].astype(bf16)
        left = max(left, 0)
        high_o[left : left + 16, :] = sums_s[...].astype(bf16)
        high_o[left + 16 : left + 16 + SPOTS, 0 : HEADS * SPOTS] = rel[...].astype(bf16)

    last = step == pl.num_programs(0) - 1

    @pl.when(last)
    def _():
        slots = slots_s[...].astype(bf16)
        slots_o[...] = slots
        embed_s[0:e_in, :] = mm_tn(arrived[...], slots[0:own]) + mm_tn(rim[...], slots[own:])
        sums_s[0:3, :] = sums[0:3, :]
        sums_s[5:6, :] = jnp.sum(slots.astype(f32), axis=0, keepdims=True)
        for block in range(up_bias.shape[1] // width):
            sums_s[6 + block : 7 + block, :] = up_bias[:, block * width : (block + 1) * width]

    @pl.when(last & (core[0] == 0))
    def _():
        give(keep_o, send_o)

    @pl.when(last & (core[0] == 1))
    def _():
        give(send_o, keep_o)


def prepare_kernel(cotangent, next_cot, pos_embed, order, cot_o, positions_o):
    block = order.shape[0]
    tokens = cotangent.shape[0]
    for at in range(0, tokens, block):
        if at + block < tokens:
            rows = cotangent[at + RIM : at + RIM + block, :]
        else:
            rows = jnp.concatenate([cotangent[at + RIM :, :], next_cot[...]], axis=0)
        cot_o[at : at + block, :] = mm(order[...].astype(bf16), rows).astype(bf16)
    grid_rows = pos_embed.shape[0]
    for at in range(0, grid_rows, block):
        if at + block < grid_rows:
            rows = pos_embed[at + RIM : at + RIM + block, :]
        else:
            rows = jnp.concatenate([pos_embed[at + RIM :, :], pos_embed[0:RIM, :]], axis=0)
        positions_o[at : at + block, :] = jnp.dot(
            order[...], rows, precision=PRECISE, preferred_element_type=f32
        )


def out_kernel(
    middle, act, down, down_bias, order, after, out_o, rim_o
):
    del after
    step = pl.program_id(0)
    last = pl.num_programs(0) - 1
    rows = middle.shape[0]
    block = order.shape[0]
    result = (
        middle[...] + mm(act[...], down[...]) + down_bias[...]
    ).astype(bf16)
    result = jnp.concatenate(
        [mm_tn(order[...], result[b : b + block]).astype(bf16) for b in range(0, rows, block)],
        axis=0,
    )

    @pl.when(step < last)
    def _():
        out_o[pl.ds(pl.multiple_of(step * rows + RIM, RIM), rows), :] = result

    @pl.when(step == last)
    def _():
        out_o[pl.ds(pl.multiple_of(step * rows + RIM, RIM), rows - RIM), :] = result[: rows - RIM]
        rim_o[...] = result[rows - RIM :]
        out_o[0:RIM, :] = jnp.zeros((RIM, result.shape[1]), bf16)


def chip_sum_kernel(*refs):
    parts, out = refs[:-1], refs[-1]
    cells = out.shape[0]
    at = 0
    for keep, got in zip(parts[::2], parts[1::2]):
        total = (keep[...].astype(f32) + got[...].astype(f32)).astype(bf16)
        rows = total.shape[0] // cells
        out[:, at : at + rows, :] = total.reshape(cells, rows, total.shape[1])
        at += rows


def plane_sum_kernel(plane, part, after, *outs):
    del after
    total_s = outs[-1]
    outs = outs[:-1]
    total_s[...] = jnp.sum(part[...].astype(f32), axis=0)
    rows = outs[0].shape[0]
    for b, out in enumerate(outs):
        at = pl.multiple_of(lax.bitwise_xor(plane[0], b) * rows, 8)
        out[...] = total_s[pl.ds(at, rows), :].astype(bf16)


def z_sum_kernel(*refs):
    total = refs[0][...].astype(f32)
    for ref in refs[1:-1]:
        total = total + ref[...].astype(f32)
    refs[-1][...] = total.astype(bf16)


def z_join_kernel(plane, *refs):
    out = refs[-1]
    for b, ref in enumerate(refs[:-2]):
        share = ref[...]
        at = lax.bitwise_xor(plane[0], b)
        for cell in range(out.shape[0]):
            out[cell, at] = share


def rest_unpack_kernel(split, core, mine, other, qkv_o, out_o, embed_o, *small_o):
    width = out_o.shape[1]
    e_in = embed_o.shape[0]

    def give(low, high):
        rows = low[:, 0:split].reshape(-1, width).astype(f32)
        qkv_o[:, 0:width] = rows[0:width]
        qkv_o[:, width : 2 * width] = rows[width:]
        rows = high[:, 0:split].reshape(-1, width).astype(f32)
        qkv_o[:, 2 * width :] = rows[0:width]
        out_o[...] = rows[width:]
        rows = low[:, split:].reshape(-1, width).astype(f32)
        half = rows.shape[0]
        embed_o[0 : min(half, e_in), :] = rows[0 : min(half, e_in)]
        rows = high[:, split:].reshape(-1, width).astype(f32)
        left = max(e_in - half, 0)
        if left:
            embed_o[half:e_in, :] = rows[0:left]
        for i, vector_o in enumerate(small_o[:6]):
            vector_o[...] = rows[left + i]
        up_bias_o, rel_o = small_o[6:]
        for i in range(up_bias_o.shape[0] // width):
            up_bias_o[i * width : (i + 1) * width] = rows[left + 6 + i]
        rel_o[...] = rows[left + 16 : left + 16 + SPOTS, 0 : HEADS * SPOTS]

    @pl.when(core[0] == 0)
    def _():
        give(mine, other)

    @pl.when(core[0] == 1)
    def _():
        give(other, mine)


def widen_kernel(down, up, down_o, up_o):
    down_o[...] = down[...].astype(f32)
    up_o[...] = up[...].astype(f32)


ANY = pl.BlockSpec(memory_space=pl.ANY)
SMEM = pl.BlockSpec(memory_space=pltpu.SMEM)


def whole(s):
    return pl.BlockSpec(s, lambda *i: (0,) * len(s))


def tile(rows, width, first=0):
    return pl.BlockSpec((rows, width), lambda i: (i + first, 0))


def params():
    return pltpu.CompilerParams(vmem_limit_bytes=VMEM_LIMIT)


def shape(s, d):
    return jax.ShapeDtypeStruct(s, d)


def at_once(kernel, args, outs, specs=None, scratch=()):
    if specs is None:
        specs = [whole(a.shape) for a in args]
    many = isinstance(outs, (list, tuple))
    out_specs = [whole(o.shape) for o in outs] if many else whole(outs.shape)
    return pl.pallas_call(
        kernel,
        grid=(1,),
        in_specs=specs,
        out_specs=out_specs,
        out_shape=outs,
        scratch_shapes=list(scratch),
        compiler_params=params(),
    )(*args)


def swap_cores(x):
    return lax.ppermute(x, "c", [(0, 1), (1, 0)])


def exchange(x, axis):
    return lax.all_to_all(x, axis, 0, 0, tiled=True)


def across_z(x, bit):
    return lax.ppermute(x, "z", [(i, i ^ bit) for i in range(lax.axis_size("z"))])


def chip_shares(pairs):
    cells = lax.axis_size("p")
    refs = [a for keep, send in pairs for a in (keep, swap_cores(send))]
    rows = sum(keep.shape[0] for keep, _ in pairs) // cells
    return at_once(chip_sum_kernel, refs, shape((cells, rows, refs[0].shape[1]), bf16))


def tree(shares, plane, after, after_z):
    cells, rows, width = shares.shape
    planes = lax.axis_size("z")
    part = exchange(shares, "p")
    sums = at_once(
        plane_sum_kernel,
        (plane, part, after),
        [shape((rows // planes, width), bf16)] * planes,
        [SMEM, whole(part.shape), ANY],
        [pltpu.VMEM((rows, width), f32)],
    )
    total = at_once(
        z_sum_kernel,
        [sums[0]] + [across_z(sums[b], b) for b in range(1, planes)],
        shape(sums[0].shape, bf16),
    )
    shares_z = [total] + [across_z(total, b) for b in range(1, planes)]
    joined = at_once(
        z_join_kernel,
        [plane, *shares_z, after_z],
        shape((cells, planes, rows // planes, width), bf16),
        [SMEM] + [whole(total.shape)] * planes + [ANY],
    )
    return exchange(joined, "p")


def order_matrix(block):
    token = np.arange(block)
    group, rest = token // (WIN * BANDS), token % (WIN * BANDS)
    frame, band = rest // BANDS, rest % BANDS
    row = group * (WIN * BANDS) + (band // WIN) * SPOTS + frame * WIN + band % WIN
    matrix = np.zeros((block, block), np.float32)
    matrix[row, token] = 1.0
    return matrix


def per_device(
    visible, embed_weight, embed_bias, mask_token, pos_embed, norm1_gain, qkv_weight, rel_table,
    out_weight, out_bias, norm2_gain, up_weight, up_bias, down_weight, down_bias, cotangent,
    visible_index, slot_counts, segment_ids,
):
    device_count = lax.axis_size(AXES)
    device_rank = lax.axis_index(AXES)
    core = lax.axis_index("c").reshape(1).astype(jnp.int32)
    plane = lax.axis_index("z").reshape(1).astype(jnp.int32)
    planes, cells = lax.axis_size("z"), lax.axis_size("p")
    tokens, width = cotangent.shape
    frames = tokens // BANDS
    hidden = down_weight.shape[0]
    e_in = visible.shape[1]
    slot_rows = visible_index.shape[2]
    slots = device_count * slot_rows
    ext = slots + RIM_SLOTS
    back = [(i, (i - 1) % device_count) for i in range(device_count)]
    ahead = [(i, (i + 1) % device_count) for i in range(device_count)]
    row = lambda v: v.reshape(1, -1)

    arrived = exchange(visible, AXES)

    spot = visible_index.reshape(slots)
    live = (
        jnp.arange(slot_rows)[None, :] < slot_counts.reshape(device_count, 1)
    ).reshape(slots)
    rim_hot = ((jnp.arange(RIM)[:, None] == spot[None, :]) & live[None, :]).astype(bf16)
    rim_seen = jnp.sum(rim_hot.astype(f32), axis=1, keepdims=True).astype(bf16)
    sent_back = jnp.concatenate(
        [cotangent[:RIM], jnp.broadcast_to(rim_seen, (RIM, width))], axis=0
    )
    from_next = lax.ppermute(sent_back, AXES, back)
    next_seen = from_next[RIM:, 0].astype(f32)
    own_places = jnp.where(live & (spot >= RIM), window_row(spot - RIM), -1)
    rim_places = jnp.where(
        next_seen > 0.5, window_row(tokens - RIM + np.arange(RIM)), -1
    )
    places = jnp.concatenate(
        [own_places, rim_places, np.full((RIM_SLOTS - RIM,), -1, np.int32)]
    ).reshape(1, ext).astype(jnp.int32)

    seg_cycle = jnp.concatenate([segment_ids, segment_ids[:SHIFT]])
    seg_tape = lax.dynamic_slice_in_dim(seg_cycle, device_rank * frames + SHIFT, frames)
    seg_win = seg_tape.reshape(frames // WIN, WIN)
    cut = jnp.repeat(
        (seg_win[:, SHIFT - 1] != seg_win[:, SHIFT]).astype(f32), BANDS // WIN
    )

    spots = np.arange(SPOTS)
    frame_of, band_of = spots // WIN, spots % WIN
    rels = 2 * WIN - 1
    rel_index = (frame_of[:, None] - frame_of[None, :] + WIN - 1) * rels + (
        band_of[:, None] - band_of[None, :] + WIN - 1
    )
    rel_hot = (rel_index[:, :, None] == np.arange(rels * rels)).astype(np.float32)
    bias = jnp.einsum("hr,ijr->jhi", rel_table, rel_hot, precision=PRECISE).reshape(
        SPOTS, HEADS * SPOTS
    )
    halves = frame_of // SHIFT
    across = np.tile(
        np.where(halves[:, None] != halves[None, :], MASKED, 0.0).astype(np.float32), (1, HEADS)
    )
    ones = jnp.asarray(
        np.arange(OCT_S)[:, None] // SPOTS == np.arange(OCT_D)[None, :] // HD, bf16
    )
    order = order_matrix(256)
    cot, positions = at_once(
        prepare_kernel,
        (cotangent, from_next[:RIM], pos_embed, order),
        [shape(cotangent.shape, bf16), shape(pos_embed.shape, f32)],
    )

    tm = min(512, tokens)
    steps = tokens // tm
    grid = (steps,)
    pos_blocks = pos_embed.shape[0] // tm
    forward_outs = [
        (width, f32), (width, bf16), (3 * width, bf16), (HEADS * SPOTS, f32), (width, bf16),
        (width, f32), (width, bf16),
    ]

    rim_rows = at_once(
        rim_kernel,
        (rim_hot, arrived, cot),
        shape((RIM, e_in), bf16),
        [whole(rim_hot.shape), whole(arrived.shape), ANY],
    )
    next_rows = lax.ppermute(rim_rows, AXES, back)
    grad_act = pl.pallas_call(
        act_back_kernel,
        grid=grid,
        in_specs=[tile(tm, width), whole((hidden, width)), ANY],
        out_specs=tile(tm, hidden),
        out_shape=shape((tokens, hidden), bf16),
        compiler_params=params(),
    )(cot, down_weight, rim_rows)
    rim = jnp.pad(next_rows, ((0, RIM_SLOTS - RIM), (0, 0)))
    forward_args = [
        cut, arrived, rim, embed_weight, row(embed_bias), places, positions, row(mask_token),
        row(norm1_gain), qkv_weight, bias, across, ones, out_weight, row(out_bias),
        row(norm2_gain), grad_act,
    ]
    specs = [SMEM] + [whole(a.shape) for a in forward_args[1:-1]] + [ANY]
    specs[6] = pl.BlockSpec((tm, width), lambda i: (lax.rem(i, pos_blocks), 0))
    start, h_one, qkv, probs, context, middle, h_two = pl.pallas_call(
        forward_kernel,
        grid=grid,
        in_specs=specs,
        out_specs=[tile(tm, w) for w, _ in forward_outs],
        out_shape=[shape((tokens, w), d) for w, d in forward_outs],
        scratch_shapes=[
            pltpu.VMEM((ext, width), bf16),
            pltpu.VMEM((tm, HEADS * SPOTS), f32),
            pltpu.VMEM((tm, width), f32),
        ],
        compiler_params=params(),
    )(*forward_args)

    act, grad_h, down_grad, up_grad, up_bias_grad = pl.pallas_call(
        feed_kernel,
        grid=grid,
        in_specs=[
            tile(tm, width),
            tile(tm, width),
            tile(tm, hidden),
            whole((width, hidden)),
            whole((1, hidden)),
        ],
        out_specs=[
            tile(tm, hidden),
            tile(tm, width),
            whole((hidden, width)),
            whole((width, hidden)),
            whole((1, hidden)),
        ],
        out_shape=[
            shape((tokens, hidden), bf16),
            shape((tokens, width), f32),
            shape((hidden, width), bf16),
            shape((width, hidden), bf16),
            shape((1, hidden), f32),
        ],
        scratch_shapes=[pltpu.VMEM((hidden, width), f32), pltpu.VMEM((width, hidden), f32)],
        compiler_params=params(),
    )(h_two, cot, grad_act, up_weight, row(up_bias))
    down_sum, up_sum = lax.psum((down_grad, up_grad), AXES)

    def rest(operands):
        (
            grad_h, cot, middle, context, qkv, probs, h_one, start, act, up_bias_grad, places,
            arrived, rim, rim_hot,
        ) = operands
        gqkv, grad_middle, keep_c, send_c, sums, rel_sum = pl.pallas_call(
            attend_back_kernel,
            grid=grid,
            in_specs=[
                SMEM,
                tile(tm, width),
                tile(tm, width),
                tile(tm, width),
                tile(tm, width),
                tile(tm, 3 * width),
                tile(tm, HEADS * SPOTS),
                tile(tm, width),
                whole((1, width)),
                whole((width, width)),
                whole((OCT_S, OCT_D)),
            ],
            out_specs=[
                tile(tm, 3 * width),
                tile(tm, width),
                whole((2 * width, width)),
                whole((2 * width, width)),
                whole((8, width)),
                whole((SPOTS, HEADS * SPOTS)),
            ],
            out_shape=[
                shape((tokens, 3 * width), bf16),
                shape((tokens, width), f32),
                shape((2 * width, width), bf16),
                shape((2 * width, width), bf16),
                shape((8, width), f32),
                shape((SPOTS, HEADS * SPOTS), f32),
            ],
            scratch_shapes=[
                pltpu.VMEM((width, width), f32),
                pltpu.VMEM((width, 3 * width), f32),
                pltpu.VMEM((tm, HEADS * SPOTS), f32),
            ],
            compiler_params=params(),
        )(
            core, grad_h, cot, middle, context, qkv, probs, h_one, row(norm2_gain),
            out_weight, ones,
        )

        unit = 16 * planes * cells
        half = -(-width // unit) * unit
        grad_slots, keep_d, send_d = pl.pallas_call(
            scatter_back_kernel,
            grid=grid,
            in_specs=[
                SMEM,
                tile(tm, 3 * width),
                tile(tm, width),
                tile(tm, width),
                whole((1, ext)),
                whole((width, 3 * width)),
                whole((1, width)),
                whole((slots, e_in)),
                whole((RIM_SLOTS, e_in)),
                whole((8, width)),
                whole((SPOTS, HEADS * SPOTS)),
                whole((1, hidden)),
            ],
            out_specs=[whole((ext, width)), whole((half, width)), whole((half, width))],
            out_shape=[shape((ext, width), bf16), shape((half, width), bf16), shape((half, width), bf16)],
            scratch_shapes=[
                pltpu.VMEM((ext, width), f32),
                pltpu.VMEM((max(e_in, half), width), f32),
                pltpu.VMEM((16, width), f32),
            ],
            compiler_params=params(),
        )(
            core, gqkv, start, grad_middle, places, qkv_weight, row(norm1_gain), arrived, rim, sums,
            rel_sum, up_bias_grad,
        )
        shares = chip_shares([(keep_c, send_c), (keep_d, send_d)])
        rim_grad = lax.ppermute(grad_slots[slots : slots + RIM], AXES, ahead)

        out, rim_out = pl.pallas_call(
            out_kernel,
            grid=grid,
            in_specs=[
                tile(tm, width),
                tile(tm, hidden),
                whole((hidden, width)),
                whole((1, width)),
                whole(order.shape),
                ANY,
            ],
            out_specs=[whole((tokens, width)), whole((RIM, width))],
            out_shape=[shape((tokens, width), bf16), shape((RIM, width), bf16)],
            compiler_params=params(),
        )(middle, act, down_weight, row(down_bias), jnp.asarray(order, bf16), shares)

        grad_embedded = (
            grad_slots[:slots].astype(f32)
            + lax.dot_general(rim_hot, rim_grad, (((0,), (0,)), ((), ())), preferred_element_type=f32)
        ).astype(bf16)
        returned = exchange(grad_embedded, AXES)
        grad_visible = lax.dot_general(
            returned, embed_weight, (((1,), (1,)), ((), ())), preferred_element_type=f32
        ).astype(bf16)
        rest_all = tree(shares, plane, rim_out, returned).reshape(cells, -1, width)
        first_rows = lax.ppermute(rim_out, AXES, ahead)
        out = lax.dynamic_update_slice(out, first_rows, (0, 0))

        return out, grad_visible, rest_all, swap_cores(rest_all)

    def nothing(operands):
        return tuple(jnp.zeros(o.shape, o.dtype) for o in jax.eval_shape(rest, operands))

    operands = (
        grad_h, cot, middle, context, qkv, probs, h_one, start, act, up_bias_grad, places,
        arrived, rim, rim_hot,
    )
    out, grad_visible, mine, other = lax.cond(device_rank < device_count, rest, nothing, operands)

    vector = shape((width,), f32)
    (
        grad_qkv_weight, grad_out_weight, grad_embed_weight, grad_norm2_gain, grad_out_bias,
        grad_down_bias, grad_norm1_gain, grad_mask_token, grad_embed_bias, grad_up_bias, rel_sums,
    ) = at_once(
        partial(rest_unpack_kernel, 2 * width // cells),
        (core, mine, other),
        [
            shape((width, 3 * width), f32),
            shape((width, width), f32),
            shape((e_in, width), f32),
            *[vector] * 6,
            shape((hidden,), f32),
            shape((SPOTS, HEADS * SPOTS), f32),
        ],
        [SMEM, whole(mine.shape), whole(other.shape)],
    )
    grad_rel = jnp.einsum(
        "jhi,ijr->hr", rel_sums.reshape(SPOTS, HEADS, SPOTS), rel_hot, precision=PRECISE
    )
    grad_down_weight, grad_up_weight = pl.pallas_call(
        widen_kernel,
        grid=(4,),
        in_specs=[tile(hidden // 4, width), tile(width // 4, hidden)],
        out_specs=[tile(hidden // 4, width), tile(width // 4, hidden)],
        out_shape=[shape((hidden, width), f32), shape((width, hidden), f32)],
        compiler_params=params(),
    )(down_sum, up_sum)
    return (
        out,
        grad_visible,
        grad_embed_weight,
        grad_embed_bias,
        grad_mask_token,
        grad_norm1_gain,
        grad_qkv_weight,
        grad_rel,
        grad_out_weight,
        grad_out_bias,
        grad_norm2_gain,
        grad_up_weight,
        grad_up_bias,
        grad_down_weight,
        grad_down_bias,
    )


def solution(mesh):
    planes = 4
    grid = Mesh(mesh.devices.reshape(planes, -1, 2), AXES)
    split = P(AXES)
    in_specs = (split,) + (P(),) * 14 + (split, split, split, P())
    out_specs = (split, split) + (P(),) * 13
    return jax.shard_map(
        per_device, mesh=grid, in_specs=in_specs, out_specs=out_specs, check_vma=False
    )
```

```python
from functools import partial

import jax
import jax.numpy as jnp
import numpy as np
from jax import lax
from jax.experimental import pallas as pl
from jax.experimental.pallas import tpu as pltpu
from jax.sharding import Mesh, PartitionSpec as P

HEADS = 16
HD = 32
BANDS = 8
WIN = 4
SHIFT = 2
RIM = SHIFT * BANDS
SPOTS = WIN * WIN
OCT = 8
OCT_D = OCT * HD
OCT_S = OCT * SPOTS
RIM_SLOTS = 128
EPSILON = 1e-06
MASKED = -1e30
SCALE = HD ** (-0.5)
PRECISE = lax.Precision.HIGHEST
VMEM_LIMIT = 60 * 2**20
FEED_PIECE = 1024
bf16 = jnp.bfloat16
f32 = jnp.float32
AXES = ("z", "p", "c")


def mm(a, b):
    return jnp.dot(a, b, preferred_element_type=f32)


def mm_nt(a, b):
    return lax.dot_general(a, b, (((1,), (1,)), ((), ())), preferred_element_type=f32)


def mm_tn(a, b):
    return lax.dot_general(a, b, (((0,), (0,)), ((), ())), preferred_element_type=f32)


def window_order(x):
    return (
        x.reshape(-1, WIN, BANDS // WIN, WIN, x.shape[-1])
        .transpose(0, 2, 1, 3, 4)
        .reshape(x.shape)
    )


def frame_order(x):
    return (
        x.reshape(-1, BANDS // WIN, WIN, WIN, x.shape[-1])
        .transpose(0, 2, 1, 3, 4)
        .reshape(x.shape)
    )


def window_row(token):
    group, rest = token // (WIN * BANDS), token % (WIN * BANDS)
    frame, band = rest // BANDS, rest % BANDS
    return group * (WIN * BANDS) + (band // WIN) * SPOTS + frame * WIN + band % WIN


def spread(x, block_ones):
    return jnp.concatenate([x] * OCT, axis=0) * block_ones


def own_heads(z):
    lane_head = lax.broadcasted_iota(jnp.int32, (SPOTS, 128), 1) // HD
    halves = []
    per = 128 // HD
    for t in range(OCT_D // 128):
        total = None
        for q in range(per):
            piece = z[(t * per + q) * SPOTS : (t * per + q + 1) * SPOTS, t * 128 : (t + 1) * 128]
            piece = jnp.where(lane_head == q, piece, 0.0)
            total = piece if total is None else total + piece
        halves.append(total)
    return jnp.concatenate(halves, axis=1)


def normalized(x):
    centred = x - jnp.mean(x, axis=-1, keepdims=True)
    inverse = lax.rsqrt(jnp.mean(centred * centred, axis=-1, keepdims=True) + EPSILON)
    return centred * inverse, inverse


def norm_back(grad, n, inverse):
    return inverse * (
        grad
        - jnp.mean(grad, axis=-1, keepdims=True)
        - n * jnp.mean(grad * n, axis=-1, keepdims=True)
    )


def slot_onehot(step, rows, places):
    row = lax.broadcasted_iota(jnp.int32, (rows, places.shape[1]), 0) + step * rows
    return jnp.where(row == places, 1.0, 0.0)


def head_slices(w, o):
    return slice(w * SPOTS, (w + 1) * SPOTS), slice(o * OCT_S, (o + 1) * OCT_S)


def first_kernel(
    cut, arrived, rim, embed_w, embed_b, places, positions, mask_token, gain1, qkv_w, bias,
    across, ones, out_w, out_b, gain2, cotangent, grad_act, up_w, up_b, down_w, down_b, order,
    start_o, qkv_o, probs_o, grad_context_o, grad_middle_o, down_o, up_o, out_grad_o, sums_o,
    up_bias_o, out_o, rim_o, slots_s, score_s, context_s, down_s, up_s, out_s,
):
    rows, width = start_o.shape
    own = arrived.shape[0]
    hidden = up_w.shape[1]
    step = pl.program_id(0)
    last = step == pl.num_programs(0) - 1

    @pl.when(step == 0)
    def _():
        slots_s[0:own, :] = (mm(arrived[...], embed_w[...]) + embed_b[...]).astype(bf16)
        slots_s[own:, :] = (mm(rim[...], embed_w[...]) + embed_b[...]).astype(bf16)
        down_s[...] = jnp.zeros_like(down_s)
        up_s[...] = jnp.zeros_like(up_s)
        out_s[...] = jnp.zeros_like(out_s)
        up_bias_o[...] = jnp.zeros_like(up_bias_o)
        sums_o[...] = jnp.zeros_like(sums_o)

    onehot = slot_onehot(step, rows, places[...])
    seen = jnp.sum(onehot, axis=1, keepdims=True)
    start = mm(onehot.astype(bf16), slots_s[...]) + (1.0 - seen) * mask_token[...] + positions[...]
    start_o[...] = start
    h_one = (normalized(start)[0] * gain1[...]).astype(bf16)
    qkv_o[...] = mm(h_one, qkv_w[...]).astype(bf16)
    block_ones = ones[...]
    windows = rows // SPOTS
    for w in range(windows):
        cut_w = cut[step * windows + w]
        for o in range(HEADS // OCT):
            r, s = head_slices(w, o)
            q = qkv_o[r, o * OCT_D : (o + 1) * OCT_D]
            k = qkv_o[r, width + o * OCT_D : width + (o + 1) * OCT_D]
            raw = mm_nt(k, spread(q, block_ones)) * SCALE + bias[:, s]
            score_s[r, s] = raw + cut_w * across[:, s]
    scores = score_s[...].reshape(windows, SPOTS, HEADS * SPOTS)
    expd = jnp.exp(scores - jnp.max(scores, axis=1, keepdims=True))
    probs = expd / jnp.sum(expd, axis=1, keepdims=True)
    probs_o[...] = probs.reshape(rows, HEADS * SPOTS)
    for w in range(windows):
        for o in range(HEADS // OCT):
            r, s = head_slices(w, o)
            v = qkv_o[r, 2 * width + o * OCT_D : 2 * width + (o + 1) * OCT_D]
            context_s[r, o * OCT_D : (o + 1) * OCT_D] = own_heads(
                mm_tn(probs_o[r, s].astype(bf16), v)
            ).astype(bf16)
    middle = start_o[...] + mm(context_s[...], out_w[...]) + out_b[...]
    n2, r2 = normalized(middle)
    h_two = (n2 * gain2[...]).astype(bf16)

    cot = cotangent[...]
    piece = min(FEED_PIECE, hidden)
    grad_h = None
    result = middle + down_b[...]
    for at in range(0, hidden, piece):
        f = slice(at, at + piece)
        up_value = mm(h_two, up_w[:, f]) + up_b[:, f]
        below = 0.5 * (1.0 + lax.erf(up_value * (0.5**0.5)))
        act = (up_value * below).astype(bf16)
        slope = below + up_value * (jnp.exp(-0.5 * up_value * up_value) * 0.3989422804014327)
        grad_up = grad_act[:, f].astype(f32) * slope
        up_bias_o[:, f] += jnp.sum(grad_up, axis=0, keepdims=True)
        grad_low = grad_up.astype(bf16)
        result = result + mm(act, down_w[f, :])
        down_s[f, :] += mm_tn(act, cot)
        up_s[:, f] += mm_tn(h_two, grad_low)
        part = mm_nt(grad_low, up_w[:, f])
        grad_h = part if grad_h is None else grad_h + part

    result = result.astype(bf16)
    block = order.shape[0]
    result = jnp.concatenate(
        [mm_tn(order[...], result[b : b + block]).astype(bf16) for b in range(0, rows, block)],
        axis=0,
    )

    @pl.when(jnp.logical_not(last))
    def _():
        out_o[pl.ds(pl.multiple_of(step * rows + RIM, RIM), rows), :] = result

    @pl.when(last)
    def _():
        out_o[pl.ds(pl.multiple_of(step * rows + RIM, RIM), rows - RIM), :] = result[: rows - RIM]
        rim_o[...] = result[rows - RIM :]
        out_o[0:RIM, :] = jnp.zeros((RIM, width), bf16)

    wide_cot = cot.astype(f32)
    sums_o[0:1, :] += jnp.sum(grad_h * n2, axis=0, keepdims=True)
    grad_middle = wide_cot + norm_back(grad_h * gain2[...], n2, r2)
    grad_middle_o[...] = grad_middle
    sums_o[1:2, :] += jnp.sum(grad_middle, axis=0, keepdims=True)
    sums_o[2:3, :] += jnp.sum(wide_cot, axis=0, keepdims=True)
    grad_middle_low = grad_middle.astype(bf16)
    out_s[...] += mm_tn(context_s[...], grad_middle_low)
    grad_context_o[...] = mm_nt(grad_middle_low, out_w[...]).astype(bf16)

    @pl.when(last)
    def _():
        down_o[...] = down_s[...].astype(bf16)
        up_o[...] = up_s[...].astype(bf16)
        out_grad_o[...] = out_s[...].astype(bf16)


def second_kernel(
    core, grad_context, qkv, probs, start, grad_middle, places, qkv_w, gain1, ones, arrived, rim,
    out_grad, sums, up_bias, slots_o, keep_c_o, send_c_o, keep_d_o, send_d_o, gqkv_s,
    qkv_s, score_s, slots_s, embed_s, sums_s, rel_s,
):
    step = pl.program_id(0)
    rows, width = start.shape
    own, e_in = arrived.shape
    windows = rows // SPOTS

    @pl.when(step == 0)
    def _():
        qkv_s[...] = jnp.zeros_like(qkv_s)
        slots_s[...] = jnp.zeros_like(slots_s)
        sums_s[...] = jnp.zeros_like(sums_s)
        embed_s[...] = jnp.zeros_like(embed_s)
        rel_s[...] = jnp.zeros_like(rel_s)

    block_ones = ones[...]
    for w in range(windows):
        for o in range(HEADS // OCT):
            r, s = head_slices(w, o)
            heads = slice(o * OCT_D, (o + 1) * OCT_D)
            v_at = slice(2 * width + o * OCT_D, 2 * width + (o + 1) * OCT_D)
            wide = spread(grad_context[r, heads], block_ones)
            score_s[r, s] = mm_nt(qkv[r, v_at], wide)
            gqkv_s[r, v_at] = mm(probs[r, s].astype(bf16), wide).astype(bf16)
    pr = probs[...].reshape(windows, SPOTS, HEADS * SPOTS)
    grad_probs = score_s[...].reshape(windows, SPOTS, HEADS * SPOTS)
    delta = jnp.sum(grad_probs * pr, axis=1, keepdims=True)
    grad_scores = pr * (grad_probs - delta)
    rel_s[...] += jnp.sum(grad_scores, axis=0)
    score_s[...] = grad_scores.reshape(rows, HEADS * SPOTS)
    for w in range(windows):
        for o in range(HEADS // OCT):
            r, s = head_slices(w, o)
            q_at = slice(o * OCT_D, (o + 1) * OCT_D)
            k_at = slice(width + o * OCT_D, width + (o + 1) * OCT_D)
            low = score_s[r, s].astype(bf16)
            gqkv_s[r, q_at] = (own_heads(mm_tn(low, qkv[r, k_at])) * SCALE).astype(bf16)
            gqkv_s[r, k_at] = (mm(low, spread(qkv[r, q_at], block_ones)) * SCALE).astype(bf16)

    n1, r1 = normalized(start[...])
    h_one = (n1 * gain1[...]).astype(bf16)
    qkv_s[...] += mm_tn(h_one, gqkv_s[...])
    grad_h_one = mm_nt(gqkv_s[...], qkv_w[...])
    sums_s[3:4, :] += jnp.sum(grad_h_one * n1, axis=0, keepdims=True)
    grad_start = grad_middle[...] + norm_back(grad_h_one * gain1[...], n1, r1)
    onehot = slot_onehot(step, rows, places[...])
    hidden = 1.0 - jnp.sum(onehot, axis=1, keepdims=True)
    sums_s[4:5, :] += jnp.sum(hidden * grad_start, axis=0, keepdims=True)
    slots_s[...] += mm_tn(onehot.astype(bf16), grad_start.astype(bf16))

    def give_c(low_o, high_o):
        low_o[0:width, :] = qkv_s[:, 0:width].astype(bf16)
        low_o[width : 2 * width, :] = qkv_s[:, width : 2 * width].astype(bf16)
        high_o[0:width, :] = qkv_s[:, 2 * width : 3 * width].astype(bf16)
        high_o[width : 2 * width, :] = out_grad[...]

    def give_d(low_o, high_o):
        half = low_o.shape[0]
        low_o[...] = embed_s[0:half, :].astype(bf16)
        left = e_in - half
        high_o[...] = jnp.zeros_like(high_o)
        if left > 0:
            high_o[0:left, :] = embed_s[half:e_in, :].astype(bf16)
        left = max(left, 0)
        high_o[left : left + 16, :] = sums_s[...].astype(bf16)
        high_o[left + 16 : left + 16 + SPOTS, 0 : HEADS * SPOTS] = rel_s[...].astype(bf16)

    last = step == pl.num_programs(0) - 1

    @pl.when(last)
    def _():
        slots = slots_s[...].astype(bf16)
        slots_o[...] = slots
        embed_s[0:e_in, :] = mm_tn(arrived[...], slots[0:own]) + mm_tn(rim[...], slots[own:])
        sums_s[0:3, :] = sums[0:3, :]
        sums_s[5:6, :] = jnp.sum(slots.astype(f32), axis=0, keepdims=True)
        for block in range(up_bias.shape[1] // width):
            sums_s[6 + block : 7 + block, :] = up_bias[:, block * width : (block + 1) * width]

    @pl.when(last & (core[0] == 0))
    def _():
        give_c(keep_c_o, send_c_o)
        give_d(keep_d_o, send_d_o)

    @pl.when(last & (core[0] == 1))
    def _():
        give_c(send_c_o, keep_c_o)
        give_d(send_d_o, keep_d_o)


def rim_kernel(hot, arrived, after, out):
    del after
    out[...] = mm(hot[...], arrived[...]).astype(bf16)


def rim_back_kernel(hot, rim_grad, grad_slots, after_a, after_b, out):
    del after_a, after_b
    slots = out.shape[0]
    out[...] = (grad_slots[0:slots, :].astype(f32) + mm_tn(hot[...], rim_grad[...])).astype(bf16)


def act_back_kernel(cotangent, down_w, after, out):
    del after
    out[...] = mm_nt(cotangent[...], down_w[...]).astype(bf16)


def prepare_kernel(cotangent, next_cot, pos_embed, order, cot_o, positions_o):
    block = order.shape[0]
    tokens = cotangent.shape[0]
    for at in range(0, tokens, block):
        if at + block < tokens:
            rows = cotangent[at + RIM : at + RIM + block, :]
        else:
            rows = jnp.concatenate([cotangent[at + RIM :, :], next_cot[...]], axis=0)
        cot_o[at : at + block, :] = mm(order[...].astype(bf16), rows).astype(bf16)
    grid_rows = pos_embed.shape[0]
    for at in range(0, grid_rows, block):
        if at + block < grid_rows:
            rows = pos_embed[at + RIM : at + RIM + block, :]
        else:
            rows = jnp.concatenate([pos_embed[at + RIM :, :], pos_embed[0:RIM, :]], axis=0)
        positions_o[at : at + block, :] = jnp.dot(
            order[...], rows, precision=PRECISE, preferred_element_type=f32
        )


def chip_join_kernel(count, *refs):
    parts, out = refs[: 2 * count], refs[-1]
    at = 0
    for keep, got in zip(parts[::2], parts[1::2]):
        rows = keep.shape[1]
        out[0, at : at + rows, :] = (keep[0].astype(f32) + got[0].astype(f32)).astype(bf16)
        at += rows


def plane_sum_kernel(count, place, *refs):
    parts, outs, total_s = refs[:count], refs[count + 1 : -1], refs[-1]
    if count == 1:
        total_s[...] = jnp.sum(parts[0][...].astype(f32), axis=0)
    else:
        total = parts[0][...].astype(f32)
        for part in parts[1:]:
            total = total + part[...].astype(f32)
        total_s[...] = total
    rows = outs[0].shape[0]
    for b, out in enumerate(outs):
        at = pl.multiple_of(lax.bitwise_xor(place[0], b) * rows, 8)
        out[...] = total_s[pl.ds(at, rows), :].astype(bf16)


def z_sum_kernel(count, *refs):
    parts, out = refs[:count], refs[-1]
    total = parts[0][...].astype(f32)
    for part in parts[1:]:
        total = total + part[...].astype(f32)
    out[...] = total.astype(bf16)


def z_join_kernel(count, place, *refs):
    out = refs[-1]
    for b, ref in enumerate(refs[:count]):
        share = ref[...]
        at = lax.bitwise_xor(place[0], b)
        for cell in range(out.shape[0]):
            out[cell, at] = share


def widen_kernel(down, up, down_o, up_o):
    down_o[...] = down[...].astype(f32)
    up_o[...] = up[...].astype(f32)


def rest_unpack_kernel(split, core, mine, other, qkv_o, out_o, embed_o, *small_o):
    width = out_o.shape[1]
    e_in = embed_o.shape[0]

    def give(low, high):
        rows = low[:, 0:split].reshape(-1, width).astype(f32)
        qkv_o[:, 0:width] = rows[0:width]
        qkv_o[:, width : 2 * width] = rows[width:]
        rows = high[:, 0:split].reshape(-1, width).astype(f32)
        qkv_o[:, 2 * width :] = rows[0:width]
        out_o[...] = rows[width:]
        rows = low[:, split:].reshape(-1, width).astype(f32)
        half = rows.shape[0]
        embed_o[0 : min(half, e_in), :] = rows[0 : min(half, e_in)]
        rows = high[:, split:].reshape(-1, width).astype(f32)
        left = max(e_in - half, 0)
        if left:
            embed_o[half:e_in, :] = rows[0:left]
        for i, vector_o in enumerate(small_o[:6]):
            vector_o[...] = rows[left + i]
        up_bias_o, rel_o = small_o[6:]
        for i in range(up_bias_o.shape[0] // width):
            up_bias_o[i * width : (i + 1) * width] = rows[left + 6 + i]
        rel_o[...] = rows[left + 16 : left + 16 + SPOTS, 0 : HEADS * SPOTS]

    @pl.when(core[0] == 0)
    def _():
        give(mine, other)

    @pl.when(core[0] == 1)
    def _():
        give(other, mine)


ANY = pl.BlockSpec(memory_space=pl.ANY)
SMEM = pl.BlockSpec(memory_space=pltpu.SMEM)


def whole(s):
    return pl.BlockSpec(s, lambda *i: (0,) * len(s))


def held(s):
    return pl.BlockSpec(s, lambda *i: (0,) * len(s), pipeline_mode=pl.Buffered(1))


def tile(rows, width, first=0):
    return pl.BlockSpec((rows, width), lambda i: (i + first, 0))


def params():
    return pltpu.CompilerParams(vmem_limit_bytes=VMEM_LIMIT)


def shape(s, d):
    return jax.ShapeDtypeStruct(s, d)


def at_once(kernel, args, outs, specs=None, scratch=()):
    if specs is None:
        specs = [whole(a.shape) for a in args]
    many = isinstance(outs, (list, tuple))
    out_specs = [whole(o.shape) for o in outs] if many else whole(outs.shape)
    return pl.pallas_call(
        kernel,
        grid=(1,),
        in_specs=specs,
        out_specs=out_specs,
        out_shape=outs,
        scratch_shapes=list(scratch),
        compiler_params=params(),
    )(*args)


def swap_cores(x):
    return lax.ppermute(x, "c", [(0, 1), (1, 0)])


def exchange(x, axis):
    return lax.all_to_all(x, axis, 0, 0, tiled=True)


def across(x, axis):
    size = lax.axis_size(axis)
    return [lax.ppermute(x[b], axis, [(i, i ^ b) for i in range(size)]) for b in range(1, size)]


def chip_join(pairs, after):
    cells = lax.axis_size("p")
    width = pairs[0][0].shape[1]
    refs = [a.reshape(cells, -1, width) for keep, send in pairs for a in (keep, swap_cores(send))]
    rows = sum(r.shape[1] for r in refs[::2])
    return pl.pallas_call(
        partial(chip_join_kernel, len(pairs)),
        grid=(cells,),
        in_specs=[pl.BlockSpec((1, *r.shape[1:]), lambda i: (i, 0, 0)) for r in refs] + [ANY] * len(after),
        out_specs=pl.BlockSpec((1, rows, width), lambda i: (i, 0, 0)),
        out_shape=shape((cells, rows, width), bf16),
        compiler_params=params(),
    )(*refs, *after)


def plane_sum(place, parts, after):
    planes = lax.axis_size("z")
    rows, width = parts[0].shape[-2:]
    return at_once(
        partial(plane_sum_kernel, len(parts)),
        (place, *parts, after),
        [shape((rows // planes, width), bf16)] * planes,
        [SMEM] + [whole(p.shape) for p in parts] + [ANY],
        [pltpu.VMEM((rows, width), f32)],
    )


def z_sum(parts, after):
    return at_once(
        partial(z_sum_kernel, len(parts)),
        (*parts, *after),
        shape(parts[0].shape, bf16),
        [whole(p.shape) for p in parts] + [ANY] * len(after),
    )


def z_join(place, parts, after):
    cells = lax.axis_size("p")
    return at_once(
        partial(z_join_kernel, len(parts)),
        (place, *parts, *after),
        shape((cells, len(parts), *parts[0].shape), bf16),
        [SMEM] + [whole(p.shape) for p in parts] + [ANY] * len(after),
    )


def order_matrix(block):
    token = np.arange(block)
    group, rest = token // (WIN * BANDS), token % (WIN * BANDS)
    frame, band = rest // BANDS, rest % BANDS
    row = group * (WIN * BANDS) + (band // WIN) * SPOTS + frame * WIN + band % WIN
    matrix = np.zeros((block, block), np.float32)
    matrix[row, token] = 1.0
    return matrix


def per_device(
    visible, embed_weight, embed_bias, mask_token, pos_embed, norm1_gain, qkv_weight, rel_table,
    out_weight, out_bias, norm2_gain, up_weight, up_bias, down_weight, down_bias, cotangent,
    visible_index, slot_counts, segment_ids,
):
    device_count = lax.axis_size(AXES)
    device_rank = lax.axis_index(AXES)
    core = lax.axis_index("c").reshape(1).astype(jnp.int32)
    z_place = lax.axis_index("z").reshape(1).astype(jnp.int32)
    planes, cells = lax.axis_size("z"), lax.axis_size("p")
    tokens, width = cotangent.shape
    frames = tokens // BANDS
    hidden = down_weight.shape[0]
    e_in = visible.shape[1]
    slot_rows = visible_index.shape[2]
    slots = device_count * slot_rows
    ext = slots + RIM_SLOTS
    back = [(i, (i - 1) % device_count) for i in range(device_count)]
    ahead = [(i, (i + 1) % device_count) for i in range(device_count)]
    row = lambda v: v.reshape(1, -1)

    arrived = exchange(visible, AXES)

    spot = visible_index.reshape(slots)
    live = (
        jnp.arange(slot_rows)[None, :] < slot_counts.reshape(device_count, 1)
    ).reshape(slots)
    rim_hot = ((jnp.arange(RIM)[:, None] == spot[None, :]) & live[None, :]).astype(bf16)
    rim_seen = jnp.sum(rim_hot.astype(f32), axis=1, keepdims=True).astype(bf16)
    sent_back = jnp.concatenate(
        [cotangent[:RIM], jnp.broadcast_to(rim_seen, (RIM, width))], axis=0
    )
    from_next = lax.ppermute(sent_back, AXES, back)
    next_seen = from_next[RIM:, 0].astype(f32)
    own_places = jnp.where(live & (spot >= RIM), window_row(spot - RIM), -1)
    rim_places = jnp.where(
        next_seen > 0.5, window_row(tokens - RIM + np.arange(RIM)), -1
    )
    places = jnp.concatenate(
        [own_places, rim_places, np.full((RIM_SLOTS - RIM,), -1, np.int32)]
    ).reshape(1, ext).astype(jnp.int32)

    seg_cycle = jnp.concatenate([segment_ids, segment_ids[:SHIFT]])
    seg_tape = lax.dynamic_slice_in_dim(seg_cycle, device_rank * frames + SHIFT, frames)
    seg_win = seg_tape.reshape(frames // WIN, WIN)
    cut = jnp.repeat(
        (seg_win[:, SHIFT - 1] != seg_win[:, SHIFT]).astype(f32), BANDS // WIN
    )

    spots = np.arange(SPOTS)
    frame_of, band_of = spots // WIN, spots % WIN
    rels = 2 * WIN - 1
    rel_index = (frame_of[:, None] - frame_of[None, :] + WIN - 1) * rels + (
        band_of[:, None] - band_of[None, :] + WIN - 1
    )
    rel_hot = (rel_index[:, :, None] == np.arange(rels * rels)).astype(np.float32)
    bias = jnp.einsum("hr,ijr->jhi", rel_table, rel_hot, precision=PRECISE).reshape(
        SPOTS, HEADS * SPOTS
    )
    halves = frame_of // SHIFT
    apart = np.tile(
        np.where(halves[:, None] != halves[None, :], MASKED, 0.0).astype(np.float32), (1, HEADS)
    )
    ones = jnp.asarray(
        np.arange(OCT_S)[:, None] // SPOTS == np.arange(OCT_D)[None, :] // HD, bf16
    )
    order = order_matrix(256)
    cot, positions = at_once(
        prepare_kernel,
        (cotangent, from_next[:RIM], pos_embed, order),
        [shape(cotangent.shape, bf16), shape(pos_embed.shape, f32)],
    )

    tm = min(512, tokens)
    grid = (tokens // tm,)
    pos_blocks = pos_embed.shape[0] // tm
    rim_rows = at_once(
        rim_kernel,
        (rim_hot, arrived, cot),
        shape((RIM, e_in), bf16),
        [whole(rim_hot.shape), whole(arrived.shape), ANY],
    )
    next_rows = lax.ppermute(rim_rows, AXES, back)
    grad_act = pl.pallas_call(
        act_back_kernel,
        grid=grid,
        in_specs=[tile(tm, width), whole((hidden, width)), ANY],
        out_specs=tile(tm, hidden),
        out_shape=shape((tokens, hidden), bf16),
        compiler_params=params(),
    )(cot, down_weight, rim_rows)
    rim = jnp.pad(next_rows, ((0, RIM_SLOTS - RIM), (0, 0)))
    first_args = [
        cut, arrived, rim, embed_weight, row(embed_bias), places, positions,
        row(mask_token), row(norm1_gain), qkv_weight, bias, apart, ones, out_weight,
        row(out_bias), row(norm2_gain), cot, grad_act, up_weight, row(up_bias), down_weight,
        row(down_bias), jnp.asarray(order, bf16),
    ]
    specs = [SMEM] + [held(a.shape) for a in first_args[1:]]
    specs[6] = pl.BlockSpec((tm, width), lambda i: (lax.rem(i, pos_blocks), 0))
    specs[16] = tile(tm, width)
    specs[17] = tile(tm, hidden)
    (
        start, qkv, probs, grad_context, grad_middle, down_grad, up_grad, out_grad, sums,
        up_bias_grad, out, rim_out,
    ) = pl.pallas_call(
        first_kernel,
        grid=grid,
        in_specs=specs,
        out_specs=[
            tile(tm, width),
            tile(tm, 3 * width),
            tile(tm, HEADS * SPOTS),
            tile(tm, width),
            tile(tm, width),
            whole((hidden, width)),
            whole((width, hidden)),
            whole((width, width)),
            whole((8, width)),
            whole((1, hidden)),
            whole((tokens, width)),
            whole((RIM, width)),
        ],
        out_shape=[
            shape((tokens, width), f32),
            shape((tokens, 3 * width), bf16),
            shape((tokens, HEADS * SPOTS), f32),
            shape((tokens, width), bf16),
            shape((tokens, width), f32),
            shape((hidden, width), bf16),
            shape((width, hidden), bf16),
            shape((width, width), bf16),
            shape((8, width), f32),
            shape((1, hidden), f32),
            shape((tokens, width), bf16),
            shape((RIM, width), bf16),
        ],
        scratch_shapes=[
            pltpu.VMEM((ext, width), bf16),
            pltpu.VMEM((tm, HEADS * SPOTS), f32),
            pltpu.VMEM((tm, width), bf16),
            pltpu.VMEM((hidden, width), f32),
            pltpu.VMEM((width, hidden), f32),
            pltpu.VMEM((width, width), f32),
        ],
        compiler_params=params(),
    )(*first_args)
    down_sum, up_sum = lax.psum((down_grad, up_grad), AXES)

    unit = 16 * planes * cells
    half = -(-width // unit) * unit
    def rest(operands):
        (
            grad_context, qkv, probs, start, grad_middle, places, arrived, rim, rim_hot, out_grad,
            sums, up_bias_grad, out, rim_out,
        ) = operands
        grad_slots, keep_c, send_c, keep_d, send_d = pl.pallas_call(
            second_kernel,
            grid=grid,
            in_specs=[
                SMEM,
                tile(tm, width),
                tile(tm, 3 * width),
                tile(tm, HEADS * SPOTS),
                tile(tm, width),
                tile(tm, width),
                held((1, ext)),
                held((width, 3 * width)),
                held((1, width)),
                held((OCT_S, OCT_D)),
                held((slots, e_in)),
                held((RIM_SLOTS, e_in)),
                held((width, width)),
                held((8, width)),
                held((1, hidden)),
            ],
            out_specs=[
                whole((ext, width)),
                whole((2 * width, width)),
                whole((2 * width, width)),
                whole((half, width)),
                whole((half, width)),
            ],
            out_shape=[
                shape((ext, width), bf16),
                shape((2 * width, width), bf16),
                shape((2 * width, width), bf16),
                shape((half, width), bf16),
                shape((half, width), bf16),
            ],
            scratch_shapes=[
                pltpu.VMEM((tm, 3 * width), bf16),
                pltpu.VMEM((width, 3 * width), f32),
                pltpu.VMEM((tm, HEADS * SPOTS), f32),
                pltpu.VMEM((ext, width), f32),
                pltpu.VMEM((max(e_in, half), width), f32),
                pltpu.VMEM((16, width), f32),
                pltpu.VMEM((SPOTS, HEADS * SPOTS), f32),
            ],
            compiler_params=params(),
        )(
            core, grad_context, qkv, probs, start, grad_middle, places, qkv_weight, row(norm1_gain),
            ones, arrived, rim, out_grad, sums, up_bias_grad,
        )
        rim_grad = lax.ppermute(grad_slots[slots : slots + RIM], AXES, ahead)
        shares = chip_join([(keep_c, send_c), (keep_d, send_d)], ())
        part = exchange(shares, "p")
        first_rows = lax.ppermute(rim_out, AXES, ahead)
        out = lax.dynamic_update_slice(out, first_rows, (0, 0))
        grad_embedded = at_once(
            rim_back_kernel,
            (rim_hot, rim_grad, grad_slots, shares, first_rows),
            shape((slots, width), bf16),
            [whole(a.shape) for a in (rim_hot, rim_grad, grad_slots)] + [ANY, ANY],
        )
        returned = exchange(grad_embedded, AXES)
        grad_visible = lax.dot_general(
            returned, embed_weight, (((1,), (1,)), ((), ())), preferred_element_type=f32
        ).astype(bf16)
        sums_c = plane_sum(z_place, [part], grad_embedded)
        total = z_sum([sums_c[0], *across(sums_c, "z")], ())
        joined = z_join(z_place, [total, *across([total] * planes, "z")], (returned,))
        mine = exchange(joined, "p").reshape(cells, -1, width)
        return out, grad_visible, mine, swap_cores(mine)

    def nothing(operands):
        return tuple(jnp.zeros(o.shape, o.dtype) for o in jax.eval_shape(rest, operands))

    operands = (
        grad_context, qkv, probs, start, grad_middle, places, arrived, rim, rim_hot, out_grad,
        sums, up_bias_grad, out, rim_out,
    )
    out, grad_visible, mine, other = lax.cond(device_rank < device_count, rest, nothing, operands)

    vector = shape((width,), f32)
    (
        grad_qkv_weight, grad_out_weight, grad_embed_weight, grad_norm2_gain, grad_out_bias,
        grad_down_bias, grad_norm1_gain, grad_mask_token, grad_embed_bias, grad_up_bias, rel_sums,
    ) = at_once(
        partial(rest_unpack_kernel, 2 * width // cells),
        (core, mine, other),
        [
            shape((width, 3 * width), f32),
            shape((width, width), f32),
            shape((e_in, width), f32),
            *[vector] * 6,
            shape((hidden,), f32),
            shape((SPOTS, HEADS * SPOTS), f32),
        ],
        [SMEM, whole(mine.shape), whole(other.shape)],
    )
    grad_rel = jnp.einsum(
        "jhi,ijr->hr", rel_sums.reshape(SPOTS, HEADS, SPOTS), rel_hot, precision=PRECISE
    )
    grad_down_weight, grad_up_weight = pl.pallas_call(
        widen_kernel,
        grid=(4,),
        in_specs=[tile(hidden // 4, width), tile(width // 4, hidden)],
        out_specs=[tile(hidden // 4, width), tile(width // 4, hidden)],
        out_shape=[shape((hidden, width), f32), shape((width, hidden), f32)],
        compiler_params=params(),
    )(down_sum, up_sum)
    return (
        out,
        grad_visible,
        grad_embed_weight,
        grad_embed_bias,
        grad_mask_token,
        grad_norm1_gain,
        grad_qkv_weight,
        grad_rel,
        grad_out_weight,
        grad_out_bias,
        grad_norm2_gain,
        grad_up_weight,
        grad_up_bias,
        grad_down_weight,
        grad_down_bias,
    )


def solution(mesh):
    planes = 4
    grid = Mesh(mesh.devices.reshape(planes, -1, 2), AXES)
    split = P(AXES)
    in_specs = (split,) + (P(),) * 14 + (split, split, split, P())
    out_specs = (split, split) + (P(),) * 13
    return jax.shard_map(
        per_device, mesh=grid, in_specs=in_specs, out_specs=out_specs, check_vma=False
    )
```

```python
from functools import partial

import jax
import jax.numpy as jnp
import numpy as np
from jax import lax
from jax.experimental import pallas as pl
from jax.experimental.pallas import tpu as pltpu
from jax.sharding import Mesh, PartitionSpec as P

HEADS = 16
HD = 32
BANDS = 8
WIN = 4
SHIFT = 2
RIM = SHIFT * BANDS
SPOTS = WIN * WIN
OCT = 8
OCT_D = OCT * HD
OCT_S = OCT * SPOTS
RIM_SLOTS = 128
EPSILON = 1e-06
MASKED = -1e30
SCALE = HD ** (-0.5)
PRECISE = lax.Precision.HIGHEST
VMEM_LIMIT = 60 * 2**20
FEED_PIECE = 2048
bf16 = jnp.bfloat16
f32 = jnp.float32
AXES = ("z", "p", "c")


def mm(a, b):
    return jnp.dot(a, b, preferred_element_type=f32)


def mm_nt(a, b):
    return lax.dot_general(a, b, (((1,), (1,)), ((), ())), preferred_element_type=f32)


def mm_tn(a, b):
    return lax.dot_general(a, b, (((0,), (0,)), ((), ())), preferred_element_type=f32)


def window_order(x):
    return (
        x.reshape(-1, WIN, BANDS // WIN, WIN, x.shape[-1])
        .transpose(0, 2, 1, 3, 4)
        .reshape(x.shape)
    )


def frame_order(x):
    return (
        x.reshape(-1, BANDS // WIN, WIN, WIN, x.shape[-1])
        .transpose(0, 2, 1, 3, 4)
        .reshape(x.shape)
    )


def window_row(token):
    group, rest = token // (WIN * BANDS), token % (WIN * BANDS)
    frame, band = rest // BANDS, rest % BANDS
    return group * (WIN * BANDS) + (band // WIN) * SPOTS + frame * WIN + band % WIN


def spread(x, block_ones):
    return jnp.concatenate([x] * OCT, axis=0) * block_ones


def own_heads(z):
    lane_head = lax.broadcasted_iota(jnp.int32, (SPOTS, 128), 1) // HD
    halves = []
    per = 128 // HD
    for t in range(OCT_D // 128):
        total = None
        for q in range(per):
            piece = z[(t * per + q) * SPOTS : (t * per + q + 1) * SPOTS, t * 128 : (t + 1) * 128]
            piece = jnp.where(lane_head == q, piece, 0.0)
            total = piece if total is None else total + piece
        halves.append(total)
    return jnp.concatenate(halves, axis=1)


def normalized(x):
    centred = x - jnp.mean(x, axis=-1, keepdims=True)
    inverse = lax.rsqrt(jnp.mean(centred * centred, axis=-1, keepdims=True) + EPSILON)
    return centred * inverse, inverse


def norm_back(grad, n, inverse):
    return inverse * (
        grad
        - jnp.mean(grad, axis=-1, keepdims=True)
        - n * jnp.mean(grad * n, axis=-1, keepdims=True)
    )


def slot_onehot(step, rows, places):
    row = lax.broadcasted_iota(jnp.int32, (rows, places.shape[1]), 0) + step * rows
    return jnp.where(row == places, 1.0, 0.0)


def head_slices(w, o):
    return slice(w * SPOTS, (w + 1) * SPOTS), slice(o * OCT_S, (o + 1) * OCT_S)


def first_kernel(
    cut, arrived, rim, embed_w, embed_b, places, positions, mask_token, gain1, qkv_w, bias,
    across, ones, out_w, out_b, gain2, cotangent, down_w, up_w, up_b, start_o, qkv_o, probs_o,
    context_o, middle_o, act_o, grad_up_o, down_o, up_o, up_bias_o, slots_s, score_s, down_s, up_s,
):
    rows, width = start_o.shape
    own = arrived.shape[0]
    hidden = up_w.shape[1]
    step = pl.program_id(0)
    last = step == pl.num_programs(0) - 1

    @pl.when(step == 0)
    def _():
        slots_s[0:own, :] = (mm(arrived[...], embed_w[...]) + embed_b[...]).astype(bf16)
        slots_s[own:, :] = (mm(rim[...], embed_w[...]) + embed_b[...]).astype(bf16)
        down_s[...] = jnp.zeros_like(down_s)
        up_s[...] = jnp.zeros_like(up_s)
        up_bias_o[...] = jnp.zeros_like(up_bias_o)

    onehot = slot_onehot(step, rows, places[...])
    seen = jnp.sum(onehot, axis=1, keepdims=True)
    start = mm(onehot.astype(bf16), slots_s[...]) + (1.0 - seen) * mask_token[...] + positions[...]
    start_o[...] = start
    h_one = (normalized(start)[0] * gain1[...]).astype(bf16)
    qkv_o[...] = mm(h_one, qkv_w[...]).astype(bf16)
    block_ones = ones[...]
    windows = rows // SPOTS
    for w in range(windows):
        cut_w = cut[step * windows + w]
        for o in range(HEADS // OCT):
            r, s = head_slices(w, o)
            q = qkv_o[r, o * OCT_D : (o + 1) * OCT_D]
            k = qkv_o[r, width + o * OCT_D : width + (o + 1) * OCT_D]
            raw = mm_nt(k, spread(q, block_ones)) * SCALE + bias[:, s]
            score_s[r, s] = raw + cut_w * across[:, s]
    scores = score_s[...].reshape(windows, SPOTS, HEADS * SPOTS)
    expd = jnp.exp(scores - jnp.max(scores, axis=1, keepdims=True))
    probs = expd / jnp.sum(expd, axis=1, keepdims=True)
    probs_o[...] = probs.reshape(rows, HEADS * SPOTS)
    for w in range(windows):
        for o in range(HEADS // OCT):
            r, s = head_slices(w, o)
            v = qkv_o[r, 2 * width + o * OCT_D : 2 * width + (o + 1) * OCT_D]
            context_o[r, o * OCT_D : (o + 1) * OCT_D] = own_heads(
                mm_tn(probs_o[r, s].astype(bf16), v)
            ).astype(bf16)
    middle = start_o[...] + mm(context_o[...], out_w[...]) + out_b[...]
    middle_o[...] = middle
    h_two = (normalized(middle)[0] * gain2[...]).astype(bf16)

    cot = cotangent[...]
    piece = min(FEED_PIECE, hidden)
    for at in range(0, hidden, piece):
        f = slice(at, at + piece)
        up_value = mm(h_two, up_w[:, f]) + up_b[:, f]
        below = 0.5 * (1.0 + lax.erf(up_value * (0.5**0.5)))
        act = (up_value * below).astype(bf16)
        act_o[:, f] = act
        slope = below + up_value * (jnp.exp(-0.5 * up_value * up_value) * 0.3989422804014327)
        grad_up = mm_nt(cot, down_w[f, :]) * slope
        up_bias_o[:, f] += jnp.sum(grad_up, axis=0, keepdims=True)
        grad_low = grad_up.astype(bf16)
        grad_up_o[:, f] = grad_low
        down_s[f, :] += mm_tn(act, cot)
        up_s[:, f] += mm_tn(h_two, grad_low)

    @pl.when(last)
    def _():
        down_o[...] = down_s[...].astype(bf16)
        up_o[...] = up_s[...].astype(bf16)


def second_kernel(
    core, qkv, probs, start, grad_up, middle, context, cotangent, places, qkv_w, gain1, ones,
    arrived, rim, up_bias, up_w, gain2, out_w, slots_o, keep_c_o, send_c_o, keep_d_o, send_d_o,
    gqkv_s, qkv_s, score_s, slots_s, embed_s, sums_s, rel_s, out_s, grad_context_s, grad_middle_s,
):
    step = pl.program_id(0)
    rows, width = start.shape
    own, e_in = arrived.shape
    windows = rows // SPOTS

    @pl.when(step == 0)
    def _():
        qkv_s[...] = jnp.zeros_like(qkv_s)
        slots_s[...] = jnp.zeros_like(slots_s)
        sums_s[...] = jnp.zeros_like(sums_s)
        embed_s[...] = jnp.zeros_like(embed_s)
        rel_s[...] = jnp.zeros_like(rel_s)
        out_s[...] = jnp.zeros_like(out_s)

    cot = cotangent[...].astype(f32)
    grad_h_two = mm_nt(grad_up[...], up_w[...])
    n2, r2 = normalized(middle[...])
    sums_s[0:1, :] += jnp.sum(grad_h_two * n2, axis=0, keepdims=True)
    grad_middle = cot + norm_back(grad_h_two * gain2[...], n2, r2)
    grad_middle_s[...] = grad_middle
    sums_s[1:2, :] += jnp.sum(grad_middle, axis=0, keepdims=True)
    sums_s[2:3, :] += jnp.sum(cot, axis=0, keepdims=True)
    grad_middle_low = grad_middle.astype(bf16)
    out_s[...] += mm_tn(context[...], grad_middle_low)
    grad_context_s[...] = mm_nt(grad_middle_low, out_w[...]).astype(bf16)
    block_ones = ones[...]
    for w in range(windows):
        for o in range(HEADS // OCT):
            r, s = head_slices(w, o)
            heads = slice(o * OCT_D, (o + 1) * OCT_D)
            v_at = slice(2 * width + o * OCT_D, 2 * width + (o + 1) * OCT_D)
            wide = spread(grad_context_s[r, heads], block_ones)
            score_s[r, s] = mm_nt(qkv[r, v_at], wide)
            gqkv_s[r, v_at] = mm(probs[r, s].astype(bf16), wide).astype(bf16)
    pr = probs[...].reshape(windows, SPOTS, HEADS * SPOTS)
    grad_probs = score_s[...].reshape(windows, SPOTS, HEADS * SPOTS)
    delta = jnp.sum(grad_probs * pr, axis=1, keepdims=True)
    grad_scores = pr * (grad_probs - delta)
    rel_s[...] += jnp.sum(grad_scores, axis=0)
    score_s[...] = grad_scores.reshape(rows, HEADS * SPOTS)
    for w in range(windows):
        for o in range(HEADS // OCT):
            r, s = head_slices(w, o)
            q_at = slice(o * OCT_D, (o + 1) * OCT_D)
            k_at = slice(width + o * OCT_D, width + (o + 1) * OCT_D)
            low = score_s[r, s].astype(bf16)
            gqkv_s[r, q_at] = (own_heads(mm_tn(low, qkv[r, k_at])) * SCALE).astype(bf16)
            gqkv_s[r, k_at] = (mm(low, spread(qkv[r, q_at], block_ones)) * SCALE).astype(bf16)

    n1, r1 = normalized(start[...])
    h_one = (n1 * gain1[...]).astype(bf16)
    qkv_s[...] += mm_tn(h_one, gqkv_s[...])
    grad_h_one = mm_nt(gqkv_s[...], qkv_w[...])
    sums_s[3:4, :] += jnp.sum(grad_h_one * n1, axis=0, keepdims=True)
    grad_start = grad_middle_s[...] + norm_back(grad_h_one * gain1[...], n1, r1)
    onehot = slot_onehot(step, rows, places[...])
    hidden = 1.0 - jnp.sum(onehot, axis=1, keepdims=True)
    sums_s[4:5, :] += jnp.sum(hidden * grad_start, axis=0, keepdims=True)
    slots_s[...] += mm_tn(onehot.astype(bf16), grad_start.astype(bf16))

    def give_c(low_o, high_o):
        low_o[0:width, :] = qkv_s[:, 0:width].astype(bf16)
        low_o[width : 2 * width, :] = qkv_s[:, width : 2 * width].astype(bf16)
        high_o[0:width, :] = qkv_s[:, 2 * width : 3 * width].astype(bf16)
        high_o[width : 2 * width, :] = out_s[...].astype(bf16)

    def give_d(low_o, high_o):
        half = low_o.shape[0]
        low_o[...] = embed_s[0:half, :].astype(bf16)
        left = e_in - half
        high_o[...] = jnp.zeros_like(high_o)
        if left > 0:
            high_o[0:left, :] = embed_s[half:e_in, :].astype(bf16)
        left = max(left, 0)
        high_o[left : left + 16, :] = sums_s[...].astype(bf16)
        high_o[left + 16 : left + 16 + SPOTS, 0 : HEADS * SPOTS] = rel_s[...].astype(bf16)

    last = step == pl.num_programs(0) - 1

    @pl.when(last)
    def _():
        slots = slots_s[...].astype(bf16)
        slots_o[...] = slots
        embed_s[0:e_in, :] = mm_tn(arrived[...], slots[0:own]) + mm_tn(rim[...], slots[own:])
        sums_s[5:6, :] = jnp.sum(slots.astype(f32), axis=0, keepdims=True)
        for block in range(up_bias.shape[1] // width):
            sums_s[6 + block : 7 + block, :] = up_bias[:, block * width : (block + 1) * width]

    @pl.when(last & (core[0] == 0))
    def _():
        give_c(keep_c_o, send_c_o)
        give_d(keep_d_o, send_d_o)

    @pl.when(last & (core[0] == 1))
    def _():
        give_c(send_c_o, keep_c_o)
        give_d(send_d_o, keep_d_o)


def rim_back_kernel(hot, rim_grad, grad_slots, after_a, after_b, out):
    del after_a, after_b
    slots = out.shape[0]
    out[...] = (grad_slots[0:slots, :].astype(f32) + mm_tn(hot[...], rim_grad[...])).astype(bf16)


def prepare_kernel(cotangent, next_cot, pos_embed, order, cot_o, positions_o):
    block = order.shape[0]
    tokens = cotangent.shape[0]
    for at in range(0, tokens, block):
        if at + block < tokens:
            rows = cotangent[at + RIM : at + RIM + block, :]
        else:
            rows = jnp.concatenate([cotangent[at + RIM :, :], next_cot[...]], axis=0)
        cot_o[at : at + block, :] = mm(order[...].astype(bf16), rows).astype(bf16)
    grid_rows = pos_embed.shape[0]
    for at in range(0, grid_rows, block):
        if at + block < grid_rows:
            rows = pos_embed[at + RIM : at + RIM + block, :]
        else:
            rows = jnp.concatenate([pos_embed[at + RIM :, :], pos_embed[0:RIM, :]], axis=0)
        positions_o[at : at + block, :] = jnp.dot(
            order[...], rows, precision=PRECISE, preferred_element_type=f32
        )


def out_kernel(
    middle, act, down, down_bias, order, after, out_o, rim_o
):
    del after
    step = pl.program_id(0)
    last = pl.num_programs(0) - 1
    rows = middle.shape[0]
    block = order.shape[0]
    result = (
        middle[...] + mm(act[...], down[...]) + down_bias[...]
    ).astype(bf16)
    result = jnp.concatenate(
        [mm_tn(order[...], result[b : b + block]).astype(bf16) for b in range(0, rows, block)],
        axis=0,
    )

    @pl.when(step < last)
    def _():
        out_o[pl.ds(pl.multiple_of(step * rows + RIM, RIM), rows), :] = result

    @pl.when(step == last)
    def _():
        out_o[pl.ds(pl.multiple_of(step * rows + RIM, RIM), rows - RIM), :] = result[: rows - RIM]
        rim_o[...] = result[rows - RIM :]
        out_o[0:RIM, :] = jnp.zeros((RIM, result.shape[1]), bf16)


def chip_join_kernel(count, *refs):
    parts, out = refs[: 2 * count], refs[-1]
    at = 0
    for keep, got in zip(parts[::2], parts[1::2]):
        rows = keep.shape[1]
        out[0, at : at + rows, :] = (keep[0].astype(f32) + got[0].astype(f32)).astype(bf16)
        at += rows


def plane_sum_kernel(count, place, *refs):
    parts, outs, total_s = refs[:count], refs[count + 1 : -1], refs[-1]
    if count == 1:
        total_s[...] = jnp.sum(parts[0][...].astype(f32), axis=0)
    else:
        total = parts[0][...].astype(f32)
        for part in parts[1:]:
            total = total + part[...].astype(f32)
        total_s[...] = total
    rows = outs[0].shape[0]
    for b, out in enumerate(outs):
        at = pl.multiple_of(lax.bitwise_xor(place[0], b) * rows, 8)
        out[...] = total_s[pl.ds(at, rows), :].astype(bf16)


def z_sum_kernel(count, *refs):
    parts, out = refs[:count], refs[-1]
    total = parts[0][...].astype(f32)
    for part in parts[1:]:
        total = total + part[...].astype(f32)
    out[...] = total.astype(bf16)


def z_join_kernel(count, place, *refs):
    out = refs[-1]
    for b, ref in enumerate(refs[:count]):
        share = ref[...]
        at = lax.bitwise_xor(place[0], b)
        for cell in range(out.shape[0]):
            out[cell, at] = share


def widen_kernel(down, up, down_o, up_o):
    down_o[...] = down[...].astype(f32)
    up_o[...] = up[...].astype(f32)


def rest_unpack_kernel(split, core, mine, other, qkv_o, out_o, embed_o, *small_o):
    width = out_o.shape[1]
    e_in = embed_o.shape[0]

    def give(low, high):
        rows = low[:, 0:split].reshape(-1, width).astype(f32)
        qkv_o[:, 0:width] = rows[0:width]
        qkv_o[:, width : 2 * width] = rows[width:]
        rows = high[:, 0:split].reshape(-1, width).astype(f32)
        qkv_o[:, 2 * width :] = rows[0:width]
        out_o[...] = rows[width:]
        rows = low[:, split:].reshape(-1, width).astype(f32)
        half = rows.shape[0]
        embed_o[0 : min(half, e_in), :] = rows[0 : min(half, e_in)]
        rows = high[:, split:].reshape(-1, width).astype(f32)
        left = max(e_in - half, 0)
        if left:
            embed_o[half:e_in, :] = rows[0:left]
        for i, vector_o in enumerate(small_o[:6]):
            vector_o[...] = rows[left + i]
        up_bias_o, rel_o = small_o[6:]
        for i in range(up_bias_o.shape[0] // width):
            up_bias_o[i * width : (i + 1) * width] = rows[left + 6 + i]
        rel_o[...] = rows[left + 16 : left + 16 + SPOTS, 0 : HEADS * SPOTS]

    @pl.when(core[0] == 0)
    def _():
        give(mine, other)

    @pl.when(core[0] == 1)
    def _():
        give(other, mine)


ANY = pl.BlockSpec(memory_space=pl.ANY)
SMEM = pl.BlockSpec(memory_space=pltpu.SMEM)


def whole(s):
    return pl.BlockSpec(s, lambda *i: (0,) * len(s))


def held(s):
    return pl.BlockSpec(s, lambda *i: (0,) * len(s), pipeline_mode=pl.Buffered(1))


def tile(rows, width, first=0):
    return pl.BlockSpec((rows, width), lambda i: (i + first, 0))


def params():
    return pltpu.CompilerParams(vmem_limit_bytes=VMEM_LIMIT)


def shape(s, d):
    return jax.ShapeDtypeStruct(s, d)


def at_once(kernel, args, outs, specs=None, scratch=()):
    if specs is None:
        specs = [whole(a.shape) for a in args]
    many = isinstance(outs, (list, tuple))
    out_specs = [whole(o.shape) for o in outs] if many else whole(outs.shape)
    return pl.pallas_call(
        kernel,
        grid=(1,),
        in_specs=specs,
        out_specs=out_specs,
        out_shape=outs,
        scratch_shapes=list(scratch),
        compiler_params=params(),
    )(*args)


def swap_cores(x):
    return lax.ppermute(x, "c", [(0, 1), (1, 0)])


def exchange(x, axis):
    return lax.all_to_all(x, axis, 0, 0, tiled=True)


def across(x, axis):
    size = lax.axis_size(axis)
    return [lax.ppermute(x[b], axis, [(i, i ^ b) for i in range(size)]) for b in range(1, size)]


def chip_join(pairs, after):
    cells = lax.axis_size("p")
    width = pairs[0][0].shape[1]
    refs = [a.reshape(cells, -1, width) for keep, send in pairs for a in (keep, swap_cores(send))]
    rows = sum(r.shape[1] for r in refs[::2])
    return pl.pallas_call(
        partial(chip_join_kernel, len(pairs)),
        grid=(cells,),
        in_specs=[pl.BlockSpec((1, *r.shape[1:]), lambda i: (i, 0, 0)) for r in refs] + [ANY] * len(after),
        out_specs=pl.BlockSpec((1, rows, width), lambda i: (i, 0, 0)),
        out_shape=shape((cells, rows, width), bf16),
        compiler_params=params(),
    )(*refs, *after)


def plane_sum(place, parts, after):
    planes = lax.axis_size("z")
    rows, width = parts[0].shape[-2:]
    return at_once(
        partial(plane_sum_kernel, len(parts)),
        (place, *parts, after),
        [shape((rows // planes, width), bf16)] * planes,
        [SMEM] + [whole(p.shape) for p in parts] + [ANY],
        [pltpu.VMEM((rows, width), f32)],
    )


def z_sum(parts, after):
    return at_once(
        partial(z_sum_kernel, len(parts)),
        (*parts, *after),
        shape(parts[0].shape, bf16),
        [whole(p.shape) for p in parts] + [ANY] * len(after),
    )


def z_join(place, parts, after):
    cells = lax.axis_size("p")
    return at_once(
        partial(z_join_kernel, len(parts)),
        (place, *parts, *after),
        shape((cells, len(parts), *parts[0].shape), bf16),
        [SMEM] + [whole(p.shape) for p in parts] + [ANY] * len(after),
    )


def order_matrix(block):
    token = np.arange(block)
    group, rest = token // (WIN * BANDS), token % (WIN * BANDS)
    frame, band = rest // BANDS, rest % BANDS
    row = group * (WIN * BANDS) + (band // WIN) * SPOTS + frame * WIN + band % WIN
    matrix = np.zeros((block, block), np.float32)
    matrix[row, token] = 1.0
    return matrix


def per_device(
    visible, embed_weight, embed_bias, mask_token, pos_embed, norm1_gain, qkv_weight, rel_table,
    out_weight, out_bias, norm2_gain, up_weight, up_bias, down_weight, down_bias, cotangent,
    visible_index, slot_counts, segment_ids,
):
    device_count = lax.axis_size(AXES)
    device_rank = lax.axis_index(AXES)
    core = lax.axis_index("c").reshape(1).astype(jnp.int32)
    z_place = lax.axis_index("z").reshape(1).astype(jnp.int32)
    planes, cells = lax.axis_size("z"), lax.axis_size("p")
    tokens, width = cotangent.shape
    frames = tokens // BANDS
    hidden = down_weight.shape[0]
    e_in = visible.shape[1]
    slot_rows = visible_index.shape[2]
    slots = device_count * slot_rows
    ext = slots + RIM_SLOTS
    back = [(i, (i - 1) % device_count) for i in range(device_count)]
    ahead = [(i, (i + 1) % device_count) for i in range(device_count)]
    row = lambda v: v.reshape(1, -1)

    arrived = exchange(visible, AXES)

    spot = visible_index.reshape(slots)
    live = (
        jnp.arange(slot_rows)[None, :] < slot_counts.reshape(device_count, 1)
    ).reshape(slots)
    rim_hot = ((jnp.arange(RIM)[:, None] == spot[None, :]) & live[None, :]).astype(bf16)
    rim_seen = jnp.sum(rim_hot.astype(f32), axis=1, keepdims=True).astype(bf16)
    sent_back = jnp.concatenate(
        [cotangent[:RIM], jnp.broadcast_to(rim_seen, (RIM, width))], axis=0
    )
    from_next = lax.ppermute(sent_back, AXES, back)
    next_seen = from_next[RIM:, 0].astype(f32)
    own_places = jnp.where(live & (spot >= RIM), window_row(spot - RIM), -1)
    rim_places = jnp.where(
        next_seen > 0.5, window_row(tokens - RIM + np.arange(RIM)), -1
    )
    places = jnp.concatenate(
        [own_places, rim_places, np.full((RIM_SLOTS - RIM,), -1, np.int32)]
    ).reshape(1, ext).astype(jnp.int32)

    seg_cycle = jnp.concatenate([segment_ids, segment_ids[:SHIFT]])
    seg_tape = lax.dynamic_slice_in_dim(seg_cycle, device_rank * frames + SHIFT, frames)
    seg_win = seg_tape.reshape(frames // WIN, WIN)
    cut = jnp.repeat(
        (seg_win[:, SHIFT - 1] != seg_win[:, SHIFT]).astype(f32), BANDS // WIN
    )

    spots = np.arange(SPOTS)
    frame_of, band_of = spots // WIN, spots % WIN
    rels = 2 * WIN - 1
    rel_index = (frame_of[:, None] - frame_of[None, :] + WIN - 1) * rels + (
        band_of[:, None] - band_of[None, :] + WIN - 1
    )
    rel_hot = (rel_index[:, :, None] == np.arange(rels * rels)).astype(np.float32)
    bias = jnp.einsum("hr,ijr->jhi", rel_table, rel_hot, precision=PRECISE).reshape(
        SPOTS, HEADS * SPOTS
    )
    halves = frame_of // SHIFT
    apart = np.tile(
        np.where(halves[:, None] != halves[None, :], MASKED, 0.0).astype(np.float32), (1, HEADS)
    )
    ones = jnp.asarray(
        np.arange(OCT_S)[:, None] // SPOTS == np.arange(OCT_D)[None, :] // HD, bf16
    )
    order = order_matrix(256)
    cot, positions = at_once(
        prepare_kernel,
        (cotangent, from_next[:RIM], pos_embed, order),
        [shape(cotangent.shape, bf16), shape(pos_embed.shape, f32)],
    )

    tm = min(512, tokens)
    grid = (tokens // tm,)
    pos_blocks = pos_embed.shape[0] // tm
    rim_rows = jnp.dot(rim_hot, arrived, preferred_element_type=f32).astype(bf16)
    next_rows = lax.ppermute(rim_rows, AXES, back)
    rim = jnp.pad(next_rows, ((0, RIM_SLOTS - RIM), (0, 0)))
    first_args = [
        cut, arrived, rim, embed_weight, row(embed_bias), places, positions,
        row(mask_token), row(norm1_gain), qkv_weight, bias, apart, ones, out_weight,
        row(out_bias), row(norm2_gain), cot, down_weight, up_weight, row(up_bias),
    ]
    specs = [SMEM] + [held(a.shape) for a in first_args[1:]]
    specs[6] = pl.BlockSpec((tm, width), lambda i: (lax.rem(i, pos_blocks), 0))
    specs[16] = tile(tm, width)
    start, qkv, probs, context, middle, act, grad_up, down_grad, up_grad, up_bias_grad = (
        pl.pallas_call(
            first_kernel,
            grid=grid,
            in_specs=specs,
            out_specs=[
                tile(tm, width),
                tile(tm, 3 * width),
                tile(tm, HEADS * SPOTS),
                tile(tm, width),
                tile(tm, width),
                tile(tm, hidden),
                tile(tm, hidden),
                whole((hidden, width)),
                whole((width, hidden)),
                whole((1, hidden)),
            ],
            out_shape=[
                shape((tokens, width), f32),
                shape((tokens, 3 * width), bf16),
                shape((tokens, HEADS * SPOTS), f32),
                shape((tokens, width), bf16),
                shape((tokens, width), f32),
                shape((tokens, hidden), bf16),
                shape((tokens, hidden), bf16),
                shape((hidden, width), bf16),
                shape((width, hidden), bf16),
                shape((1, hidden), f32),
            ],
            scratch_shapes=[
                pltpu.VMEM((ext, width), bf16),
                pltpu.VMEM((tm, HEADS * SPOTS), f32),
                pltpu.VMEM((hidden, width), f32),
                pltpu.VMEM((width, hidden), f32),
            ],
            compiler_params=params(),
        )(*first_args)
    )
    down_sum, up_sum = lax.psum((down_grad, up_grad), AXES)

    unit = 16 * planes * cells
    half = -(-width // unit) * unit
    def rest(operands):
        (
            qkv, probs, start, grad_up, middle, context, cot, act, places, arrived, rim, rim_hot,
            up_bias_grad,
        ) = operands
        grad_slots, keep_c, send_c, keep_d, send_d = pl.pallas_call(
            second_kernel,
            grid=grid,
            in_specs=[
                SMEM,
                tile(tm, 3 * width),
                tile(tm, HEADS * SPOTS),
                tile(tm, width),
                tile(tm, hidden),
                tile(tm, width),
                tile(tm, width),
                tile(tm, width),
                held((1, ext)),
                held((width, 3 * width)),
                held((1, width)),
                held((OCT_S, OCT_D)),
                held((slots, e_in)),
                held((RIM_SLOTS, e_in)),
                held((1, hidden)),
                held((width, hidden)),
                held((1, width)),
                held((width, width)),
            ],
            out_specs=[
                whole((ext, width)),
                whole((2 * width, width)),
                whole((2 * width, width)),
                whole((half, width)),
                whole((half, width)),
            ],
            out_shape=[
                shape((ext, width), bf16),
                shape((2 * width, width), bf16),
                shape((2 * width, width), bf16),
                shape((half, width), bf16),
                shape((half, width), bf16),
            ],
            scratch_shapes=[
                pltpu.VMEM((tm, 3 * width), bf16),
                pltpu.VMEM((width, 3 * width), f32),
                pltpu.VMEM((tm, HEADS * SPOTS), f32),
                pltpu.VMEM((ext, width), f32),
                pltpu.VMEM((max(e_in, half), width), f32),
                pltpu.VMEM((16, width), f32),
                pltpu.VMEM((SPOTS, HEADS * SPOTS), f32),
                pltpu.VMEM((width, width), f32),
                pltpu.VMEM((tm, width), bf16),
                pltpu.VMEM((tm, width), f32),
            ],
            compiler_params=params(),
        )(
            core, qkv, probs, start, grad_up, middle, context, cot, places, qkv_weight,
            row(norm1_gain), ones, arrived, rim, up_bias_grad, up_weight, row(norm2_gain),
            out_weight,
        )
        rim_grad = lax.ppermute(grad_slots[slots : slots + RIM], AXES, ahead)
        shares = chip_join([(keep_c, send_c), (keep_d, send_d)], ())
        part = exchange(shares, "p")
        out, rim_out = pl.pallas_call(
            out_kernel,
            grid=grid,
            in_specs=[
                tile(tm, width),
                tile(tm, hidden),
                held((hidden, width)),
                held((1, width)),
                held(order.shape),
                ANY,
            ],
            out_specs=[whole((tokens, width)), whole((RIM, width))],
            out_shape=[shape((tokens, width), bf16), shape((RIM, width), bf16)],
            compiler_params=params(),
        )(middle, act, down_weight, row(down_bias), jnp.asarray(order, bf16), shares)
        first_rows = lax.ppermute(rim_out, AXES, ahead)
        out = lax.dynamic_update_slice(out, first_rows, (0, 0))
        sums_c = plane_sum(z_place, [part], rim_out)
        grad_embedded = at_once(
            rim_back_kernel,
            (rim_hot, rim_grad, grad_slots, sums_c[0], first_rows),
            shape((slots, width), bf16),
            [whole(a.shape) for a in (rim_hot, rim_grad, grad_slots)] + [ANY, ANY],
        )
        returned = exchange(grad_embedded, AXES)
        grad_visible = lax.dot_general(
            returned, embed_weight, (((1,), (1,)), ((), ())), preferred_element_type=f32
        ).astype(bf16)
        total = z_sum([sums_c[0], *across(sums_c, "z")], ())
        joined = z_join(z_place, [total, *across([total] * planes, "z")], (returned,))
        mine = exchange(joined, "p").reshape(cells, -1, width)
        return out, grad_visible, mine, swap_cores(mine)

    def nothing(operands):
        return tuple(jnp.zeros(o.shape, o.dtype) for o in jax.eval_shape(rest, operands))

    operands = (
        qkv, probs, start, grad_up, middle, context, cot, act, places, arrived, rim, rim_hot,
        up_bias_grad,
    )
    out, grad_visible, mine, other = lax.cond(device_rank < device_count, rest, nothing, operands)

    vector = shape((width,), f32)
    (
        grad_qkv_weight, grad_out_weight, grad_embed_weight, grad_norm2_gain, grad_out_bias,
        grad_down_bias, grad_norm1_gain, grad_mask_token, grad_embed_bias, grad_up_bias, rel_sums,
    ) = at_once(
        partial(rest_unpack_kernel, 2 * width // cells),
        (core, mine, other),
        [
            shape((width, 3 * width), f32),
            shape((width, width), f32),
            shape((e_in, width), f32),
            *[vector] * 6,
            shape((hidden,), f32),
            shape((SPOTS, HEADS * SPOTS), f32),
        ],
        [SMEM, whole(mine.shape), whole(other.shape)],
    )
    grad_rel = jnp.einsum(
        "jhi,ijr->hr", rel_sums.reshape(SPOTS, HEADS, SPOTS), rel_hot, precision=PRECISE
    )
    grad_down_weight, grad_up_weight = pl.pallas_call(
        widen_kernel,
        grid=(4,),
        in_specs=[tile(hidden // 4, width), tile(width // 4, hidden)],
        out_specs=[tile(hidden // 4, width), tile(width // 4, hidden)],
        out_shape=[shape((hidden, width), f32), shape((width, hidden), f32)],
        compiler_params=params(),
    )(down_sum, up_sum)
    return (
        out,
        grad_visible,
        grad_embed_weight,
        grad_embed_bias,
        grad_mask_token,
        grad_norm1_gain,
        grad_qkv_weight,
        grad_rel,
        grad_out_weight,
        grad_out_bias,
        grad_norm2_gain,
        grad_up_weight,
        grad_up_bias,
        grad_down_weight,
        grad_down_bias,
    )


def solution(mesh):
    planes = 4
    grid = Mesh(mesh.devices.reshape(planes, -1, 2), AXES)
    split = P(AXES)
    in_specs = (split,) + (P(),) * 14 + (split, split, split, P())
    out_specs = (split, split) + (P(),) * 13
    return jax.shard_map(
        per_device, mesh=grid, in_specs=in_specs, out_specs=out_specs, check_vma=False
    )
```

```python
from functools import partial

import jax
import jax.numpy as jnp
import numpy as np
from jax import lax
from jax.experimental import pallas as pl
from jax.experimental.pallas import tpu as pltpu
from jax.sharding import Mesh, PartitionSpec as P

HEADS = 16
HD = 32
BANDS = 8
WIN = 4
SHIFT = 2
RIM = SHIFT * BANDS
SPOTS = WIN * WIN
OCT = 8
OCT_D = OCT * HD
OCT_S = OCT * SPOTS
RIM_SLOTS = 128
EPSILON = 1e-06
MASKED = -1e30
SCALE = HD ** (-0.5)
PRECISE = lax.Precision.HIGHEST
VMEM_LIMIT = 60 * 2**20
FEED_PIECE = 1024
bf16 = jnp.bfloat16
f32 = jnp.float32
AXES = ("z", "p", "c")


def mm(a, b):
    return jnp.dot(a, b, preferred_element_type=f32)


def mm_nt(a, b):
    return lax.dot_general(a, b, (((1,), (1,)), ((), ())), preferred_element_type=f32)


def mm_tn(a, b):
    return lax.dot_general(a, b, (((0,), (0,)), ((), ())), preferred_element_type=f32)


def window_order(x):
    return (
        x.reshape(-1, WIN, BANDS // WIN, WIN, x.shape[-1])
        .transpose(0, 2, 1, 3, 4)
        .reshape(x.shape)
    )


def frame_order(x):
    return (
        x.reshape(-1, BANDS // WIN, WIN, WIN, x.shape[-1])
        .transpose(0, 2, 1, 3, 4)
        .reshape(x.shape)
    )


def window_row(token):
    group, rest = token // (WIN * BANDS), token % (WIN * BANDS)
    frame, band = rest // BANDS, rest % BANDS
    return group * (WIN * BANDS) + (band // WIN) * SPOTS + frame * WIN + band % WIN


def spread(x, block_ones):
    return jnp.concatenate([x] * OCT, axis=0) * block_ones


def own_heads(z):
    lane_head = lax.broadcasted_iota(jnp.int32, (SPOTS, 128), 1) // HD
    halves = []
    per = 128 // HD
    for t in range(OCT_D // 128):
        total = None
        for q in range(per):
            piece = z[(t * per + q) * SPOTS : (t * per + q + 1) * SPOTS, t * 128 : (t + 1) * 128]
            piece = jnp.where(lane_head == q, piece, 0.0)
            total = piece if total is None else total + piece
        halves.append(total)
    return jnp.concatenate(halves, axis=1)


def normalized(x):
    centred = x - jnp.mean(x, axis=-1, keepdims=True)
    inverse = lax.rsqrt(jnp.mean(centred * centred, axis=-1, keepdims=True) + EPSILON)
    return centred * inverse, inverse


def norm_back(grad, n, inverse):
    return inverse * (
        grad
        - jnp.mean(grad, axis=-1, keepdims=True)
        - n * jnp.mean(grad * n, axis=-1, keepdims=True)
    )


def slot_onehot(step, rows, places):
    row = lax.broadcasted_iota(jnp.int32, (rows, places.shape[1]), 0) + step * rows
    return jnp.where(row == places, 1.0, 0.0)


def head_slices(w, o):
    return slice(w * SPOTS, (w + 1) * SPOTS), slice(o * OCT_S, (o + 1) * OCT_S)


def first_kernel(
    cut, arrived, rim, embed_w, embed_b, places, positions, mask_token, gain1, qkv_w, bias,
    across, ones, out_w, out_b, gain2, cotangent, down_w, up_w, up_b, start_o, qkv_o, probs_o,
    context_o, middle_o, act_o, grad_up_o, down_o, up_o, up_bias_o, slots_s, score_s, down_s, up_s,
):
    rows, width = start_o.shape
    own = arrived.shape[0]
    hidden = up_w.shape[1]
    step = pl.program_id(0)
    last = step == pl.num_programs(0) - 1

    @pl.when(step == 0)
    def _():
        slots_s[0:own, :] = (mm(arrived[...], embed_w[...]) + embed_b[...]).astype(bf16)
        slots_s[own:, :] = (mm(rim[...], embed_w[...]) + embed_b[...]).astype(bf16)
        down_s[...] = jnp.zeros_like(down_s)
        up_s[...] = jnp.zeros_like(up_s)
        up_bias_o[...] = jnp.zeros_like(up_bias_o)

    onehot = slot_onehot(step, rows, places[...])
    seen = jnp.sum(onehot, axis=1, keepdims=True)
    start = mm(onehot.astype(bf16), slots_s[...]) + (1.0 - seen) * mask_token[...] + positions[...]
    start_o[...] = start
    h_one = (normalized(start)[0] * gain1[...]).astype(bf16)
    qkv_o[...] = mm(h_one, qkv_w[...]).astype(bf16)
    block_ones = ones[...]
    windows = rows // SPOTS
    for w in range(windows):
        cut_w = cut[step * windows + w]
        for o in range(HEADS // OCT):
            r, s = head_slices(w, o)
            q = qkv_o[r, o * OCT_D : (o + 1) * OCT_D]
            k = qkv_o[r, width + o * OCT_D : width + (o + 1) * OCT_D]
            raw = mm_nt(k, spread(q, block_ones)) * SCALE + bias[:, s]
            score_s[r, s] = raw + cut_w * across[:, s]
    scores = score_s[...].reshape(windows, SPOTS, HEADS * SPOTS)
    expd = jnp.exp(scores - jnp.max(scores, axis=1, keepdims=True))
    probs = expd / jnp.sum(expd, axis=1, keepdims=True)
    probs_o[...] = probs.reshape(rows, HEADS * SPOTS)
    for w in range(windows):
        for o in range(HEADS // OCT):
            r, s = head_slices(w, o)
            v = qkv_o[r, 2 * width + o * OCT_D : 2 * width + (o + 1) * OCT_D]
            context_o[r, o * OCT_D : (o + 1) * OCT_D] = own_heads(
                mm_tn(probs_o[r, s].astype(bf16), v)
            ).astype(bf16)
    middle = start_o[...] + mm(context_o[...], out_w[...]) + out_b[...]
    middle_o[...] = middle
    h_two = (normalized(middle)[0] * gain2[...]).astype(bf16)

    cot = cotangent[...]
    piece = min(FEED_PIECE, hidden)
    for at in range(0, hidden, piece):
        f = slice(at, at + piece)
        up_value = mm(h_two, up_w[:, f]) + up_b[:, f]
        below = 0.5 * (1.0 + lax.erf(up_value * (0.5**0.5)))
        act = (up_value * below).astype(bf16)
        act_o[:, f] = act
        slope = below + up_value * (jnp.exp(-0.5 * up_value * up_value) * 0.3989422804014327)
        grad_up = mm_nt(cot, down_w[f, :]) * slope
        up_bias_o[:, f] += jnp.sum(grad_up, axis=0, keepdims=True)
        grad_low = grad_up.astype(bf16)
        grad_up_o[:, f] = grad_low
        down_s[f, :] += mm_tn(act, cot)
        up_s[:, f] += mm_tn(h_two, grad_low)

    @pl.when(last)
    def _():
        down_o[...] = down_s[...].astype(bf16)
        up_o[...] = up_s[...].astype(bf16)


def second_kernel(
    core, qkv, probs, start, grad_up, middle, context, cotangent, places, qkv_w, gain1, ones,
    arrived, rim, up_bias, up_w, gain2, out_w, slots_o, keep_c_o, send_c_o, keep_d_o, send_d_o,
    gqkv_s, qkv_s, score_s, slots_s, embed_s, sums_s, rel_s, out_s, grad_context_s, grad_middle_s,
):
    step = pl.program_id(0)
    rows, width = start.shape
    own, e_in = arrived.shape
    windows = rows // SPOTS

    @pl.when(step == 0)
    def _():
        qkv_s[...] = jnp.zeros_like(qkv_s)
        slots_s[...] = jnp.zeros_like(slots_s)
        sums_s[...] = jnp.zeros_like(sums_s)
        embed_s[...] = jnp.zeros_like(embed_s)
        rel_s[...] = jnp.zeros_like(rel_s)
        out_s[...] = jnp.zeros_like(out_s)

    cot = cotangent[...].astype(f32)
    grad_h_two = mm_nt(grad_up[...], up_w[...])
    n2, r2 = normalized(middle[...])
    sums_s[0:1, :] += jnp.sum(grad_h_two * n2, axis=0, keepdims=True)
    grad_middle = cot + norm_back(grad_h_two * gain2[...], n2, r2)
    grad_middle_s[...] = grad_middle
    sums_s[1:2, :] += jnp.sum(grad_middle, axis=0, keepdims=True)
    sums_s[2:3, :] += jnp.sum(cot, axis=0, keepdims=True)
    grad_middle_low = grad_middle.astype(bf16)
    out_s[...] += mm_tn(context[...], grad_middle_low)
    grad_context_s[...] = mm_nt(grad_middle_low, out_w[...]).astype(bf16)
    block_ones = ones[...]
    for w in range(windows):
        for o in range(HEADS // OCT):
            r, s = head_slices(w, o)
            heads = slice(o * OCT_D, (o + 1) * OCT_D)
            v_at = slice(2 * width + o * OCT_D, 2 * width + (o + 1) * OCT_D)
            wide = spread(grad_context_s[r, heads], block_ones)
            score_s[r, s] = mm_nt(qkv[r, v_at], wide)
            gqkv_s[r, v_at] = mm(probs[r, s].astype(bf16), wide).astype(bf16)
    pr = probs[...].reshape(windows, SPOTS, HEADS * SPOTS)
    grad_probs = score_s[...].reshape(windows, SPOTS, HEADS * SPOTS)
    delta = jnp.sum(grad_probs * pr, axis=1, keepdims=True)
    grad_scores = pr * (grad_probs - delta)
    rel_s[...] += jnp.sum(grad_scores, axis=0)
    score_s[...] = grad_scores.reshape(rows, HEADS * SPOTS)
    for w in range(windows):
        for o in range(HEADS // OCT):
            r, s = head_slices(w, o)
            q_at = slice(o * OCT_D, (o + 1) * OCT_D)
            k_at = slice(width + o * OCT_D, width + (o + 1) * OCT_D)
            low = score_s[r, s].astype(bf16)
            gqkv_s[r, q_at] = (own_heads(mm_tn(low, qkv[r, k_at])) * SCALE).astype(bf16)
            gqkv_s[r, k_at] = (mm(low, spread(qkv[r, q_at], block_ones)) * SCALE).astype(bf16)

    n1, r1 = normalized(start[...])
    h_one = (n1 * gain1[...]).astype(bf16)
    qkv_s[...] += mm_tn(h_one, gqkv_s[...])
    grad_h_one = mm_nt(gqkv_s[...], qkv_w[...])
    sums_s[3:4, :] += jnp.sum(grad_h_one * n1, axis=0, keepdims=True)
    grad_start = grad_middle_s[...] + norm_back(grad_h_one * gain1[...], n1, r1)
    onehot = slot_onehot(step, rows, places[...])
    hidden = 1.0 - jnp.sum(onehot, axis=1, keepdims=True)
    sums_s[4:5, :] += jnp.sum(hidden * grad_start, axis=0, keepdims=True)
    slots_s[...] += mm_tn(onehot.astype(bf16), grad_start.astype(bf16))

    def give_c(low_o, high_o):
        low_o[0:width, :] = qkv_s[:, 0:width].astype(bf16)
        low_o[width : 2 * width, :] = qkv_s[:, width : 2 * width].astype(bf16)
        high_o[0:width, :] = qkv_s[:, 2 * width : 3 * width].astype(bf16)
        high_o[width : 2 * width, :] = out_s[...].astype(bf16)

    def give_d(low_o, high_o):
        half = low_o.shape[0]
        low_o[...] = embed_s[0:half, :].astype(bf16)
        left = e_in - half
        high_o[...] = jnp.zeros_like(high_o)
        if left > 0:
            high_o[0:left, :] = embed_s[half:e_in, :].astype(bf16)
        left = max(left, 0)
        high_o[left : left + 16, :] = sums_s[...].astype(bf16)
        high_o[left + 16 : left + 16 + SPOTS, 0 : HEADS * SPOTS] = rel_s[...].astype(bf16)

    last = step == pl.num_programs(0) - 1

    @pl.when(last)
    def _():
        slots = slots_s[...].astype(bf16)
        slots_o[...] = slots
        embed_s[0:e_in, :] = mm_tn(arrived[...], slots[0:own]) + mm_tn(rim[...], slots[own:])
        sums_s[5:6, :] = jnp.sum(slots.astype(f32), axis=0, keepdims=True)
        for block in range(up_bias.shape[1] // width):
            sums_s[6 + block : 7 + block, :] = up_bias[:, block * width : (block + 1) * width]

    @pl.when(last & (core[0] == 0))
    def _():
        give_c(keep_c_o, send_c_o)
        give_d(keep_d_o, send_d_o)

    @pl.when(last & (core[0] == 1))
    def _():
        give_c(send_c_o, keep_c_o)
        give_d(send_d_o, keep_d_o)


def rim_back_kernel(hot, rim_grad, grad_slots, after_a, after_b, out):
    del after_a, after_b
    slots = out.shape[0]
    out[...] = (grad_slots[0:slots, :].astype(f32) + mm_tn(hot[...], rim_grad[...])).astype(bf16)


def prepare_kernel(cotangent, next_cot, pos_embed, order, cot_o, positions_o):
    block = order.shape[0]
    tokens = cotangent.shape[0]
    for at in range(0, tokens, block):
        if at + block < tokens:
            rows = cotangent[at + RIM : at + RIM + block, :]
        else:
            rows = jnp.concatenate([cotangent[at + RIM :, :], next_cot[...]], axis=0)
        cot_o[at : at + block, :] = mm(order[...].astype(bf16), rows).astype(bf16)
    grid_rows = pos_embed.shape[0]
    for at in range(0, grid_rows, block):
        if at + block < grid_rows:
            rows = pos_embed[at + RIM : at + RIM + block, :]
        else:
            rows = jnp.concatenate([pos_embed[at + RIM :, :], pos_embed[0:RIM, :]], axis=0)
        positions_o[at : at + block, :] = jnp.dot(
            order[...], rows, precision=PRECISE, preferred_element_type=f32
        )


def out_kernel(
    middle, act, down, down_bias, order, after, out_o, rim_o
):
    del after
    step = pl.program_id(0)
    last = pl.num_programs(0) - 1
    rows = middle.shape[0]
    block = order.shape[0]
    result = (
        middle[...] + mm(act[...], down[...]) + down_bias[...]
    ).astype(bf16)
    result = jnp.concatenate(
        [mm_tn(order[...], result[b : b + block]).astype(bf16) for b in range(0, rows, block)],
        axis=0,
    )

    @pl.when(step < last)
    def _():
        out_o[pl.ds(pl.multiple_of(step * rows + RIM, RIM), rows), :] = result

    @pl.when(step == last)
    def _():
        out_o[pl.ds(pl.multiple_of(step * rows + RIM, RIM), rows - RIM), :] = result[: rows - RIM]
        rim_o[...] = result[rows - RIM :]
        out_o[0:RIM, :] = jnp.zeros((RIM, result.shape[1]), bf16)


def chip_join_kernel(count, *refs):
    parts, out = refs[: 2 * count], refs[-1]
    at = 0
    for keep, got in zip(parts[::2], parts[1::2]):
        rows = keep.shape[1]
        out[0, at : at + rows, :] = (keep[0].astype(f32) + got[0].astype(f32)).astype(bf16)
        at += rows


def plane_sum_kernel(count, place, *refs):
    parts, outs, total_s = refs[:count], refs[count + 1 : -1], refs[-1]
    if count == 1:
        total_s[...] = jnp.sum(parts[0][...].astype(f32), axis=0)
    else:
        total = parts[0][...].astype(f32)
        for part in parts[1:]:
            total = total + part[...].astype(f32)
        total_s[...] = total
    rows = outs[0].shape[0]
    for b, out in enumerate(outs):
        at = pl.multiple_of(lax.bitwise_xor(place[0], b) * rows, 8)
        out[...] = total_s[pl.ds(at, rows), :].astype(bf16)


def z_sum_kernel(count, *refs):
    parts, out = refs[:count], refs[-1]
    total = parts[0][...].astype(f32)
    for part in parts[1:]:
        total = total + part[...].astype(f32)
    out[...] = total.astype(bf16)


def z_join_kernel(count, place, *refs):
    out = refs[-1]
    for b, ref in enumerate(refs[:count]):
        share = ref[...]
        at = lax.bitwise_xor(place[0], b)
        for cell in range(out.shape[0]):
            out[cell, at] = share


def unpack_kernel(split, core, down, up, mine, other, down_o, up_o, qkv_o, out_o, embed_o, *small_o):
    step = pl.program_id(0)
    down_o[...] = down[...].astype(f32)
    up_o[...] = up[...].astype(f32)
    width = out_o.shape[1]
    e_in = embed_o.shape[0]

    def give(low, high):
        rows = low[:, 0:split].reshape(-1, width).astype(f32)
        qkv_o[:, 0:width] = rows[0:width]
        qkv_o[:, width : 2 * width] = rows[width:]
        rows = high[:, 0:split].reshape(-1, width).astype(f32)
        qkv_o[:, 2 * width :] = rows[0:width]
        out_o[...] = rows[width:]
        rows = low[:, split:].reshape(-1, width).astype(f32)
        half = rows.shape[0]
        embed_o[0 : min(half, e_in), :] = rows[0 : min(half, e_in)]
        rows = high[:, split:].reshape(-1, width).astype(f32)
        left = max(e_in - half, 0)
        if left:
            embed_o[half:e_in, :] = rows[0:left]
        for i, vector_o in enumerate(small_o[:6]):
            vector_o[...] = rows[left + i]
        up_bias_o, rel_o = small_o[6:]
        for i in range(up_bias_o.shape[0] // width):
            up_bias_o[i * width : (i + 1) * width] = rows[left + 6 + i]
        rel_o[...] = rows[left + 16 : left + 16 + SPOTS, 0 : HEADS * SPOTS]

    @pl.when((step == 0) & (core[0] == 0))
    def _():
        give(mine, other)

    @pl.when((step == 0) & (core[0] == 1))
    def _():
        give(other, mine)


ANY = pl.BlockSpec(memory_space=pl.ANY)
SMEM = pl.BlockSpec(memory_space=pltpu.SMEM)


def whole(s):
    return pl.BlockSpec(s, lambda *i: (0,) * len(s))


def held(s):
    return pl.BlockSpec(s, lambda *i: (0,) * len(s), pipeline_mode=pl.Buffered(1))


def tile(rows, width, first=0):
    return pl.BlockSpec((rows, width), lambda i: (i + first, 0))


def params():
    return pltpu.CompilerParams(vmem_limit_bytes=VMEM_LIMIT)


def shape(s, d):
    return jax.ShapeDtypeStruct(s, d)


def at_once(kernel, args, outs, specs=None, scratch=()):
    if specs is None:
        specs = [whole(a.shape) for a in args]
    many = isinstance(outs, (list, tuple))
    out_specs = [whole(o.shape) for o in outs] if many else whole(outs.shape)
    return pl.pallas_call(
        kernel,
        grid=(1,),
        in_specs=specs,
        out_specs=out_specs,
        out_shape=outs,
        scratch_shapes=list(scratch),
        compiler_params=params(),
    )(*args)


def swap_cores(x):
    return lax.ppermute(x, "c", [(0, 1), (1, 0)])


def exchange(x, axis):
    return lax.all_to_all(x, axis, 0, 0, tiled=True)


def across(x, axis):
    size = lax.axis_size(axis)
    return [lax.ppermute(x[b], axis, [(i, i ^ b) for i in range(size)]) for b in range(1, size)]


def chip_join(pairs, after):
    cells = lax.axis_size("p")
    width = pairs[0][0].shape[1]
    refs = [a.reshape(cells, -1, width) for keep, send in pairs for a in (keep, swap_cores(send))]
    rows = sum(r.shape[1] for r in refs[::2])
    return pl.pallas_call(
        partial(chip_join_kernel, len(pairs)),
        grid=(cells,),
        in_specs=[pl.BlockSpec((1, *r.shape[1:]), lambda i: (i, 0, 0)) for r in refs] + [ANY] * len(after),
        out_specs=pl.BlockSpec((1, rows, width), lambda i: (i, 0, 0)),
        out_shape=shape((cells, rows, width), bf16),
        compiler_params=params(),
    )(*refs, *after)


def plane_sum(place, parts, after):
    planes = lax.axis_size("z")
    rows, width = parts[0].shape[-2:]
    return at_once(
        partial(plane_sum_kernel, len(parts)),
        (place, *parts, after),
        [shape((rows // planes, width), bf16)] * planes,
        [SMEM] + [whole(p.shape) for p in parts] + [ANY],
        [pltpu.VMEM((rows, width), f32)],
    )


def z_sum(parts, after):
    return at_once(
        partial(z_sum_kernel, len(parts)),
        (*parts, *after),
        shape(parts[0].shape, bf16),
        [whole(p.shape) for p in parts] + [ANY] * len(after),
    )


def z_join(place, parts, after):
    cells = lax.axis_size("p")
    return at_once(
        partial(z_join_kernel, len(parts)),
        (place, *parts, *after),
        shape((cells, len(parts), *parts[0].shape), bf16),
        [SMEM] + [whole(p.shape) for p in parts] + [ANY] * len(after),
    )


def order_matrix(block):
    token = np.arange(block)
    group, rest = token // (WIN * BANDS), token % (WIN * BANDS)
    frame, band = rest // BANDS, rest % BANDS
    row = group * (WIN * BANDS) + (band // WIN) * SPOTS + frame * WIN + band % WIN
    matrix = np.zeros((block, block), np.float32)
    matrix[row, token] = 1.0
    return matrix


def per_device(
    visible, embed_weight, embed_bias, mask_token, pos_embed, norm1_gain, qkv_weight, rel_table,
    out_weight, out_bias, norm2_gain, up_weight, up_bias, down_weight, down_bias, cotangent,
    visible_index, slot_counts, segment_ids,
):
    device_count = lax.axis_size(AXES)
    device_rank = lax.axis_index(AXES)
    core = lax.axis_index("c").reshape(1).astype(jnp.int32)
    z_place = lax.axis_index("z").reshape(1).astype(jnp.int32)
    planes, cells = lax.axis_size("z"), lax.axis_size("p")
    tokens, width = cotangent.shape
    frames = tokens // BANDS
    hidden = down_weight.shape[0]
    e_in = visible.shape[1]
    slot_rows = visible_index.shape[2]
    slots = device_count * slot_rows
    ext = slots + RIM_SLOTS
    back = [(i, (i - 1) % device_count) for i in range(device_count)]
    ahead = [(i, (i + 1) % device_count) for i in range(device_count)]
    row = lambda v: v.reshape(1, -1)

    arrived = exchange(visible, AXES)

    spot = visible_index.reshape(slots)
    live = (
        jnp.arange(slot_rows)[None, :] < slot_counts.reshape(device_count, 1)
    ).reshape(slots)
    rim_hot = ((jnp.arange(RIM)[:, None] == spot[None, :]) & live[None, :]).astype(bf16)
    rim_seen = jnp.sum(rim_hot.astype(f32), axis=1, keepdims=True).astype(bf16)
    sent_back = jnp.concatenate(
        [cotangent[:RIM], jnp.broadcast_to(rim_seen, (RIM, width))], axis=0
    )
    from_next = lax.ppermute(sent_back, AXES, back)
    next_seen = from_next[RIM:, 0].astype(f32)
    own_places = jnp.where(live & (spot >= RIM), window_row(spot - RIM), -1)
    rim_places = jnp.where(
        next_seen > 0.5, window_row(tokens - RIM + np.arange(RIM)), -1
    )
    places = jnp.concatenate(
        [own_places, rim_places, np.full((RIM_SLOTS - RIM,), -1, np.int32)]
    ).reshape(1, ext).astype(jnp.int32)

    seg_cycle = jnp.concatenate([segment_ids, segment_ids[:SHIFT]])
    seg_tape = lax.dynamic_slice_in_dim(seg_cycle, device_rank * frames + SHIFT, frames)
    seg_win = seg_tape.reshape(frames // WIN, WIN)
    cut = jnp.repeat(
        (seg_win[:, SHIFT - 1] != seg_win[:, SHIFT]).astype(f32), BANDS // WIN
    )

    spots = np.arange(SPOTS)
    frame_of, band_of = spots // WIN, spots % WIN
    rels = 2 * WIN - 1
    rel_index = (frame_of[:, None] - frame_of[None, :] + WIN - 1) * rels + (
        band_of[:, None] - band_of[None, :] + WIN - 1
    )
    rel_hot = (rel_index[:, :, None] == np.arange(rels * rels)).astype(np.float32)
    bias = jnp.einsum("hr,ijr->jhi", rel_table, rel_hot, precision=PRECISE).reshape(
        SPOTS, HEADS * SPOTS
    )
    halves = frame_of // SHIFT
    apart = np.tile(
        np.where(halves[:, None] != halves[None, :], MASKED, 0.0).astype(np.float32), (1, HEADS)
    )
    ones = jnp.asarray(
        np.arange(OCT_S)[:, None] // SPOTS == np.arange(OCT_D)[None, :] // HD, bf16
    )
    order = order_matrix(256)
    cot, positions = at_once(
        prepare_kernel,
        (cotangent, from_next[:RIM], pos_embed, order),
        [shape(cotangent.shape, bf16), shape(pos_embed.shape, f32)],
    )

    tm = min(512, tokens)
    grid = (tokens // tm,)
    pos_blocks = pos_embed.shape[0] // tm
    rim_rows = jnp.dot(rim_hot, arrived, preferred_element_type=f32).astype(bf16)
    next_rows = lax.ppermute(rim_rows, AXES, back)
    rim = jnp.pad(next_rows, ((0, RIM_SLOTS - RIM), (0, 0)))
    first_args = [
        cut, arrived, rim, embed_weight, row(embed_bias), places, positions,
        row(mask_token), row(norm1_gain), qkv_weight, bias, apart, ones, out_weight,
        row(out_bias), row(norm2_gain), cot, down_weight, up_weight, row(up_bias),
    ]
    specs = [SMEM] + [held(a.shape) for a in first_args[1:]]
    specs[6] = pl.BlockSpec((tm, width), lambda i: (lax.rem(i, pos_blocks), 0))
    specs[16] = tile(tm, width)
    start, qkv, probs, context, middle, act, grad_up, down_grad, up_grad, up_bias_grad = (
        pl.pallas_call(
            first_kernel,
            grid=grid,
            in_specs=specs,
            out_specs=[
                tile(tm, width),
                tile(tm, 3 * width),
                tile(tm, HEADS * SPOTS),
                tile(tm, width),
                tile(tm, width),
                tile(tm, hidden),
                tile(tm, hidden),
                whole((hidden, width)),
                whole((width, hidden)),
                whole((1, hidden)),
            ],
            out_shape=[
                shape((tokens, width), f32),
                shape((tokens, 3 * width), bf16),
                shape((tokens, HEADS * SPOTS), f32),
                shape((tokens, width), bf16),
                shape((tokens, width), f32),
                shape((tokens, hidden), bf16),
                shape((tokens, hidden), bf16),
                shape((hidden, width), bf16),
                shape((width, hidden), bf16),
                shape((1, hidden), f32),
            ],
            scratch_shapes=[
                pltpu.VMEM((ext, width), bf16),
                pltpu.VMEM((tm, HEADS * SPOTS), f32),
                pltpu.VMEM((hidden, width), f32),
                pltpu.VMEM((width, hidden), f32),
            ],
            compiler_params=params(),
        )(*first_args)
    )
    down_sum, up_sum = lax.psum((down_grad, up_grad), AXES)

    unit = 16 * planes * cells
    half = -(-width // unit) * unit
    def rest(operands):
        (
            qkv, probs, start, grad_up, middle, context, cot, act, places, arrived, rim, rim_hot,
            up_bias_grad,
        ) = operands
        grad_slots, keep_c, send_c, keep_d, send_d = pl.pallas_call(
            second_kernel,
            grid=grid,
            in_specs=[
                SMEM,
                tile(tm, 3 * width),
                tile(tm, HEADS * SPOTS),
                tile(tm, width),
                tile(tm, hidden),
                tile(tm, width),
                tile(tm, width),
                tile(tm, width),
                held((1, ext)),
                held((width, 3 * width)),
                held((1, width)),
                held((OCT_S, OCT_D)),
                held((slots, e_in)),
                held((RIM_SLOTS, e_in)),
                held((1, hidden)),
                held((width, hidden)),
                held((1, width)),
                held((width, width)),
            ],
            out_specs=[
                whole((ext, width)),
                whole((2 * width, width)),
                whole((2 * width, width)),
                whole((half, width)),
                whole((half, width)),
            ],
            out_shape=[
                shape((ext, width), bf16),
                shape((2 * width, width), bf16),
                shape((2 * width, width), bf16),
                shape((half, width), bf16),
                shape((half, width), bf16),
            ],
            scratch_shapes=[
                pltpu.VMEM((tm, 3 * width), bf16),
                pltpu.VMEM((width, 3 * width), f32),
                pltpu.VMEM((tm, HEADS * SPOTS), f32),
                pltpu.VMEM((ext, width), f32),
                pltpu.VMEM((max(e_in, half), width), f32),
                pltpu.VMEM((16, width), f32),
                pltpu.VMEM((SPOTS, HEADS * SPOTS), f32),
                pltpu.VMEM((width, width), f32),
                pltpu.VMEM((tm, width), bf16),
                pltpu.VMEM((tm, width), f32),
            ],
            compiler_params=params(),
        )(
            core, qkv, probs, start, grad_up, middle, context, cot, places, qkv_weight,
            row(norm1_gain), ones, arrived, rim, up_bias_grad, up_weight, row(norm2_gain),
            out_weight,
        )
        rim_grad = lax.ppermute(grad_slots[slots : slots + RIM], AXES, ahead)
        shares = chip_join([(keep_c, send_c), (keep_d, send_d)], ())
        part = exchange(shares, "p")
        out, rim_out = pl.pallas_call(
            out_kernel,
            grid=grid,
            in_specs=[
                tile(tm, width),
                tile(tm, hidden),
                held((hidden, width)),
                held((1, width)),
                held(order.shape),
                ANY,
            ],
            out_specs=[whole((tokens, width)), whole((RIM, width))],
            out_shape=[shape((tokens, width), bf16), shape((RIM, width), bf16)],
            compiler_params=params(),
        )(middle, act, down_weight, row(down_bias), jnp.asarray(order, bf16), shares)
        first_rows = lax.ppermute(rim_out, AXES, ahead)
        out = lax.dynamic_update_slice(out, first_rows, (0, 0))
        sums_c = plane_sum(z_place, [part], rim_out)
        grad_embedded = at_once(
            rim_back_kernel,
            (rim_hot, rim_grad, grad_slots, sums_c[0], first_rows),
            shape((slots, width), bf16),
            [whole(a.shape) for a in (rim_hot, rim_grad, grad_slots)] + [ANY, ANY],
        )
        returned = exchange(grad_embedded, AXES)
        grad_visible = lax.dot_general(
            returned, embed_weight, (((1,), (1,)), ((), ())), preferred_element_type=f32
        ).astype(bf16)
        total = z_sum([sums_c[0], *across(sums_c, "z")], ())
        joined = z_join(z_place, [total, *across([total] * planes, "z")], (returned,))
        mine = exchange(joined, "p").reshape(cells, -1, width)
        return out, grad_visible, mine, swap_cores(mine)

    def nothing(operands):
        return tuple(jnp.zeros(o.shape, o.dtype) for o in jax.eval_shape(rest, operands))

    operands = (
        qkv, probs, start, grad_up, middle, context, cot, act, places, arrived, rim, rim_hot,
        up_bias_grad,
    )
    out, grad_visible, mine, other = lax.cond(device_rank < device_count, rest, nothing, operands)

    vector = shape((width,), f32)
    unpacked = [
        shape((width, 3 * width), f32),
        shape((width, width), f32),
        shape((e_in, width), f32),
        *[vector] * 6,
        shape((hidden,), f32),
        shape((SPOTS, HEADS * SPOTS), f32),
    ]
    turns = 4
    wide = [tile(hidden // turns, width), tile(width // turns, hidden)]
    (
        grad_down_weight, grad_up_weight, grad_qkv_weight, grad_out_weight, grad_embed_weight,
        grad_norm2_gain, grad_out_bias, grad_down_bias, grad_norm1_gain, grad_mask_token,
        grad_embed_bias, grad_up_bias, rel_sums,
    ) = pl.pallas_call(
        partial(unpack_kernel, 2 * width // cells),
        grid=(turns,),
        in_specs=[SMEM, *wide, held(mine.shape), held(other.shape)],
        out_specs=wide + [whole(o.shape) for o in unpacked],
        out_shape=[shape((hidden, width), f32), shape((width, hidden), f32), *unpacked],
        compiler_params=params(),
    )(core, down_sum, up_sum, mine, other)
    grad_rel = jnp.einsum(
        "jhi,ijr->hr", rel_sums.reshape(SPOTS, HEADS, SPOTS), rel_hot, precision=PRECISE
    )
    return (
        out,
        grad_visible,
        grad_embed_weight,
        grad_embed_bias,
        grad_mask_token,
        grad_norm1_gain,
        grad_qkv_weight,
        grad_rel,
        grad_out_weight,
        grad_out_bias,
        grad_norm2_gain,
        grad_up_weight,
        grad_up_bias,
        grad_down_weight,
        grad_down_bias,
    )


def solution(mesh):
    planes = 4
    grid = Mesh(mesh.devices.reshape(planes, -1, 2), AXES)
    split = P(AXES)
    in_specs = (split,) + (P(),) * 14 + (split, split, split, P())
    out_specs = (split, split) + (P(),) * 13
    return jax.shard_map(
        per_device, mesh=grid, in_specs=in_specs, out_specs=out_specs, check_vma=False
    )
```

```python
from functools import partial

import jax
import jax.numpy as jnp
import numpy as np
from jax import lax
from jax.experimental import pallas as pl
from jax.experimental.pallas import tpu as pltpu
from jax.sharding import Mesh, PartitionSpec as P

HEADS = 16
HD = 32
BANDS = 8
WIN = 4
SHIFT = 2
RIM = SHIFT * BANDS
SPOTS = WIN * WIN
OCT = 8
OCT_D = OCT * HD
OCT_S = OCT * SPOTS
RIM_SLOTS = 128
EPSILON = 1e-06
MASKED = -1e30
SCALE = HD ** (-0.5)
PRECISE = lax.Precision.HIGHEST
VMEM_LIMIT = 60 * 2**20
FEED_PIECE = 1024
bf16 = jnp.bfloat16
f32 = jnp.float32
AXES = ("z", "p", "c")


def mm(a, b):
    return jnp.dot(a, b, preferred_element_type=f32)


def mm_nt(a, b):
    return lax.dot_general(a, b, (((1,), (1,)), ((), ())), preferred_element_type=f32)


def mm_tn(a, b):
    return lax.dot_general(a, b, (((0,), (0,)), ((), ())), preferred_element_type=f32)


def window_order(x):
    return (
        x.reshape(-1, WIN, BANDS // WIN, WIN, x.shape[-1])
        .transpose(0, 2, 1, 3, 4)
        .reshape(x.shape)
    )


def frame_order(x):
    return (
        x.reshape(-1, BANDS // WIN, WIN, WIN, x.shape[-1])
        .transpose(0, 2, 1, 3, 4)
        .reshape(x.shape)
    )


def window_row(token):
    group, rest = token // (WIN * BANDS), token % (WIN * BANDS)
    frame, band = rest // BANDS, rest % BANDS
    return group * (WIN * BANDS) + (band // WIN) * SPOTS + frame * WIN + band % WIN


def spread(x, block_ones):
    return jnp.concatenate([x] * OCT, axis=0) * block_ones


def own_heads(z):
    lane_head = lax.broadcasted_iota(jnp.int32, (SPOTS, 128), 1) // HD
    halves = []
    per = 128 // HD
    for t in range(OCT_D // 128):
        total = None
        for q in range(per):
            piece = z[(t * per + q) * SPOTS : (t * per + q + 1) * SPOTS, t * 128 : (t + 1) * 128]
            piece = jnp.where(lane_head == q, piece, 0.0)
            total = piece if total is None else total + piece
        halves.append(total)
    return jnp.concatenate(halves, axis=1)


def normalized(x):
    centred = x - jnp.mean(x, axis=-1, keepdims=True)
    inverse = lax.rsqrt(jnp.mean(centred * centred, axis=-1, keepdims=True) + EPSILON)
    return centred * inverse, inverse


def norm_back(grad, n, inverse):
    return inverse * (
        grad
        - jnp.mean(grad, axis=-1, keepdims=True)
        - n * jnp.mean(grad * n, axis=-1, keepdims=True)
    )


def slot_onehot(step, rows, places):
    row = lax.broadcasted_iota(jnp.int32, (rows, places.shape[1]), 0) + step * rows
    return jnp.where(row == places, 1.0, 0.0)


def head_slices(w, o):
    return slice(w * SPOTS, (w + 1) * SPOTS), slice(o * OCT_S, (o + 1) * OCT_S)


def first_kernel(
    cut, arrived, rim, embed_w, embed_b, places, positions, mask_token, gain1, qkv_w, bias,
    across, ones, out_w, out_b, gain2, cotangent, down_w, up_w, up_b, start_o, qkv_o, probs_o,
    context_o, middle_o, act_o, grad_up_o, down_o, up_o, up_bias_o, slots_s, score_s, down_s, up_s,
):
    rows, width = start_o.shape
    own = arrived.shape[0]
    hidden = up_w.shape[1]
    step = pl.program_id(0)
    last = step == pl.num_programs(0) - 1

    @pl.when(step == 0)
    def _():
        slots_s[0:own, :] = (mm(arrived[...], embed_w[...]) + embed_b[...]).astype(bf16)
        slots_s[own:, :] = (mm(rim[...], embed_w[...]) + embed_b[...]).astype(bf16)
        down_s[...] = jnp.zeros_like(down_s)
        up_s[...] = jnp.zeros_like(up_s)
        up_bias_o[...] = jnp.zeros_like(up_bias_o)

    onehot = slot_onehot(step, rows, places[...])
    seen = jnp.sum(onehot, axis=1, keepdims=True)
    start = mm(onehot.astype(bf16), slots_s[...]) + (1.0 - seen) * mask_token[...] + positions[...]
    start_o[...] = start
    h_one = (normalized(start)[0] * gain1[...]).astype(bf16)
    qkv_o[...] = mm(h_one, qkv_w[...]).astype(bf16)
    block_ones = ones[...]
    windows = rows // SPOTS
    for w in range(windows):
        cut_w = cut[step * windows + w]
        for o in range(HEADS // OCT):
            r, s = head_slices(w, o)
            q = qkv_o[r, o * OCT_D : (o + 1) * OCT_D]
            k = qkv_o[r, width + o * OCT_D : width + (o + 1) * OCT_D]
            raw = mm_nt(k, spread(q, block_ones)) * SCALE + bias[:, s]
            score_s[r, s] = raw + cut_w * across[:, s]
    scores = score_s[...].reshape(windows, SPOTS, HEADS * SPOTS)
    expd = jnp.exp(scores - jnp.max(scores, axis=1, keepdims=True))
    probs = expd / jnp.sum(expd, axis=1, keepdims=True)
    probs_o[...] = probs.reshape(rows, HEADS * SPOTS)
    for w in range(windows):
        for o in range(HEADS // OCT):
            r, s = head_slices(w, o)
            v = qkv_o[r, 2 * width + o * OCT_D : 2 * width + (o + 1) * OCT_D]
            context_o[r, o * OCT_D : (o + 1) * OCT_D] = own_heads(
                mm_tn(probs_o[r, s].astype(bf16), v)
            ).astype(bf16)
    middle = start_o[...] + mm(context_o[...], out_w[...]) + out_b[...]
    middle_o[...] = middle
    h_two = (normalized(middle)[0] * gain2[...]).astype(bf16)

    cot = cotangent[...]
    piece = min(FEED_PIECE, hidden)
    for at in range(0, hidden, piece):
        f = slice(at, at + piece)
        up_value = mm(h_two, up_w[:, f]) + up_b[:, f]
        below = 0.5 * (1.0 + lax.erf(up_value * (0.5**0.5)))
        act = (up_value * below).astype(bf16)
        act_o[:, f] = act
        slope = below + up_value * (jnp.exp(-0.5 * up_value * up_value) * 0.3989422804014327)
        grad_up = mm_nt(cot, down_w[f, :]) * slope
        up_bias_o[:, f] += jnp.sum(grad_up, axis=0, keepdims=True)
        grad_low = grad_up.astype(bf16)
        grad_up_o[:, f] = grad_low
        down_s[f, :] += mm_tn(act, cot)
        up_s[:, f] += mm_tn(h_two, grad_low)

    @pl.when(last)
    def _():
        down_o[...] = down_s[...].astype(bf16)
        up_o[...] = up_s[...].astype(bf16)


def second_kernel(
    core, qkv, probs, start, grad_up, middle, context, cotangent, places, qkv_w, gain1, ones,
    arrived, rim, up_bias, up_w, gain2, out_w, slots_o, keep_c_o, send_c_o, keep_d_o, send_d_o,
    gqkv_s, qkv_s, score_s, slots_s, embed_s, sums_s, rel_s, out_s, grad_context_s, grad_middle_s,
):
    step = pl.program_id(0)
    rows, width = start.shape
    own, e_in = arrived.shape
    windows = rows // SPOTS

    @pl.when(step == 0)
    def _():
        qkv_s[...] = jnp.zeros_like(qkv_s)
        slots_s[...] = jnp.zeros_like(slots_s)
        sums_s[...] = jnp.zeros_like(sums_s)
        embed_s[...] = jnp.zeros_like(embed_s)
        rel_s[...] = jnp.zeros_like(rel_s)
        out_s[...] = jnp.zeros_like(out_s)

    cot = cotangent[...].astype(f32)
    grad_h_two = mm_nt(grad_up[...], up_w[...])
    n2, r2 = normalized(middle[...])
    sums_s[0:1, :] += jnp.sum(grad_h_two * n2, axis=0, keepdims=True)
    grad_middle = cot + norm_back(grad_h_two * gain2[...], n2, r2)
    grad_middle_s[...] = grad_middle
    sums_s[1:2, :] += jnp.sum(grad_middle, axis=0, keepdims=True)
    sums_s[2:3, :] += jnp.sum(cot, axis=0, keepdims=True)
    grad_middle_low = grad_middle.astype(bf16)
    out_s[...] += mm_tn(context[...], grad_middle_low)
    grad_context_s[...] = mm_nt(grad_middle_low, out_w[...]).astype(bf16)
    block_ones = ones[...]
    for w in range(windows):
        for o in range(HEADS // OCT):
            r, s = head_slices(w, o)
            heads = slice(o * OCT_D, (o + 1) * OCT_D)
            v_at = slice(2 * width + o * OCT_D, 2 * width + (o + 1) * OCT_D)
            wide = spread(grad_context_s[r, heads], block_ones)
            score_s[r, s] = mm_nt(qkv[r, v_at], wide)
            gqkv_s[r, v_at] = mm(probs[r, s].astype(bf16), wide).astype(bf16)
    pr = probs[...].reshape(windows, SPOTS, HEADS * SPOTS)
    grad_probs = score_s[...].reshape(windows, SPOTS, HEADS * SPOTS)
    delta = jnp.sum(grad_probs * pr, axis=1, keepdims=True)
    grad_scores = pr * (grad_probs - delta)
    rel_s[...] += jnp.sum(grad_scores, axis=0)
    score_s[...] = grad_scores.reshape(rows, HEADS * SPOTS)
    for w in range(windows):
        for o in range(HEADS // OCT):
            r, s = head_slices(w, o)
            q_at = slice(o * OCT_D, (o + 1) * OCT_D)
            k_at = slice(width + o * OCT_D, width + (o + 1) * OCT_D)
            low = score_s[r, s].astype(bf16)
            gqkv_s[r, q_at] = (own_heads(mm_tn(low, qkv[r, k_at])) * SCALE).astype(bf16)
            gqkv_s[r, k_at] = (mm(low, spread(qkv[r, q_at], block_ones)) * SCALE).astype(bf16)

    n1, r1 = normalized(start[...])
    h_one = (n1 * gain1[...]).astype(bf16)
    qkv_s[...] += mm_tn(h_one, gqkv_s[...])
    grad_h_one = mm_nt(gqkv_s[...], qkv_w[...])
    sums_s[3:4, :] += jnp.sum(grad_h_one * n1, axis=0, keepdims=True)
    grad_start = grad_middle_s[...] + norm_back(grad_h_one * gain1[...], n1, r1)
    onehot = slot_onehot(step, rows, places[...])
    hidden = 1.0 - jnp.sum(onehot, axis=1, keepdims=True)
    sums_s[4:5, :] += jnp.sum(hidden * grad_start, axis=0, keepdims=True)
    slots_s[...] += mm_tn(onehot.astype(bf16), grad_start.astype(bf16))

    def give_c(low_o, high_o):
        low_o[0:width, :] = qkv_s[:, 0:width].astype(bf16)
        low_o[width : 2 * width, :] = qkv_s[:, width : 2 * width].astype(bf16)
        high_o[0:width, :] = qkv_s[:, 2 * width : 3 * width].astype(bf16)
        high_o[width : 2 * width, :] = out_s[...].astype(bf16)

    def give_d(low_o, high_o):
        half = low_o.shape[0]
        low_o[...] = embed_s[0:half, :].astype(bf16)
        left = e_in - half
        high_o[...] = jnp.zeros_like(high_o)
        if left > 0:
            high_o[0:left, :] = embed_s[half:e_in, :].astype(bf16)
        left = max(left, 0)
        high_o[left : left + 16, :] = sums_s[...].astype(bf16)
        high_o[left + 16 : left + 16 + SPOTS, 0 : HEADS * SPOTS] = rel_s[...].astype(bf16)

    last = step == pl.num_programs(0) - 1

    @pl.when(last)
    def _():
        slots = slots_s[...].astype(bf16)
        slots_o[...] = slots
        embed_s[0:e_in, :] = mm_tn(arrived[...], slots[0:own]) + mm_tn(rim[...], slots[own:])
        sums_s[5:6, :] = jnp.sum(slots.astype(f32), axis=0, keepdims=True)
        for block in range(up_bias.shape[1] // width):
            sums_s[6 + block : 7 + block, :] = up_bias[:, block * width : (block + 1) * width]

    @pl.when(last & (core[0] == 0))
    def _():
        give_c(keep_c_o, send_c_o)
        give_d(keep_d_o, send_d_o)

    @pl.when(last & (core[0] == 1))
    def _():
        give_c(send_c_o, keep_c_o)
        give_d(send_d_o, keep_d_o)


def rim_back_kernel(hot, rim_grad, grad_slots, after_a, after_b, out):
    del after_a, after_b
    slots = out.shape[0]
    out[...] = (grad_slots[0:slots, :].astype(f32) + mm_tn(hot[...], rim_grad[...])).astype(bf16)


def prepare_kernel(cotangent, next_cot, pos_embed, order, cot_o, positions_o):
    block = order.shape[0]
    tokens = cotangent.shape[0]
    for at in range(0, tokens, block):
        if at + block < tokens:
            rows = cotangent[at + RIM : at + RIM + block, :]
        else:
            rows = jnp.concatenate([cotangent[at + RIM :, :], next_cot[...]], axis=0)
        cot_o[at : at + block, :] = mm(order[...].astype(bf16), rows).astype(bf16)
    grid_rows = pos_embed.shape[0]
    for at in range(0, grid_rows, block):
        if at + block < grid_rows:
            rows = pos_embed[at + RIM : at + RIM + block, :]
        else:
            rows = jnp.concatenate([pos_embed[at + RIM :, :], pos_embed[0:RIM, :]], axis=0)
        positions_o[at : at + block, :] = jnp.dot(
            order[...], rows, precision=PRECISE, preferred_element_type=f32
        )


def out_kernel(
    middle, act, down, down_bias, order, after, out_o, rim_o
):
    del after
    step = pl.program_id(0)
    last = pl.num_programs(0) - 1
    rows = middle.shape[0]
    block = order.shape[0]
    result = (
        middle[...] + mm(act[...], down[...]) + down_bias[...]
    ).astype(bf16)
    result = jnp.concatenate(
        [mm_tn(order[...], result[b : b + block]).astype(bf16) for b in range(0, rows, block)],
        axis=0,
    )

    @pl.when(step < last)
    def _():
        out_o[pl.ds(pl.multiple_of(step * rows + RIM, RIM), rows), :] = result

    @pl.when(step == last)
    def _():
        out_o[pl.ds(pl.multiple_of(step * rows + RIM, RIM), rows - RIM), :] = result[: rows - RIM]
        rim_o[...] = result[rows - RIM :]
        out_o[0:RIM, :] = jnp.zeros((RIM, result.shape[1]), bf16)


def chip_join_kernel(count, *refs):
    parts, out = refs[: 2 * count], refs[-1]
    at = 0
    for keep, got in zip(parts[::2], parts[1::2]):
        rows = keep.shape[1]
        out[0, at : at + rows, :] = (keep[0].astype(f32) + got[0].astype(f32)).astype(bf16)
        at += rows


def plane_sum_kernel(count, place, *refs):
    parts, outs, total_s = refs[:count], refs[count + 1 : -1], refs[-1]
    if count == 1:
        total_s[...] = jnp.sum(parts[0][...].astype(f32), axis=0)
    else:
        total = parts[0][...].astype(f32)
        for part in parts[1:]:
            total = total + part[...].astype(f32)
        total_s[...] = total
    rows = outs[0].shape[0]
    for b, out in enumerate(outs):
        at = pl.multiple_of(lax.bitwise_xor(place[0], b) * rows, 8)
        out[...] = total_s[pl.ds(at, rows), :].astype(bf16)


def z_sum_kernel(count, *refs):
    parts, out = refs[:count], refs[-1]
    total = parts[0][...].astype(f32)
    for part in parts[1:]:
        total = total + part[...].astype(f32)
    out[...] = total.astype(bf16)


def z_join_kernel(count, place, *refs):
    out = refs[-1]
    for b, ref in enumerate(refs[:count]):
        share = ref[...]
        at = lax.bitwise_xor(place[0], b)
        for cell in range(out.shape[0]):
            out[cell, at] = share


def unpack_kernel(split, core, down, up, mine, other, rel_hot, down_o, up_o, qkv_o, out_o, embed_o, *small_o):
    step = pl.program_id(0)
    down_o[...] = down[...].astype(f32)
    up_o[...] = up[...].astype(f32)
    width = out_o.shape[1]
    e_in = embed_o.shape[0]

    def give(low, high):
        rows = low[:, 0:split].reshape(-1, width).astype(f32)
        qkv_o[:, 0:width] = rows[0:width]
        qkv_o[:, width : 2 * width] = rows[width:]
        rows = high[:, 0:split].reshape(-1, width).astype(f32)
        qkv_o[:, 2 * width :] = rows[0:width]
        out_o[...] = rows[width:]
        rows = low[:, split:].reshape(-1, width).astype(f32)
        half = rows.shape[0]
        embed_o[0 : min(half, e_in), :] = rows[0 : min(half, e_in)]
        rows = high[:, split:].reshape(-1, width).astype(f32)
        left = max(e_in - half, 0)
        if left:
            embed_o[half:e_in, :] = rows[0:left]
        for i, vector_o in enumerate(small_o[:6]):
            vector_o[...] = rows[left + i]
        up_bias_o, rel_o = small_o[6:]
        for i in range(up_bias_o.shape[0] // width):
            up_bias_o[i * width : (i + 1) * width] = rows[left + 6 + i]
        sums = rows[left + 16 : left + 16 + SPOTS, 0 : HEADS * SPOTS]
        head = lax.broadcasted_iota(jnp.int32, (HEADS, HEADS * SPOTS), 0)
        own = head == lax.broadcasted_iota(jnp.int32, (HEADS, HEADS * SPOTS), 1) // SPOTS
        by_head = jnp.concatenate(
            [jnp.where(own, sums[j : j + 1], 0.0) for j in range(SPOTS)], axis=1
        )
        rel_o[...] = jnp.dot(
            by_head, rel_hot[...], precision=PRECISE, preferred_element_type=f32
        )

    @pl.when((step == 0) & (core[0] == 0))
    def _():
        give(mine, other)

    @pl.when((step == 0) & (core[0] == 1))
    def _():
        give(other, mine)


ANY = pl.BlockSpec(memory_space=pl.ANY)
SMEM = pl.BlockSpec(memory_space=pltpu.SMEM)


def whole(s):
    return pl.BlockSpec(s, lambda *i: (0,) * len(s))


def held(s):
    return pl.BlockSpec(s, lambda *i: (0,) * len(s), pipeline_mode=pl.Buffered(1))


def tile(rows, width, first=0):
    return pl.BlockSpec((rows, width), lambda i: (i + first, 0))


def params():
    return pltpu.CompilerParams(vmem_limit_bytes=VMEM_LIMIT)


def shape(s, d):
    return jax.ShapeDtypeStruct(s, d)


def at_once(kernel, args, outs, specs=None, scratch=()):
    if specs is None:
        specs = [whole(a.shape) for a in args]
    many = isinstance(outs, (list, tuple))
    out_specs = [whole(o.shape) for o in outs] if many else whole(outs.shape)
    return pl.pallas_call(
        kernel,
        grid=(1,),
        in_specs=specs,
        out_specs=out_specs,
        out_shape=outs,
        scratch_shapes=list(scratch),
        compiler_params=params(),
    )(*args)


def swap_cores(x):
    return lax.ppermute(x, "c", [(0, 1), (1, 0)])


def exchange(x, axis):
    return lax.all_to_all(x, axis, 0, 0, tiled=True)


def across(x, axis):
    size = lax.axis_size(axis)
    return [lax.ppermute(x[b], axis, [(i, i ^ b) for i in range(size)]) for b in range(1, size)]


def chip_join(pairs, after):
    cells = lax.axis_size("p")
    width = pairs[0][0].shape[1]
    refs = [a.reshape(cells, -1, width) for keep, send in pairs for a in (keep, swap_cores(send))]
    rows = sum(r.shape[1] for r in refs[::2])
    return pl.pallas_call(
        partial(chip_join_kernel, len(pairs)),
        grid=(cells,),
        in_specs=[pl.BlockSpec((1, *r.shape[1:]), lambda i: (i, 0, 0)) for r in refs] + [ANY] * len(after),
        out_specs=pl.BlockSpec((1, rows, width), lambda i: (i, 0, 0)),
        out_shape=shape((cells, rows, width), bf16),
        compiler_params=params(),
    )(*refs, *after)


def plane_sum(place, parts, after):
    planes = lax.axis_size("z")
    rows, width = parts[0].shape[-2:]
    return at_once(
        partial(plane_sum_kernel, len(parts)),
        (place, *parts, after),
        [shape((rows // planes, width), bf16)] * planes,
        [SMEM] + [whole(p.shape) for p in parts] + [ANY],
        [pltpu.VMEM((rows, width), f32)],
    )


def z_sum(parts, after):
    return at_once(
        partial(z_sum_kernel, len(parts)),
        (*parts, *after),
        shape(parts[0].shape, bf16),
        [whole(p.shape) for p in parts] + [ANY] * len(after),
    )


def z_join(place, parts, after):
    cells = lax.axis_size("p")
    return at_once(
        partial(z_join_kernel, len(parts)),
        (place, *parts, *after),
        shape((cells, len(parts), *parts[0].shape), bf16),
        [SMEM] + [whole(p.shape) for p in parts] + [ANY] * len(after),
    )


def order_matrix(block):
    token = np.arange(block)
    group, rest = token // (WIN * BANDS), token % (WIN * BANDS)
    frame, band = rest // BANDS, rest % BANDS
    row = group * (WIN * BANDS) + (band // WIN) * SPOTS + frame * WIN + band % WIN
    matrix = np.zeros((block, block), np.float32)
    matrix[row, token] = 1.0
    return matrix


def per_device(
    visible, embed_weight, embed_bias, mask_token, pos_embed, norm1_gain, qkv_weight, rel_table,
    out_weight, out_bias, norm2_gain, up_weight, up_bias, down_weight, down_bias, cotangent,
    visible_index, slot_counts, segment_ids,
):
    device_count = lax.axis_size(AXES)
    device_rank = lax.axis_index(AXES)
    core = lax.axis_index("c").reshape(1).astype(jnp.int32)
    z_place = lax.axis_index("z").reshape(1).astype(jnp.int32)
    planes, cells = lax.axis_size("z"), lax.axis_size("p")
    tokens, width = cotangent.shape
    frames = tokens // BANDS
    hidden = down_weight.shape[0]
    e_in = visible.shape[1]
    slot_rows = visible_index.shape[2]
    slots = device_count * slot_rows
    ext = slots + RIM_SLOTS
    back = [(i, (i - 1) % device_count) for i in range(device_count)]
    ahead = [(i, (i + 1) % device_count) for i in range(device_count)]
    row = lambda v: v.reshape(1, -1)

    arrived = exchange(visible, AXES)

    spot = visible_index.reshape(slots)
    live = (
        jnp.arange(slot_rows)[None, :] < slot_counts.reshape(device_count, 1)
    ).reshape(slots)
    rim_hot = ((jnp.arange(RIM)[:, None] == spot[None, :]) & live[None, :]).astype(bf16)
    rim_seen = jnp.sum(rim_hot.astype(f32), axis=1, keepdims=True).astype(bf16)
    sent_back = jnp.concatenate(
        [cotangent[:RIM], jnp.broadcast_to(rim_seen, (RIM, width))], axis=0
    )
    from_next = lax.ppermute(sent_back, AXES, back)
    next_seen = from_next[RIM:, 0].astype(f32)
    own_places = jnp.where(live & (spot >= RIM), window_row(spot - RIM), -1)
    rim_places = jnp.where(
        next_seen > 0.5, window_row(tokens - RIM + np.arange(RIM)), -1
    )
    places = jnp.concatenate(
        [own_places, rim_places, np.full((RIM_SLOTS - RIM,), -1, np.int32)]
    ).reshape(1, ext).astype(jnp.int32)

    seg_cycle = jnp.concatenate([segment_ids, segment_ids[:SHIFT]])
    seg_tape = lax.dynamic_slice_in_dim(seg_cycle, device_rank * frames + SHIFT, frames)
    seg_win = seg_tape.reshape(frames // WIN, WIN)
    cut = jnp.repeat(
        (seg_win[:, SHIFT - 1] != seg_win[:, SHIFT]).astype(f32), BANDS // WIN
    )

    spots = np.arange(SPOTS)
    frame_of, band_of = spots // WIN, spots % WIN
    rels = 2 * WIN - 1
    rel_index = (frame_of[:, None] - frame_of[None, :] + WIN - 1) * rels + (
        band_of[:, None] - band_of[None, :] + WIN - 1
    )
    rel_hot = (rel_index[:, :, None] == np.arange(rels * rels)).astype(np.float32)
    bias = jnp.einsum("hr,ijr->jhi", rel_table, rel_hot, precision=PRECISE).reshape(
        SPOTS, HEADS * SPOTS
    )
    halves = frame_of // SHIFT
    apart = np.tile(
        np.where(halves[:, None] != halves[None, :], MASKED, 0.0).astype(np.float32), (1, HEADS)
    )
    ones = jnp.asarray(
        np.arange(OCT_S)[:, None] // SPOTS == np.arange(OCT_D)[None, :] // HD, bf16
    )
    order = order_matrix(256)
    cot, positions = at_once(
        prepare_kernel,
        (cotangent, from_next[:RIM], pos_embed, order),
        [shape(cotangent.shape, bf16), shape(pos_embed.shape, f32)],
    )

    tm = min(512, tokens)
    grid = (tokens // tm,)
    pos_blocks = pos_embed.shape[0] // tm
    rim_rows = jnp.dot(rim_hot, arrived, preferred_element_type=f32).astype(bf16)
    next_rows = lax.ppermute(rim_rows, AXES, back)
    rim = jnp.pad(next_rows, ((0, RIM_SLOTS - RIM), (0, 0)))
    first_args = [
        cut, arrived, rim, embed_weight, row(embed_bias), places, positions,
        row(mask_token), row(norm1_gain), qkv_weight, bias, apart, ones, out_weight,
        row(out_bias), row(norm2_gain), cot, down_weight, up_weight, row(up_bias),
    ]
    specs = [SMEM] + [held(a.shape) for a in first_args[1:]]
    specs[6] = pl.BlockSpec((tm, width), lambda i: (lax.rem(i, pos_blocks), 0))
    specs[16] = tile(tm, width)
    start, qkv, probs, context, middle, act, grad_up, down_grad, up_grad, up_bias_grad = (
        pl.pallas_call(
            first_kernel,
            grid=grid,
            in_specs=specs,
            out_specs=[
                tile(tm, width),
                tile(tm, 3 * width),
                tile(tm, HEADS * SPOTS),
                tile(tm, width),
                tile(tm, width),
                tile(tm, hidden),
                tile(tm, hidden),
                whole((hidden, width)),
                whole((width, hidden)),
                whole((1, hidden)),
            ],
            out_shape=[
                shape((tokens, width), f32),
                shape((tokens, 3 * width), bf16),
                shape((tokens, HEADS * SPOTS), f32),
                shape((tokens, width), bf16),
                shape((tokens, width), f32),
                shape((tokens, hidden), bf16),
                shape((tokens, hidden), bf16),
                shape((hidden, width), bf16),
                shape((width, hidden), bf16),
                shape((1, hidden), f32),
            ],
            scratch_shapes=[
                pltpu.VMEM((ext, width), bf16),
                pltpu.VMEM((tm, HEADS * SPOTS), f32),
                pltpu.VMEM((hidden, width), f32),
                pltpu.VMEM((width, hidden), f32),
            ],
            compiler_params=params(),
        )(*first_args)
    )
    down_sum, up_sum = lax.psum((down_grad, up_grad), AXES)

    unit = 16 * planes * cells
    half = -(-width // unit) * unit
    def rest(operands):
        (
            qkv, probs, start, grad_up, middle, context, cot, act, places, arrived, rim, rim_hot,
            up_bias_grad,
        ) = operands
        grad_slots, keep_c, send_c, keep_d, send_d = pl.pallas_call(
            second_kernel,
            grid=grid,
            in_specs=[
                SMEM,
                tile(tm, 3 * width),
                tile(tm, HEADS * SPOTS),
                tile(tm, width),
                tile(tm, hidden),
                tile(tm, width),
                tile(tm, width),
                tile(tm, width),
                held((1, ext)),
                held((width, 3 * width)),
                held((1, width)),
                held((OCT_S, OCT_D)),
                held((slots, e_in)),
                held((RIM_SLOTS, e_in)),
                held((1, hidden)),
                held((width, hidden)),
                held((1, width)),
                held((width, width)),
            ],
            out_specs=[
                whole((ext, width)),
                whole((2 * width, width)),
                whole((2 * width, width)),
                whole((half, width)),
                whole((half, width)),
            ],
            out_shape=[
                shape((ext, width), bf16),
                shape((2 * width, width), bf16),
                shape((2 * width, width), bf16),
                shape((half, width), bf16),
                shape((half, width), bf16),
            ],
            scratch_shapes=[
                pltpu.VMEM((tm, 3 * width), bf16),
                pltpu.VMEM((width, 3 * width), f32),
                pltpu.VMEM((tm, HEADS * SPOTS), f32),
                pltpu.VMEM((ext, width), f32),
                pltpu.VMEM((max(e_in, half), width), f32),
                pltpu.VMEM((16, width), f32),
                pltpu.VMEM((SPOTS, HEADS * SPOTS), f32),
                pltpu.VMEM((width, width), f32),
                pltpu.VMEM((tm, width), bf16),
                pltpu.VMEM((tm, width), f32),
            ],
            compiler_params=params(),
        )(
            core, qkv, probs, start, grad_up, middle, context, cot, places, qkv_weight,
            row(norm1_gain), ones, arrived, rim, up_bias_grad, up_weight, row(norm2_gain),
            out_weight,
        )
        rim_grad = lax.ppermute(grad_slots[slots : slots + RIM], AXES, ahead)
        shares = chip_join([(keep_c, send_c), (keep_d, send_d)], ())
        part = exchange(shares, "p")
        out, rim_out = pl.pallas_call(
            out_kernel,
            grid=grid,
            in_specs=[
                tile(tm, width),
                tile(tm, hidden),
                held((hidden, width)),
                held((1, width)),
                held(order.shape),
                ANY,
            ],
            out_specs=[whole((tokens, width)), whole((RIM, width))],
            out_shape=[shape((tokens, width), bf16), shape((RIM, width), bf16)],
            compiler_params=params(),
        )(middle, act, down_weight, row(down_bias), jnp.asarray(order, bf16), shares)
        first_rows = lax.ppermute(rim_out, AXES, ahead)
        out = lax.dynamic_update_slice(out, first_rows, (0, 0))
        sums_c = plane_sum(z_place, [part], rim_out)
        grad_embedded = at_once(
            rim_back_kernel,
            (rim_hot, rim_grad, grad_slots, sums_c[0], first_rows),
            shape((slots, width), bf16),
            [whole(a.shape) for a in (rim_hot, rim_grad, grad_slots)] + [ANY, ANY],
        )
        returned = exchange(grad_embedded, AXES)
        grad_visible = lax.dot_general(
            returned, embed_weight, (((1,), (1,)), ((), ())), preferred_element_type=f32
        ).astype(bf16)
        total = z_sum([sums_c[0], *across(sums_c, "z")], ())
        joined = z_join(z_place, [total, *across([total] * planes, "z")], (returned,))
        mine = exchange(joined, "p").reshape(cells, -1, width)
        return out, grad_visible, mine, swap_cores(mine)

    def nothing(operands):
        return tuple(jnp.zeros(o.shape, o.dtype) for o in jax.eval_shape(rest, operands))

    operands = (
        qkv, probs, start, grad_up, middle, context, cot, act, places, arrived, rim, rim_hot,
        up_bias_grad,
    )
    out, grad_visible, mine, other = lax.cond(device_rank < device_count, rest, nothing, operands)

    vector = shape((width,), f32)
    unpacked = [
        shape((width, 3 * width), f32),
        shape((width, width), f32),
        shape((e_in, width), f32),
        *[vector] * 6,
        shape((hidden,), f32),
        shape((HEADS, rels * rels), f32),
    ]
    turns = 4
    rel_rows = np.repeat(rel_hot.transpose(1, 0, 2)[:, None], HEADS, axis=1).reshape(
        SPOTS * HEADS * SPOTS, rels * rels
    )
    wide = [tile(hidden // turns, width), tile(width // turns, hidden)]
    (
        grad_down_weight, grad_up_weight, grad_qkv_weight, grad_out_weight, grad_embed_weight,
        grad_norm2_gain, grad_out_bias, grad_down_bias, grad_norm1_gain, grad_mask_token,
        grad_embed_bias, grad_up_bias, grad_rel,
    ) = pl.pallas_call(
        partial(unpack_kernel, 2 * width // cells),
        grid=(turns,),
        in_specs=[SMEM, *wide, held(mine.shape), held(other.shape), held(rel_rows.shape)],
        out_specs=wide + [whole(o.shape) for o in unpacked],
        out_shape=[shape((hidden, width), f32), shape((width, hidden), f32), *unpacked],
        compiler_params=params(),
    )(core, down_sum, up_sum, mine, other, rel_rows)
    return (
        out,
        grad_visible,
        grad_embed_weight,
        grad_embed_bias,
        grad_mask_token,
        grad_norm1_gain,
        grad_qkv_weight,
        grad_rel,
        grad_out_weight,
        grad_out_bias,
        grad_norm2_gain,
        grad_up_weight,
        grad_up_bias,
        grad_down_weight,
        grad_down_bias,
    )


def solution(mesh):
    planes = 4
    grid = Mesh(mesh.devices.reshape(planes, -1, 2), AXES)
    split = P(AXES)
    in_specs = (split,) + (P(),) * 14 + (split, split, split, P())
    out_specs = (split, split) + (P(),) * 13
    return jax.shard_map(
        per_device, mesh=grid, in_specs=in_specs, out_specs=out_specs, check_vma=False
    )
```
